256 devices in a mesh: gx: 4 (over y), gy: 8 (over z), gz: 8 (over x, core).
Axes of the slice: x: 4, y: 4, z: 8, core: 2. Of those that a mesh axis runs over, the one named last changes fastest.
Arguments:
- rhs: float32 [64, 384, 1024], P('gx', 'gy', 'gz'), may hold values from -6000 to 6000
- coef_b: float32 [64, 384, 1024], P('gx', 'gy', 'gz'), may hold values from 1 to 10
- coef_c: float32 [64, 384, 1024], P('gx', 'gy', 'gz'), may hold values from 1 to 10
Outputs:
- solution: float32 [64, 384, 1024], P('gx', 'gy', 'gz')
The draws below stay inside these ranges and needn't reach their ends.
All inputs are finite; a program needn't handle non-finite values.
Results may differ from the reference program's by a relative error of at most 0.0001.
Values sent between devices are 32-bit elements; how exact they have to be, the bound alone decides.
A program may use at most 128 MiB of HBM per device.

```python
import math
import jax
import jax.numpy as jnp

LEVELS = 4
SWEEPS = 2
COARSE_SWEEPS = 6
NX = 64
NY = 384
NZ = 1024


def block_levels(stream_key, extent, shards, smallest, high):
    loudness = 1.0
    for dim, blocks in shards:
        steps = jax.random.uniform(jax.random.fold_in(jax.random.fold_in(stream_key, 6), dim), (blocks,), jnp.float32, smallest / len(shards), high / len(shards))
        loudness = loudness * jnp.repeat(jnp.exp(steps), extent[dim] // blocks).reshape((-1,) + (1,) * (len(extent) - 1 - dim))
    return loudness


def gaussian(rng, extent, scale, bound, pieces=(), dtype=jnp.bfloat16):
    gain = block_levels(rng, extent, pieces, -0.22, 0.18) if pieces else 1.0
    drawn = jax.random.normal(rng, extent, jnp.float32) * scale * gain
    return jnp.minimum(jnp.maximum(drawn, -bound), bound).astype(dtype)


def setup_inputs(seed: int = 0) -> dict:
    key_of = jax.random.split(jax.random.key(seed), 4)
    rhs = gaussian(key_of[0], (NX, NY, NZ), 1000.0, 6000.0, ((0, 4), (1, 8), (2, 8)), jnp.float32)
    coef_b = jnp.clip(jnp.exp(math.log(10.0) - 2.3025851 * jax.random.uniform(key_of[1], (NX, NY, NZ), jnp.float32) ** block_levels(key_of[1], (NX, NY, NZ), ((0, 4), (1, 8), (2, 8)), -0.2, 0.2)), 1.0, 10.0)
    coef_c = jnp.clip(jnp.exp(math.log(10.0) - 2.3025851 * jax.random.uniform(key_of[2], (NX, NY, NZ), jnp.float32) ** block_levels(key_of[2], (NX, NY, NZ), ((0, 4), (1, 8), (2, 8)), -0.2, 0.2)), 1.0, 10.0)
    return dict(rhs=rhs, coef_b=coef_b, coef_c=coef_c)


CENTRE = 1.1
RADIUS = 0.9


def neighbours(padded):
    return (padded[:-2, 1:-1, 1:-1], padded[2:, 1:-1, 1:-1],
            padded[1:-1, :-2, 1:-1], padded[1:-1, 2:, 1:-1],
            padded[1:-1, 1:-1, :-2], padded[1:-1, 1:-1, 2:])


def faces_of(coef_pad):
    middle = coef_pad[1:-1, 1:-1, 1:-1]
    return tuple(0.5 * (middle + other) for other in neighbours(coef_pad))


def diagonal_of(face_terms, cell_term, level_scale):
    summed = face_terms[0] + face_terms[1] + face_terms[2] + face_terms[3] + face_terms[4] + face_terms[5]
    return cell_term + level_scale * summed


def operator(padded, face_terms, cell_term, level_scale):
    middle = padded[1:-1, 1:-1, 1:-1]
    beside = neighbours(padded)
    summed = face_terms[0] * (middle - beside[0])
    for position in range(1, 6):
        summed = summed + face_terms[position] * (middle - beside[position])
    return cell_term * middle + level_scale * summed


def coarsen(values):
    shape = values.shape
    return values.reshape(shape[0] // 2, 2, shape[1] // 2, 2, shape[2] // 2, 2).mean(axis=(1, 3, 5))


def refine(values):
    return jnp.repeat(jnp.repeat(jnp.repeat(values, 2, axis=0), 2, axis=1), 2, axis=2)


def smooth(approx, source, face_terms, cell_term, level_scale, diagonal, sweeps, padder, from_zero):
    if from_zero:
        remain = source
    else:
        remain = source - operator(padder(approx), face_terms, cell_term, level_scale)
    update = remain / (CENTRE * diagonal)
    approx = update if from_zero else approx + update
    ratio_now = RADIUS / CENTRE
    for sweep_index in range(sweeps - 1):
        remain = source - operator(padder(approx), face_terms, cell_term, level_scale)
        ratio_next = 1.0 / (2.0 * CENTRE / RADIUS - ratio_now)
        update = ratio_next * ratio_now * update + (2.0 * ratio_next / RADIUS) * remain / diagonal
        approx = approx + update
        ratio_now = ratio_next
    return approx


def zero_pad(values):
    return jnp.pad(values, 1)


def reference(rhs, coef_b, coef_c):
    source = rhs
    coef_now = coef_b
    cell_term = coef_c
    saved = []
    for level_index in range(LEVELS - 1):
        level_scale = 4.0 ** (LEVELS - 1 - level_index)
        face_terms = faces_of(zero_pad(coef_now))
        diagonal = diagonal_of(face_terms, cell_term, level_scale)
        approx = smooth(None, source, face_terms, cell_term, level_scale, diagonal, SWEEPS, zero_pad, True)
        remain = source - operator(zero_pad(approx), face_terms, cell_term, level_scale)
        saved.append((approx, source, face_terms, cell_term, level_scale, diagonal))
        source = coarsen(remain)
        coef_now = coarsen(coef_now)
        cell_term = coarsen(cell_term)
    level_scale = 1.0
    face_terms = faces_of(zero_pad(coef_now))
    diagonal = diagonal_of(face_terms, cell_term, level_scale)
    coarse = smooth(None, source, face_terms, cell_term, level_scale, diagonal, COARSE_SWEEPS, zero_pad, True)
    for level_index in range(LEVELS - 2, -1, -1):
        approx, source, face_terms, cell_term, level_scale, diagonal = saved[level_index]
        approx = approx + refine(coarse)
        coarse = smooth(approx, source, face_terms, cell_term, level_scale, diagonal, SWEEPS, zero_pad, False)
    return coarse
```

```python
import jax
import jax.numpy as jnp
from jax import lax
from jax.experimental import pallas as pl
from jax.experimental.pallas import tpu as pltpu
from jax.sharding import PartitionSpec as P

LEVELS = 4
COARSE_SWEEPS = 6
CENTRE = 1.1
RADIUS = 0.9
LANES = 128
PAD = 8

MESH = pl.DeviceIdType.MESH
AXES = ("gx", "gy", "gz")


def chebyshev(sweeps):
    ratio = RADIUS / CENTRE
    factors = [(0.0, 1.0 / CENTRE)]
    for _ in range(sweeps - 1):
        following = 1.0 / (2.0 * CENTRE / RADIUS - ratio)
        factors.append((following * ratio, 2.0 * following / RADIUS))
        ratio = following
    return factors


def round_up(value):
    return -(-value // 8) * 8


class Names:
    pass


def exact_dot(left, matrix):
    high = left.astype(jnp.bfloat16)
    rest = left - high.astype(jnp.float32)
    middle = rest.astype(jnp.bfloat16)
    low = (rest - middle.astype(jnp.float32)).astype(jnp.bfloat16)
    total = jnp.dot(low, matrix, preferred_element_type=jnp.float32)
    total = total + jnp.dot(middle, matrix, preferred_element_type=jnp.float32)
    return total + jnp.dot(high, matrix, preferred_element_type=jnp.float32)


def make_kernel(shape, sizes, plan):
    count = {axis: sizes[axis] for axis in AXES}

    def kernel(rhs, coef_b, coef_c, out, *scratch):
        refs = plan.unpack(scratch)
        place = {axis: lax.axis_index(axis) for axis in AXES}
        after = {axis: lax.rem(place[axis] + 1, count[axis]) for axis in AXES}
        before = {axis: lax.rem(place[axis] + count[axis] - 1, count[axis]) for axis in AXES}
        has_before = {a: jnp.where(place[a] > 0, 1.0, 0.0).astype(jnp.float32) for a in AXES}
        has_after = {a: jnp.where(place[a] < count[a] - 1, 1.0, 0.0).astype(jnp.float32) for a in AXES}

        barrier = pltpu.get_barrier_semaphore()
        for axis in AXES:
            for other in (before[axis], after[axis]):
                pl.semaphore_signal(barrier, inc=1, device_id={axis: other}, device_id_type=MESH)
        pl.semaphore_wait(barrier, 6)

        lane = lax.broadcasted_iota(jnp.int32, (1, LANES), 1)

        def dims(level):
            return tuple(n >> level for n in shape)

        def copies(level, h):
            nx, ny, _ = dims(level)
            rows = pl.ds(PAD, round_up(ny))
            vp, zs, zr, ys, yr = h.vp, h.zs, h.zr, h.ys, h.yr
            pairs = (
                (vp.at[nx, rows], vp.at[0, rows], "gx", after),
                (vp.at[1, rows], vp.at[nx + 1, rows], "gx", before),
                (ys.at[0], yr.at[0], "gy", after),
                (ys.at[1], yr.at[1], "gy", before),
                (zs.at[0], zr.at[0], "gz", after),
                (zs.at[1], zr.at[1], "gz", before),
            )
            return [
                pltpu.make_async_remote_copy(
                    src_ref=src, dst_ref=dst, send_sem=h.send.at[i], recv_sem=h.recv.at[i],
                    device_id={axis: where[axis]}, device_id_type=MESH)
                for i, (src, dst, axis, where) in enumerate(pairs)
            ]

        def start(level, h):
            for copy in copies(level, h):
                copy.start()

        def finish(level, h):
            nx, ny, _ = dims(level)
            for copy in copies(level, h):
                copy.wait()
            for x in range(nx):
                h.vp[x + 1, pl.ds(PAD - 1, 1), :] = h.yr[0, pl.ds(x, 1), :]
                h.vp[x + 1, pl.ds(PAD + ny, 1), :] = h.yr[1, pl.ds(x, 1), :]

        def sweep(level, make, h=None, extra=()):
            nx, ny, nz = dims(level)
            zero = jnp.zeros((ny, LANES), jnp.float32)

            def body(x, carry):
                high, low = carry
                plane = make(x)
                h.vp[x + 1, pl.ds(PAD, ny), :] = plane
                h.ys[0, pl.ds(x, 1), :] = plane[ny - 1:ny]
                h.ys[1, pl.ds(x, 1), :] = plane[0:1]
                here = lane == x
                high = jnp.where(here, pltpu.roll(plane, lax.rem(x + LANES - (nz - 1), LANES), 1), high)
                low = jnp.where(here, pltpu.roll(plane, x, 1), low)
                return high, low

            high, low = lax.fori_loop(0, nx, body, (zero, zero))
            h.zs[0, pl.ds(0, ny), :] = high
            h.zs[1, pl.ds(0, ny), :] = low
            start(level, h)

        def around(level, h, x):
            nx, ny, nz = dims(level)
            vp = h.vp
            mid = vp[x + 1, pl.ds(PAD, ny), :]
            zlow = h.zr[0, pl.ds(0, ny), :]
            zhigh = h.zr[1, pl.ds(0, ny), :]
            zm = jnp.where(lane == 0, pltpu.roll(zlow, lax.rem(LANES - x, LANES), 1), pltpu.roll(mid, 1, 1))
            zp = jnp.where(lane == nz - 1, pltpu.roll(zhigh, lax.rem(LANES + nz - 1 - x, LANES), 1),
                           pltpu.roll(mid, LANES - 1, 1))
            return (mid, vp[x, pl.ds(PAD, ny), :], vp[x + 2, pl.ds(PAD, ny), :],
                    vp[x + 1, pl.ds(PAD - 1, ny), :], vp[x + 1, pl.ds(PAD + 1, ny), :], zm, zp)

        def residual(level, h, x):
            g = refs.level[level]
            mid, xm, xp, ym, yp, zm, zp = around(level, h, x)
            total = g.sx[x] * xm + g.sx[x + 1] * xp + g.sym[x] * ym + g.syp[x] * yp + g.szm[x] * zm + g.szp[x] * zp
            return mid, source(level, x) - g.q[x] * mid + total

        def source(level, x):
            return rhs[x] if level == 0 else refs.level[level].f[x]

        def reaction(level, x):
            return coef_c[x] if level == 0 else refs.level[level].c[x]

        row_of = lax.broadcasted_iota(jnp.int32, (LANES, LANES), 0)
        col_of = lax.broadcasted_iota(jnp.int32, (LANES, LANES), 1)
        shrink = jnp.where((row_of // 2 == col_of), 0.125, 0.0).astype(jnp.bfloat16)
        grow = jnp.where((col_of // 2 == row_of), 1.0, 0.0).astype(jnp.bfloat16)

        def coarsen(level, get, put):
            nx, ny, nz = dims(level)
            pair = refs.level[level].pair

            def body(x, carry):
                pair[x] = get(2 * x) + get(2 * x + 1)
                return carry

            lax.fori_loop(0, nx // 2, body, 0)
            for x in range(nx // 2):
                even = pair[x, pl.ds(0, ny // 2, 2), :]
                odd = pair[x, pl.ds(1, ny // 2, 2), :]
                mean = exact_dot(even + odd, shrink)
                put(x, jnp.where(lane < nz // 2, mean, 0.0))

        def refine(level, get):
            nx, ny, nz = dims(level)
            pair = refs.level[level].pair
            for x in range(nx // 2):
                wide = exact_dot(get(x), grow)
                pair[x, pl.ds(0, ny // 2, 2), :] = wide
                pair[x, pl.ds(1, ny // 2, 2), :] = wide

        for level in range(LEVELS):
            ny = dims(level)[1]
            if level == 0:
                sweep(level, lambda x: coef_b[x], refs.level[level].b)
            else:
                g = refs.level[level]
                upper = refs.level[level - 1]
                above_y = dims(level - 1)[1]

                def put_b(x, plane, g=g, ny=ny):
                    g.f[x] = plane

                def put_c(x, plane, g=g):
                    g.c[x] = plane

                coarsen(level - 1, lambda x: upper.b.vp[x + 1, pl.ds(PAD, above_y), :], put_b)
                coarsen(level - 1, lambda x: reaction(level - 1, x), put_c)
                sweep(level, lambda x: g.f[x], g.b)

        def setup(level):
            g = refs.level[level]
            nx, ny, nz = dims(level)
            half = 0.5 * 4.0 ** (LEVELS - 1 - level)
            finish(level, g.b)
            g.b.vp[0, pl.ds(PAD, ny), :] = g.b.vp[0, pl.ds(PAD, ny), :] * has_before["gx"]
            g.b.vp[nx + 1, pl.ds(PAD, ny), :] = g.b.vp[nx + 1, pl.ds(PAD, ny), :] * has_after["gx"]
            row = lax.broadcasted_iota(jnp.int32, (ny, 1), 0)
            keep_ym = jnp.where(row == 0, has_before["gy"], 1.0)
            keep_yp = jnp.where(row == ny - 1, has_after["gy"], 1.0)
            keep_zm = jnp.where(lane == 0, has_before["gz"], 1.0)
            keep_zp = jnp.where(lane == nz - 1, has_after["gz"], 1.0)

            def body(x, carry):
                mid, xm, xp, ym, yp, zm, zp = around(level, g.b, x)
                fxm, fxp = half * (mid + xm), half * (mid + xp)
                fym, fyp = half * (mid + ym * keep_ym), half * (mid + yp * keep_yp)
                fzm, fzp = half * (mid + zm * keep_zm), half * (mid + zp * keep_zp)
                q = reaction(level, x) + (fxm + fxp + fym + fyp + fzm + fzp)
                g.q[x] = q
                g.rq[x] = jnp.where(lane < nz, 1.0 / q, 0.0)
                g.sx[x] = fxm * jnp.where(x == 0, has_before["gx"], 1.0)
                g.sym[x] = fym * keep_ym
                g.syp[x] = fyp * keep_yp
                g.szm[x] = fzm * keep_zm
                g.szp[x] = fzp * keep_zp
                return carry

            lax.fori_loop(0, nx, body, 0)
            last = g.b.vp[nx, pl.ds(PAD, ny), :] + g.b.vp[nx + 1, pl.ds(PAD, ny), :]
            g.sx[nx] = half * last * has_after["gx"]

        steps = chebyshev(2)
        (_, first), (carry_e, weight_r) = steps

        for level in range(LEVELS - 1):
            g = refs.level[level]
            setup(level)
            sweep(level, lambda x: source(level, x) * g.rq[x] * first, g.it[0])
            finish(level, g.it[0])

            def second(x):
                mid, rest = residual(level, g.it[0], x)
                return mid * (1.0 + carry_e) + weight_r * rest * g.rq[x]

            sweep(level, second, g.it[1])
            finish(level, g.it[1])
            below = refs.level[level + 1]

            def put_f(x, plane, below=below):
                below.f[x] = plane

            coarsen(level, lambda x: residual(level, g.it[1], x)[1], put_f)

        level = LEVELS - 1
        g = refs.level[level]
        setup(level)
        steps = chebyshev(COARSE_SWEEPS)

        def begin(x):
            update = source(level, x) * g.rq[x] * steps[0][1]
            g.e[x] = update
            return update

        sweep(level, begin, g.it[0])
        for step in range(1, COARSE_SWEEPS):
            finish(level, g.it[step - 1])

            def advance(x, step=step):
                mid, rest = residual(level, g.it[step - 1], x)
                update = steps[step][0] * g.e[x] + steps[step][1] * rest * g.rq[x]
                g.e[x] = update
                return mid + update

            if step < COARSE_SWEEPS - 1:
                sweep(level, advance, g.it[step])
            else:
                for x in range(dims(level)[0]):
                    g.f[x] = advance(x)

        for level in range(LEVELS - 2, -1, -1):
            g = refs.level[level]
            nx, ny, nz = dims(level)
            below = refs.level[level + 1]
            refine(level, lambda x: below.f[x])
            sweep(level, lambda x: g.it[1].vp[x + 1, pl.ds(PAD, ny), :] + g.pair[x // 2], g.it[2])
            finish(level, g.it[2])

            def third(x):
                mid, rest = residual(level, g.it[2], x)
                update = first * rest * g.rq[x]
                g.e[x] = update
                return mid + update

            sweep(level, third, g.it[3])
            finish(level, g.it[3])

            def last(x, carry):
                mid, rest = residual(level, g.it[3], x)
                result = mid + carry_e * g.e[x] + weight_r * rest * g.rq[x]
                if level == 0:
                    out[x] = result
                else:
                    g.f[x] = result
                return carry

            lax.fori_loop(0, nx, last, 0)

    return kernel


class Plan:
    def __init__(self, shape):
        self.shapes = []
        self.tree = Names()
        self.tree.level = []
        for level in range(LEVELS):
            nx, ny, _ = (n >> level for n in shape)
            g = Names()

            def planes(n, ny=ny):
                return self.add(pltpu.VMEM((n, ny, LANES), jnp.float32))

            def halo(nx=nx, ny=ny):
                h = Names()
                h.vp = self.add(pltpu.VMEM((nx + 2, round_up(ny) + 2 * PAD, LANES), jnp.float32))
                h.zs = self.add(pltpu.VMEM((2, round_up(ny), LANES), jnp.float32))
                h.zr = self.add(pltpu.VMEM((2, round_up(ny), LANES), jnp.float32))
                h.ys = self.add(pltpu.VMEM((2, round_up(nx), LANES), jnp.float32))
                h.yr = self.add(pltpu.VMEM((2, round_up(nx), LANES), jnp.float32))
                h.send = self.add(pltpu.SemaphoreType.DMA((6,)))
                h.recv = self.add(pltpu.SemaphoreType.DMA((6,)))
                return h

            g.b = halo()
            g.sx = planes(nx + 1)
            for name in ("sym", "syp", "szm", "szp", "q", "rq", "e"):
                setattr(g, name, planes(nx))
            if level > 0:
                g.f = planes(nx)
                g.c = planes(nx)
            if level < LEVELS - 1:
                g.pair = planes(nx // 2)
            g.it = [halo() for _ in range(COARSE_SWEEPS - 1 if level == LEVELS - 1 else 4)]
            self.tree.level.append(g)

    def add(self, shape):
        self.shapes.append(shape)
        return len(self.shapes) - 1

    def unpack(self, refs):
        def walk(node):
            if isinstance(node, int):
                return refs[node]
            if isinstance(node, list):
                return [walk(item) for item in node]
            result = Names()
            for name, item in vars(node).items():
                setattr(result, name, walk(item))
            return result

        return walk(self.tree)


def solution(mesh):
    sizes = dict(mesh.shape)

    def local(rhs, coef_b, coef_c):
        shape = rhs.shape
        plan = Plan(shape)
        return pl.pallas_call(
            make_kernel(shape, sizes, plan),
            out_shape=jax.ShapeDtypeStruct(shape, jnp.float32),
            in_specs=[pl.BlockSpec(memory_space=pltpu.VMEM)] * 3,
            out_specs=pl.BlockSpec(memory_space=pltpu.VMEM),
            scratch_shapes=plan.shapes,
            compiler_params=pltpu.CompilerParams(
                collective_id=0, has_side_effects=True, vmem_limit_bytes=40 * 2**20),
        )(rhs, coef_b, coef_c)

    return jax.shard_map(
        local,
        mesh=mesh,
        in_specs=(P(*AXES),) * 3,
        out_specs=P(*AXES),
        check_vma=False,
    )
```

```python
import jax
import jax.numpy as jnp
from jax import lax
from jax.experimental import pallas as pl
from jax.experimental.pallas import tpu as pltpu
from jax.sharding import PartitionSpec as P

LEVELS = 4
COARSE_SWEEPS = 6
CENTRE = 1.1
RADIUS = 0.9
LANES = 128
PAD = 8

MESH = pl.DeviceIdType.MESH
AXES = ("gx", "gy", "gz")


def chebyshev(sweeps):
    ratio = RADIUS / CENTRE
    factors = [(0.0, 1.0 / CENTRE)]
    for _ in range(sweeps - 1):
        following = 1.0 / (2.0 * CENTRE / RADIUS - ratio)
        factors.append((following * ratio, 2.0 * following / RADIUS))
        ratio = following
    return factors


def round_up(value):
    return -(-value // 8) * 8


class Names:
    pass


def exact_dot(left, matrix):
    high = left.astype(jnp.bfloat16)
    rest = left - high.astype(jnp.float32)
    middle = rest.astype(jnp.bfloat16)
    low = (rest - middle.astype(jnp.float32)).astype(jnp.bfloat16)
    total = jnp.dot(low, matrix, preferred_element_type=jnp.float32)
    total = total + jnp.dot(middle, matrix, preferred_element_type=jnp.float32)
    return total + jnp.dot(high, matrix, preferred_element_type=jnp.float32)


WINDOW = (None, None, (16, 48), (8, 24))
FIRST_ROW = (0, 0, 18, 9)
NEAR = (-2, -1, 1, 2)


def make_kernel(shape, sizes, plan):
    count = {axis: sizes[axis] for axis in AXES}

    def kernel(rhs, coef_b, coef_c, out, *scratch):
        refs = plan.unpack(scratch)
        place = {axis: lax.axis_index(axis) for axis in AXES}

        def beyond(axis, step):
            return lax.rem(place[axis] + count[axis] + step, count[axis])

        after = {axis: beyond(axis, 1) for axis in AXES}
        before = {axis: beyond(axis, -1) for axis in AXES}
        has_before = {a: jnp.where(place[a] > 0, 1.0, 0.0).astype(jnp.float32) for a in AXES}
        has_after = {a: jnp.where(place[a] < count[a] - 1, 1.0, 0.0).astype(jnp.float32) for a in AXES}
        around_xz = [(dx, dz) for dx in range(4) for dz in (-1, 0, 1) if (dx, dz) != (0, 0)]

        barrier = pltpu.get_barrier_semaphore()
        for dy in NEAR:
            pl.semaphore_signal(barrier, inc=1, device_id={"gy": beyond("gy", dy)}, device_id_type=MESH)
        for dx, dz in around_xz:
            pl.semaphore_signal(barrier, inc=1, device_id={"gx": beyond("gx", dx), "gz": beyond("gz", dz)},
                                device_id_type=MESH)
        pl.semaphore_wait(barrier, len(NEAR) + len(around_xz))

        lane = lax.broadcasted_iota(jnp.int32, (1, LANES), 1)

        def own(level):
            return tuple(n >> level for n in shape)

        def dims(level):
            return WINDOW[level] or own(level)[:2]

        def clear_rim(level, h):
            nx, ny = dims(level)
            h.vp[0] = jnp.zeros(h.vp.shape[1:], jnp.float32)
            h.vp[nx + 1] = jnp.zeros(h.vp.shape[1:], jnp.float32)
            rim = jnp.zeros((nx, PAD, LANES), jnp.float32)
            h.vp[pl.ds(1, nx), pl.ds(0, PAD), :] = rim
            h.vp[pl.ds(1, nx), pl.ds(PAD + ny, PAD), :] = rim

        for level in range(LEVELS):
            if WINDOW[level]:
                for h in [refs.level[level].b] + refs.level[level].it:
                    clear_rim(level, h)

        def copies(level, h):
            nx, ny = dims(level)
            rows = pl.ds(PAD, round_up(ny))
            vp, zs, zr, ys, yr = h.vp, h.zs, h.zr, h.ys, h.yr
            pairs = (
                (vp.at[nx, rows], vp.at[0, rows], "gx", after),
                (vp.at[1, rows], vp.at[nx + 1, rows], "gx", before),
                (ys.at[0], yr.at[0], "gy", after),
                (ys.at[1], yr.at[1], "gy", before),
                (zs.at[0], zr.at[0], "gz", after),
                (zs.at[1], zr.at[1], "gz", before),
            )
            return [
                pltpu.make_async_remote_copy(
                    src_ref=src, dst_ref=dst, send_sem=h.send.at[i], recv_sem=h.recv.at[i],
                    device_id={axis: where[axis]}, device_id_type=MESH)
                for i, (src, dst, axis, where) in enumerate(pairs)
            ]

        def finish(level, h):
            if WINDOW[level]:
                return
            nx, ny = dims(level)
            nz = own(level)[2]
            for copy in copies(level, h):
                copy.wait()
            for x in range(nx):
                h.vp[x + 1, pl.ds(PAD - 1, 1), :] = h.yr[0, pl.ds(x, 1), :]
                h.vp[x + 1, pl.ds(PAD + ny, 1), :] = h.yr[1, pl.ds(x, 1), :]
            if level > 0:
                low, high = h.zr[0, pl.ds(0, ny), :], h.zr[1, pl.ds(0, ny), :]
                for x in range(nx):
                    plane = h.vp[x + 1, pl.ds(PAD, ny), :]
                    plane = jnp.where(lane == LANES - 1, pltpu.roll(low, LANES - 1 - x, 1), plane)
                    h.vp[x + 1, pl.ds(PAD, ny), :] = jnp.where(lane == nz, pltpu.roll(high, nz - x, 1), plane)

        def sweep(level, make, h):
            nx, ny = dims(level)
            nz = own(level)[2]
            if WINDOW[level]:
                def inside(x, carry):
                    h.vp[x + 1, pl.ds(PAD, ny), :] = make(x)
                    return carry

                lax.fori_loop(0, nx, inside, 0)
                return
            zero = jnp.zeros((ny, LANES), jnp.float32)

            def body(x, carry):
                high, low = carry
                plane = make(x)
                h.vp[x + 1, pl.ds(PAD, ny), :] = plane
                h.ys[0, pl.ds(x, 1), :] = plane[ny - 1:ny]
                h.ys[1, pl.ds(x, 1), :] = plane[0:1]
                here = lane == x
                high = jnp.where(here, pltpu.roll(plane, lax.rem(x + LANES - (nz - 1), LANES), 1), high)
                low = jnp.where(here, pltpu.roll(plane, x, 1), low)
                return high, low

            high, low = lax.fori_loop(0, nx, body, (zero, zero))
            h.zs[0, pl.ds(0, ny), :] = high
            h.zs[1, pl.ds(0, ny), :] = low
            for copy in copies(level, h):
                copy.start()

        def around(level, h, x):
            nx, ny = dims(level)
            vp = h.vp
            mid = vp[x + 1, pl.ds(PAD, ny), :]
            zm, zp = pltpu.roll(mid, 1, 1), pltpu.roll(mid, LANES - 1, 1)
            if level == 0:
                zlow, zhigh = h.zr[0], h.zr[1]
                zm = jnp.where(lane == 0, pltpu.roll(zlow, lax.rem(LANES - x, LANES), 1), zm)
                zp = jnp.where(lane == LANES - 1, pltpu.roll(zhigh, LANES - 1 - x, 1), zp)
            return (mid, vp[x, pl.ds(PAD, ny), :], vp[x + 2, pl.ds(PAD, ny), :],
                    vp[x + 1, pl.ds(PAD - 1, ny), :], vp[x + 1, pl.ds(PAD + 1, ny), :], zm, zp)

        def residual(level, h, x):
            g = refs.level[level]
            mid, xm, xp, ym, yp, zm, zp = around(level, h, x)
            total = g.sx[x] * xm + g.sx[x + 1] * xp + g.sym[x] * ym + g.syp[x] * yp + g.szm[x] * zm + g.szp[x] * zp
            return mid, source(level, x) - g.q[x] * mid + total

        def source(level, x):
            return rhs[x] if level == 0 else refs.level[level].f[x]

        def reaction(level, x):
            return coef_c[x] if level == 0 else refs.level[level].c[x]

        row_of = lax.broadcasted_iota(jnp.int32, (LANES, LANES), 0)
        col_of = lax.broadcasted_iota(jnp.int32, (LANES, LANES), 1)

        def pairing(level, wide, narrow):
            half = wide // 2
            return (half if level == 0 else half + jnp.where(wide >= 96, 64, 0)) == narrow

        def coarsen(level, get, put):
            nx, ny = dims(level)
            pair = refs.level[level].pair
            shrink = jnp.where(pairing(level, row_of, col_of), 0.125, 0.0).astype(jnp.bfloat16)

            def body(x, carry):
                pair[x, pl.ds(0, ny), :] = get(2 * x) + get(2 * x + 1)
                return carry

            lax.fori_loop(0, nx // 2, body, 0)
            for x in range(nx // 2):
                even = pair[x, pl.ds(0, ny // 2, 2), :]
                odd = pair[x, pl.ds(1, ny // 2, 2), :]
                put(x, exact_dot(even + odd, shrink))

        def refine(level, planes, get):
            pair = refs.level[level].pair
            grow = jnp.where(pairing(level, col_of, row_of), 1.0, 0.0).astype(jnp.bfloat16)
            for x in range(planes):
                wide = exact_dot(get(x), grow)
                rows = wide.shape[0]
                pair[x, pl.ds(0, rows, 2), :] = wide
                pair[x, pl.ds(1, rows, 2), :] = wide

        def store(ref):
            def put(x, plane):
                ref[x] = plane

            return put

        def block_to(h, which):
            def put(x, plane):
                mean = pltpu.roll(jnp.where(lane < 32, plane, 0.0), 32 * x, 1)
                rows = pl.ds(0, 12)
                h.block[which, rows, :] = mean if x == 0 else h.block[which, rows, :] + mean

            return put

        def near_copies(h):
            return [
                pltpu.make_async_remote_copy(
                    src_ref=h.block, dst_ref=h.near.at[3 - i], send_sem=h.near_send.at[i],
                    recv_sem=h.near_recv.at[3 - i], device_id={"gy": beyond("gy", dy)}, device_id_type=MESH)
                for i, dy in enumerate(NEAR)
            ]

        def all_copies(h):
            return [
                pltpu.make_async_remote_copy(
                    src_ref=h.column, dst_ref=h.all.at[1 - dz, place["gx"]], send_sem=h.all_send.at[1 - dz, dx],
                    recv_sem=h.all_recv.at[1 - dz, dx],
                    device_id={"gx": beyond("gx", dx), "gz": beyond("gz", dz)}, device_id_type=MESH)
                for dx, dz in around_xz
            ]

        def gather_near(h):
            for copy in near_copies(h):
                copy.start()

        def gather_all(h, arrays):
            for copy in near_copies(h):
                copy.wait()
            for k in range(arrays):
                h.column[k, pl.ds(0, 6), :] = h.near[0, k, pl.ds(6, 6), :]
                h.column[k, pl.ds(6, 12), :] = h.near[1, k, pl.ds(0, 12), :]
                h.column[k, pl.ds(18, 12), :] = h.block[k, pl.ds(0, 12), :]
                h.column[k, pl.ds(30, 12), :] = h.near[2, k, pl.ds(0, 12), :]
                h.column[k, pl.ds(42, 6), :] = h.near[3, k, pl.ds(0, 6), :]
            for copy in all_copies(h):
                copy.start()
            h.all[1, place["gx"]] = h.column[...]

        def gather_end(h):
            for copy in all_copies(h):
                copy.wait()

        def gathered(h, which, x, dx):
            left, here, right = (h.all[i, x, which] for i in range(3))
            plane = jnp.where(lane < 32, pltpu.roll(here, (LANES - 32 * dx) % LANES, 1), 0.0)
            plane = jnp.where((lane >= 32) & (lane < 64), pltpu.roll(right, (LANES + 32 - 32 * dx) % LANES, 1), plane)
            return jnp.where(lane >= 96, pltpu.roll(left, 96 - 32 * dx, 1), plane)

        def setup(level):
            g = refs.level[level]
            nx, ny = dims(level)
            nz = own(level)[2]
            half = 0.5 * 4.0 ** (LEVELS - 1 - level)
            finish(level, g.b)
            if WINDOW[level]:
                first_x = last_x = 0.0
            else:
                first_x, last_x = has_before["gx"], has_after["gx"]
                g.b.vp[0, pl.ds(PAD, ny), :] = g.b.vp[0, pl.ds(PAD, ny), :] * first_x
                g.b.vp[nx + 1, pl.ds(PAD, ny), :] = g.b.vp[nx + 1, pl.ds(PAD, ny), :] * last_x
            cells_y = own(level)[1]
            row = lax.broadcasted_iota(jnp.int32, (ny, 1), 0) + place["gy"] * cells_y - FIRST_ROW[level]
            if level == 0:
                column, used = lane, lane >= 0
            else:
                column = jnp.where(lane < 96, lane, lane - LANES)
                used = (column < 2 * nz) & (column >= -nz) if WINDOW[level] else (lane < nz)
            column = column + place["gz"] * nz
            keep_ym = jnp.where(row == 0, 0.0, 1.0)
            keep_yp = jnp.where(row == cells_y * count["gy"] - 1, 0.0, 1.0)
            keep_zm = jnp.where(column == 0, 0.0, 1.0)
            keep_zp = jnp.where(column == nz * count["gz"] - 1, 0.0, 1.0)

            def body(x, carry):
                mid, xm, xp, ym, yp, zm, zp = around(level, g.b, x)
                fxm, fxp = half * (mid + xm), half * (mid + xp)
                fym, fyp = half * (mid + ym * keep_ym), half * (mid + yp * keep_yp)
                fzm, fzp = half * (mid + zm * keep_zm), half * (mid + zp * keep_zp)
                q = reaction(level, x) + (fxm + fxp + fym + fyp + fzm + fzp)
                g.q[x] = q
                g.rq[x] = jnp.where(used, 1.0 / q, 0.0)
                g.sx[x] = fxm * jnp.where(x == 0, first_x, 1.0)
                g.sym[x] = fym * keep_ym
                g.syp[x] = fyp * keep_yp
                g.szm[x] = fzm * keep_zm
                g.szp[x] = fzp * keep_zp
                return carry

            lax.fori_loop(0, nx, body, 0)
            last = g.b.vp[nx, pl.ds(PAD, ny), :] + g.b.vp[nx + 1, pl.ds(PAD, ny), :]
            g.sx[nx] = half * last * last_x

        def planes_of(level, h):
            ny = dims(level)[1]
            return lambda x: h.vp[x + 1, pl.ds(PAD, ny), :]

        levels = refs.level
        (_, first), (carry_e, weight_r) = chebyshev(2)
        of_f, of_bc = refs.gather

        def start_down(level):
            g = levels[level]
            sweep(level, lambda x: source(level, x) * g.rq[x] * first, g.it[0])

        def go_down(level):
            g = levels[level]

            def second(x):
                mid, rest = residual(level, g.it[0], x)
                return mid * (1.0 + carry_e) + weight_r * rest * g.rq[x]

            finish(level, g.it[0])
            sweep(level, second, g.it[1])

        def leave(level, put):
            g = levels[level]
            finish(level, g.it[1])
            coarsen(level, lambda x: residual(level, g.it[1], x)[1], put)

        def go_up(level, begun, ended, put):
            g = levels[level]

            def third(x):
                mid, rest = residual(level, begun, x)
                update = first * rest * g.rq[x]
                g.e[x] = update
                return mid + update

            sweep(level, third, ended)
            finish(level, ended)

            def last(x, carry):
                mid, rest = residual(level, ended, x)
                put(x, mid + carry_e * g.e[x] + weight_r * rest * g.rq[x])
                return carry

            lax.fori_loop(0, dims(level)[0], last, 0)

        sweep(0, lambda x: coef_b[x], levels[0].b)
        coarsen(0, lambda x: coef_b[x], store(levels[1].f))
        coarsen(0, lambda x: coef_c[x], store(levels[1].c))
        sweep(1, lambda x: levels[1].f[x], levels[1].b)
        coarsen(1, lambda x: levels[1].f[x], block_to(of_bc, 0))
        coarsen(1, lambda x: levels[1].c[x], block_to(of_bc, 1))
        gather_near(of_bc)

        setup(0)
        start_down(0)
        gather_all(of_bc, 2)
        setup(1)
        go_down(0)
        gather_end(of_bc)
        for dx in range(4):
            def spread(x, carry, dx=dx):
                levels[2].b.vp[4 * x + dx + 1, pl.ds(PAD, 48), :] = gathered(of_bc, 0, x, dx)
                levels[2].c[4 * x + dx] = gathered(of_bc, 1, x, dx)
                return carry

            lax.fori_loop(0, 4, spread, 0)
        coarsen(2, planes_of(2, levels[2].b), store(levels[3].f))
        sweep(3, lambda x: levels[3].f[x], levels[3].b)
        coarsen(2, lambda x: levels[2].c[x], store(levels[3].c))
        setup(2)
        setup(3)
        leave(0, store(levels[1].f))

        start_down(1)
        go_down(1)
        leave(1, block_to(of_f, 0))
        gather_near(of_f)
        gather_all(of_f, 1)
        gather_end(of_f)
        for dx in range(4):
            def spread_f(x, carry, dx=dx):
                levels[2].f[4 * x + dx] = gathered(of_f, 0, x, dx)
                return carry

            lax.fori_loop(0, 4, spread_f, 0)

        start_down(2)
        go_down(2)
        leave(2, store(levels[3].f))

        g = levels[3]
        steps = chebyshev(COARSE_SWEEPS)

        def begin(x):
            update = source(3, x) * g.rq[x] * steps[0][1]
            g.e[x] = update
            return update

        sweep(3, begin, g.it[0])
        for step in range(1, COARSE_SWEEPS):
            def advance(x, step=step):
                mid, rest = residual(3, g.it[(step - 1) % 2], x)
                update = steps[step][0] * g.e[x] + steps[step][1] * rest * g.rq[x]
                g.e[x] = update
                return mid + update

            sweep(3, advance, g.it[step % 2])

        refine(2, 8, planes_of(3, g.it[(COARSE_SWEEPS - 1) % 2]))
        g = levels[2]
        sweep(2, lambda x: planes_of(2, g.it[1])(x) + g.pair[x // 2], g.it[0])
        go_up(2, g.it[0], g.it[1], store(g.f))

        g = levels[1]
        start_x = place["gx"] * own(2)[0]
        refine(1, 6, lambda x: levels[2].f[jnp.clip(start_x + x - 1, 0, 15), pl.ds(16, 16), :])
        rows = pl.ds(PAD - 1, 26)
        for x in range(10):
            g.it[2].vp[x, rows, :] = g.it[1].vp[x, rows, :] + g.pair[(x + 1) // 2, pl.ds(3, 26), :]
        go_up(1, g.it[2], g.it[3], store(g.f))

        g = levels[0]
        refine(0, 8, lambda x: levels[1].f[x])
        sweep(0, lambda x: planes_of(0, g.it[1])(x) + g.pair[x // 2], g.it[2])
        finish(0, g.it[2])
        go_up(0, g.it[2], g.it[3], store(out))

    return kernel


class Plan:
    def __init__(self, shape):
        self.shapes = []
        self.tree = Names()
        self.tree.level = []
        for level in range(LEVELS):
            nx, ny = WINDOW[level] or tuple(n >> level for n in shape)[:2]
            g = Names()

            def planes(n, ny=ny):
                return self.add(pltpu.VMEM((n, ny, LANES), jnp.float32))

            def halo(exchanged, nx=nx, ny=ny):
                h = Names()
                h.vp = self.add(pltpu.VMEM((nx + 2, round_up(ny) + 2 * PAD, LANES), jnp.float32))
                if exchanged:
                    for name, rows in (("zs", ny), ("zr", ny), ("ys", nx), ("yr", nx)):
                        setattr(h, name, self.add(pltpu.VMEM((2, round_up(rows), LANES), jnp.float32)))
                    h.send = self.add(pltpu.SemaphoreType.DMA((6,)))
                    h.recv = self.add(pltpu.SemaphoreType.DMA((6,)))
                return h

            exchanged = WINDOW[level] is None
            g.b = halo(exchanged)
            g.sx = planes(nx + 1)
            for name in ("sym", "syp", "szm", "szp", "q", "rq", "e"):
                setattr(g, name, planes(nx))
            if level > 0:
                g.f = planes(nx)
                g.c = planes(nx)
            if level == 1:
                g.pair = self.add(pltpu.VMEM((nx // 2 + 2, 32, LANES), jnp.float32))
            elif level < LEVELS - 1:
                g.pair = planes(nx // 2)
            g.it = [halo(exchanged) for _ in range(4 if exchanged else 2)]
            self.tree.level.append(g)
        self.tree.gather = [self.gathered(1), self.gathered(2)]

    def gathered(self, arrays):
        h = Names()
        h.block = self.add(pltpu.VMEM((arrays, 16, LANES), jnp.float32))
        h.near = self.add(pltpu.VMEM((4, arrays, 16, LANES), jnp.float32))
        h.column = self.add(pltpu.VMEM((arrays, 48, LANES), jnp.float32))
        h.all = self.add(pltpu.VMEM((3, 4, arrays, 48, LANES), jnp.float32))
        h.near_send = self.add(pltpu.SemaphoreType.DMA((4,)))
        h.near_recv = self.add(pltpu.SemaphoreType.DMA((4,)))
        h.all_send = self.add(pltpu.SemaphoreType.DMA((3, 4)))
        h.all_recv = self.add(pltpu.SemaphoreType.DMA((3, 4)))
        return h

    def add(self, shape):
        self.shapes.append(shape)
        return len(self.shapes) - 1

    def unpack(self, refs):
        def walk(node):
            if isinstance(node, int):
                return refs[node]
            if isinstance(node, list):
                return [walk(item) for item in node]
            result = Names()
            for name, item in vars(node).items():
                setattr(result, name, walk(item))
            return result

        return walk(self.tree)


def solution(mesh):
    sizes = dict(mesh.shape)

    def local(rhs, coef_b, coef_c):
        shape = rhs.shape
        plan = Plan(shape)
        return pl.pallas_call(
            make_kernel(shape, sizes, plan),
            out_shape=jax.ShapeDtypeStruct(shape, jnp.float32),
            in_specs=[pl.BlockSpec(memory_space=pltpu.VMEM)] * 3,
            out_specs=pl.BlockSpec(memory_space=pltpu.VMEM),
            scratch_shapes=plan.shapes,
            compiler_params=pltpu.CompilerParams(
                collective_id=0, has_side_effects=True, vmem_limit_bytes=40 * 2**20),
        )(rhs, coef_b, coef_c)

    return jax.shard_map(
        local,
        mesh=mesh,
        in_specs=(P(*AXES),) * 3,
        out_specs=P(*AXES),
        check_vma=False,
    )
```

```python
import jax
import jax.numpy as jnp
from jax import lax
from jax.experimental import pallas as pl
from jax.experimental.pallas import tpu as pltpu
from jax.sharding import PartitionSpec as P

LEVELS = 4
COARSE_SWEEPS = 6
CENTRE = 1.1
RADIUS = 0.9
LANES = 128
PAD = 8

MESH = pl.DeviceIdType.MESH
AXES = ("gx", "gy", "gz")


def chebyshev(sweeps):
    ratio = RADIUS / CENTRE
    factors = [(0.0, 1.0 / CENTRE)]
    for _ in range(sweeps - 1):
        following = 1.0 / (2.0 * CENTRE / RADIUS - ratio)
        factors.append((following * ratio, 2.0 * following / RADIUS))
        ratio = following
    return factors


def round_up(value):
    return -(-value // 8) * 8


class Names:
    pass


def exact_dot(left, matrix):
    high = left.astype(jnp.bfloat16)
    rest = left - high.astype(jnp.float32)
    middle = rest.astype(jnp.bfloat16)
    low = (rest - middle.astype(jnp.float32)).astype(jnp.bfloat16)
    total = jnp.dot(low, matrix, preferred_element_type=jnp.float32)
    total = total + jnp.dot(middle, matrix, preferred_element_type=jnp.float32)
    return total + jnp.dot(high, matrix, preferred_element_type=jnp.float32)


WINDOW = (None, None, (16, 48), (8, 24))
FIRST_ROW = (0, 0, 18, 9)
NEAR = (-2, -1, 1, 2)
TOGETHER = 8


def make_kernel(shape, sizes, plan):
    count = {axis: sizes[axis] for axis in AXES}

    def kernel(rhs, coef_b, coef_c, out, *scratch):
        refs = plan.unpack(scratch)
        place = {axis: lax.axis_index(axis) for axis in AXES}

        def beyond(axis, step):
            return lax.rem(place[axis] + count[axis] + step, count[axis])

        after = {axis: beyond(axis, 1) for axis in AXES}
        before = {axis: beyond(axis, -1) for axis in AXES}
        has_before = {a: jnp.where(place[a] > 0, 1.0, 0.0).astype(jnp.float32) for a in AXES}
        has_after = {a: jnp.where(place[a] < count[a] - 1, 1.0, 0.0).astype(jnp.float32) for a in AXES}
        around_xz = [(dx, dz) for dx in range(4) for dz in (-1, 0, 1) if (dx, dz) != (0, 0)]

        barrier = pltpu.get_barrier_semaphore()
        for dy in NEAR:
            pl.semaphore_signal(barrier, inc=1, device_id={"gy": beyond("gy", dy)}, device_id_type=MESH)
        for dx, dz in around_xz:
            pl.semaphore_signal(barrier, inc=1, device_id={"gx": beyond("gx", dx), "gz": beyond("gz", dz)},
                                device_id_type=MESH)
        pl.semaphore_wait(barrier, len(NEAR) + len(around_xz))

        lane = lax.broadcasted_iota(jnp.int32, (1, LANES), 1)

        def own(level):
            return tuple(n >> level for n in shape)

        def dims(level):
            return WINDOW[level] or own(level)[:2]

        def clear_rim(level, h):
            nx, ny = dims(level)
            h.vp[0] = jnp.zeros(h.vp.shape[1:], jnp.float32)
            h.vp[nx + 1] = jnp.zeros(h.vp.shape[1:], jnp.float32)
            rim = jnp.zeros((nx, PAD, LANES), jnp.float32)
            h.vp[pl.ds(1, nx), pl.ds(0, PAD), :] = rim
            h.vp[pl.ds(1, nx), pl.ds(PAD + ny, PAD), :] = rim

        for level in range(LEVELS):
            if WINDOW[level]:
                for h in [refs.level[level].b] + refs.level[level].it:
                    clear_rim(level, h)

        def copies(level, h):
            nx, ny = dims(level)
            rows = pl.ds(PAD, round_up(ny))
            vp, zs, zr, ys, yr = h.vp, h.zs, h.zr, h.ys, h.yr
            pairs = (
                (vp.at[nx, rows], vp.at[0, rows], "gx", after),
                (vp.at[1, rows], vp.at[nx + 1, rows], "gx", before),
                (ys.at[0], yr.at[0], "gy", after),
                (ys.at[1], yr.at[1], "gy", before),
                (zs.at[0], zr.at[0], "gz", after),
                (zs.at[1], zr.at[1], "gz", before),
            )
            return [
                pltpu.make_async_remote_copy(
                    src_ref=src, dst_ref=dst, send_sem=h.send.at[i], recv_sem=h.recv.at[i],
                    device_id={axis: where[axis]}, device_id_type=MESH)
                for i, (src, dst, axis, where) in enumerate(pairs)
            ]

        def finish(level, h):
            if WINDOW[level]:
                return
            nx, ny = dims(level)
            nz = own(level)[2]
            for copy in copies(level, h):
                copy.wait()
            for x in range(nx):
                h.vp[x + 1, pl.ds(PAD - 1, 1), :] = h.yr[0, pl.ds(x, 1), :]
                h.vp[x + 1, pl.ds(PAD + ny, 1), :] = h.yr[1, pl.ds(x, 1), :]
            if level > 0:
                low, high = h.zr[0, pl.ds(0, ny), :], h.zr[1, pl.ds(0, ny), :]
                for x in range(nx):
                    plane = h.vp[x + 1, pl.ds(PAD, ny), :]
                    plane = jnp.where(lane == LANES - 1, pltpu.roll(low, LANES - 1 - x, 1), plane)
                    h.vp[x + 1, pl.ds(PAD, ny), :] = jnp.where(lane == nz, pltpu.roll(high, nz - x, 1), plane)

        def planes(n, make, put, carry=None):
            step = min(n, TOGETHER)

            def body(i, carry):
                made = [make(i * step + k) for k in range(step)]
                for k in range(step):
                    if carry is None:
                        put(i * step + k, made[k])
                    else:
                        carry = put(i * step + k, made[k], carry)
                return carry

            if carry is not None:
                return lax.fori_loop(0, n // step, body, carry)

            def plain(i, zero):
                body(i, None)
                return zero

            lax.fori_loop(0, n // step, plain, 0)

        def sweep(level, make, h):
            nx, ny = dims(level)
            nz = own(level)[2]
            def keep(x, plane):
                h.vp[x + 1, pl.ds(PAD, ny), :] = plane

            if WINDOW[level]:
                planes(nx, make, keep)
                return
            zero = jnp.zeros((ny, LANES), jnp.float32)

            def pack(x, plane, carry):
                keep(x, plane)
                high, low = carry
                h.ys[0, pl.ds(x, 1), :] = plane[ny - 1:ny]
                h.ys[1, pl.ds(x, 1), :] = plane[0:1]
                here = lane == x
                high = jnp.where(here, pltpu.roll(plane, lax.rem(x + LANES - (nz - 1), LANES), 1), high)
                low = jnp.where(here, pltpu.roll(plane, x, 1), low)
                return high, low

            high, low = planes(nx, make, pack, (zero, zero))
            h.zs[0, pl.ds(0, ny), :] = high
            h.zs[1, pl.ds(0, ny), :] = low
            for copy in copies(level, h):
                copy.start()

        def around(level, h, x):
            nx, ny = dims(level)
            vp = h.vp
            mid = vp[x + 1, pl.ds(PAD, ny), :]
            zm, zp = pltpu.roll(mid, 1, 1), pltpu.roll(mid, LANES - 1, 1)
            if level == 0:
                zlow, zhigh = h.zr[0], h.zr[1]
                zm = jnp.where(lane == 0, pltpu.roll(zlow, lax.rem(LANES - x, LANES), 1), zm)
                zp = jnp.where(lane == LANES - 1, pltpu.roll(zhigh, LANES - 1 - x, 1), zp)
            return (mid, vp[x, pl.ds(PAD, ny), :], vp[x + 2, pl.ds(PAD, ny), :],
                    vp[x + 1, pl.ds(PAD - 1, ny), :], vp[x + 1, pl.ds(PAD + 1, ny), :], zm, zp)

        def residual(level, h, x):
            g = refs.level[level]
            mid, xm, xp, ym, yp, zm, zp = around(level, h, x)
            total = g.sx[x] * xm + g.sx[x + 1] * xp + g.sym[x] * ym + g.syp[x] * yp + g.szm[x] * zm + g.szp[x] * zp
            return mid, source(level, x) - g.q[x] * mid + total

        def source(level, x):
            return rhs[x] if level == 0 else refs.level[level].f[x]

        def reaction(level, x):
            return coef_c[x] if level == 0 else refs.level[level].c[x]

        row_of = lax.broadcasted_iota(jnp.int32, (LANES, LANES), 0)
        col_of = lax.broadcasted_iota(jnp.int32, (LANES, LANES), 1)

        def pairing(level, wide, narrow):
            half = wide // 2
            return (half if level == 0 else half + jnp.where(wide >= 96, 64, 0)) == narrow

        def coarsen(level, get, put):
            nx, ny = dims(level)
            pair = refs.level[level].pair
            shrink = jnp.where(pairing(level, row_of, col_of), 0.125, 0.0).astype(jnp.bfloat16)

            def put_pair(x, plane):
                pair[x, pl.ds(0, ny), :] = plane

            planes(nx // 2, lambda x: get(2 * x) + get(2 * x + 1), put_pair)
            for x in range(nx // 2):
                even = pair[x, pl.ds(0, ny // 2, 2), :]
                odd = pair[x, pl.ds(1, ny // 2, 2), :]
                put(x, exact_dot(even + odd, shrink))

        def refine(level, planes, get):
            pair = refs.level[level].pair
            grow = jnp.where(pairing(level, col_of, row_of), 1.0, 0.0).astype(jnp.bfloat16)
            for x in range(planes):
                wide = exact_dot(get(x), grow)
                rows = wide.shape[0]
                pair[x, pl.ds(0, rows, 2), :] = wide
                pair[x, pl.ds(1, rows, 2), :] = wide

        def store(ref):
            def put(x, plane):
                ref[x] = plane

            return put

        def block_to(h, which):
            def put(x, plane):
                mean = pltpu.roll(jnp.where(lane < 32, plane, 0.0), 32 * x, 1)
                rows = pl.ds(0, 12)
                h.block[which, rows, :] = mean if x == 0 else h.block[which, rows, :] + mean

            return put

        def near_copies(h):
            return [
                pltpu.make_async_remote_copy(
                    src_ref=h.block, dst_ref=h.near.at[3 - i], send_sem=h.near_send.at[i],
                    recv_sem=h.near_recv.at[3 - i], device_id={"gy": beyond("gy", dy)}, device_id_type=MESH)
                for i, dy in enumerate(NEAR)
            ]

        def all_copies(h):
            return [
                pltpu.make_async_remote_copy(
                    src_ref=h.column, dst_ref=h.all.at[1 - dz, place["gx"]], send_sem=h.all_send.at[1 - dz, dx],
                    recv_sem=h.all_recv.at[1 - dz, dx],
                    device_id={"gx": beyond("gx", dx), "gz": beyond("gz", dz)}, device_id_type=MESH)
                for dx, dz in around_xz
            ]

        def gather_near(h):
            for copy in near_copies(h):
                copy.start()

        def gather_all(h, arrays):
            for copy in near_copies(h):
                copy.wait()
            for k in range(arrays):
                h.column[k, pl.ds(0, 6), :] = h.near[0, k, pl.ds(6, 6), :]
                h.column[k, pl.ds(6, 12), :] = h.near[1, k, pl.ds(0, 12), :]
                h.column[k, pl.ds(18, 12), :] = h.block[k, pl.ds(0, 12), :]
                h.column[k, pl.ds(30, 12), :] = h.near[2, k, pl.ds(0, 12), :]
                h.column[k, pl.ds(42, 6), :] = h.near[3, k, pl.ds(0, 6), :]
            for copy in all_copies(h):
                copy.start()
            h.all[1, place["gx"]] = h.column[...]

        def gather_end(h):
            for copy in all_copies(h):
                copy.wait()

        def gathered(h, which, x, dx):
            left, here, right = (h.all[i, x, which] for i in range(3))
            plane = jnp.where(lane < 32, pltpu.roll(here, (LANES - 32 * dx) % LANES, 1), 0.0)
            plane = jnp.where((lane >= 32) & (lane < 64), pltpu.roll(right, (LANES + 32 - 32 * dx) % LANES, 1), plane)
            return jnp.where(lane >= 96, pltpu.roll(left, 96 - 32 * dx, 1), plane)

        def setup(level):
            g = refs.level[level]
            nx, ny = dims(level)
            nz = own(level)[2]
            half = 0.5 * 4.0 ** (LEVELS - 1 - level)
            finish(level, g.b)
            if WINDOW[level]:
                first_x = last_x = 0.0
            else:
                first_x, last_x = has_before["gx"], has_after["gx"]
                g.b.vp[0, pl.ds(PAD, ny), :] = g.b.vp[0, pl.ds(PAD, ny), :] * first_x
                g.b.vp[nx + 1, pl.ds(PAD, ny), :] = g.b.vp[nx + 1, pl.ds(PAD, ny), :] * last_x
            cells_y = own(level)[1]
            row = lax.broadcasted_iota(jnp.int32, (ny, 1), 0) + place["gy"] * cells_y - FIRST_ROW[level]
            if level == 0:
                column, used = lane, lane >= 0
            else:
                column = jnp.where(lane < 96, lane, lane - LANES)
                used = (column < 2 * nz) & (column >= -nz) if WINDOW[level] else (lane < nz)
            column = column + place["gz"] * nz
            keep_ym = jnp.where(row == 0, 0.0, 1.0)
            keep_yp = jnp.where(row == cells_y * count["gy"] - 1, 0.0, 1.0)
            keep_zm = jnp.where(column == 0, 0.0, 1.0)
            keep_zp = jnp.where(column == nz * count["gz"] - 1, 0.0, 1.0)

            def make(x):
                mid, xm, xp, ym, yp, zm, zp = around(level, g.b, x)
                fxm, fxp = half * (mid + xm), half * (mid + xp)
                fym, fyp = half * (mid + ym * keep_ym), half * (mid + yp * keep_yp)
                fzm, fzp = half * (mid + zm * keep_zm), half * (mid + zp * keep_zp)
                q = reaction(level, x) + (fxm + fxp + fym + fyp + fzm + fzp)
                return (q, jnp.where(used, 1.0 / q, 0.0), fxm * jnp.where(x == 0, first_x, 1.0),
                        fym * keep_ym, fyp * keep_yp, fzm * keep_zm, fzp * keep_zp)

            def put(x, values):
                for name, value in zip(("q", "rq", "sx", "sym", "syp", "szm", "szp"), values):
                    getattr(g, name)[x] = value

            planes(nx, make, put)
            last = g.b.vp[nx, pl.ds(PAD, ny), :] + g.b.vp[nx + 1, pl.ds(PAD, ny), :]
            g.sx[nx] = half * last * last_x

        def planes_of(level, h):
            ny = dims(level)[1]
            return lambda x: h.vp[x + 1, pl.ds(PAD, ny), :]

        levels = refs.level
        (_, first), (carry_e, weight_r) = chebyshev(2)
        of_f, of_bc = refs.gather

        def start_down(level):
            g = levels[level]
            sweep(level, lambda x: source(level, x) * g.rq[x] * first, g.it[0])

        def go_down(level):
            g = levels[level]

            def second(x):
                mid, rest = residual(level, g.it[0], x)
                return mid * (1.0 + carry_e) + weight_r * rest * g.rq[x]

            finish(level, g.it[0])
            sweep(level, second, g.it[1])

        def leave(level, put):
            g = levels[level]
            finish(level, g.it[1])
            coarsen(level, lambda x: residual(level, g.it[1], x)[1], put)

        def go_up(level, begun, ended, put):
            g = levels[level]

            def third(x):
                mid, rest = residual(level, begun, x)
                update = first * rest * g.rq[x]
                g.e[x] = update
                return mid + update

            sweep(level, third, ended)
            finish(level, ended)

            def last(x):
                mid, rest = residual(level, ended, x)
                return mid + carry_e * g.e[x] + weight_r * rest * g.rq[x]

            planes(dims(level)[0], last, put)

        sweep(0, lambda x: coef_b[x], levels[0].b)
        coarsen(0, lambda x: coef_b[x], store(levels[1].f))
        coarsen(0, lambda x: coef_c[x], store(levels[1].c))
        sweep(1, lambda x: levels[1].f[x], levels[1].b)
        coarsen(1, lambda x: levels[1].f[x], block_to(of_bc, 0))
        coarsen(1, lambda x: levels[1].c[x], block_to(of_bc, 1))
        gather_near(of_bc)

        setup(0)
        start_down(0)
        gather_all(of_bc, 2)
        setup(1)
        go_down(0)
        gather_end(of_bc)
        for dx in range(4):
            def spread(x, carry, dx=dx):
                levels[2].b.vp[4 * x + dx + 1, pl.ds(PAD, 48), :] = gathered(of_bc, 0, x, dx)
                levels[2].c[4 * x + dx] = gathered(of_bc, 1, x, dx)
                return carry

            lax.fori_loop(0, 4, spread, 0)
        coarsen(2, planes_of(2, levels[2].b), store(levels[3].f))
        sweep(3, lambda x: levels[3].f[x], levels[3].b)
        coarsen(2, lambda x: levels[2].c[x], store(levels[3].c))
        setup(2)
        setup(3)
        leave(0, store(levels[1].f))

        start_down(1)
        go_down(1)
        leave(1, block_to(of_f, 0))
        gather_near(of_f)
        gather_all(of_f, 1)
        gather_end(of_f)
        for dx in range(4):
            def spread_f(x, carry, dx=dx):
                levels[2].f[4 * x + dx] = gathered(of_f, 0, x, dx)
                return carry

            lax.fori_loop(0, 4, spread_f, 0)

        start_down(2)
        go_down(2)
        leave(2, store(levels[3].f))

        g = levels[3]
        steps = chebyshev(COARSE_SWEEPS)

        def begin(x):
            update = source(3, x) * g.rq[x] * steps[0][1]
            g.e[x] = update
            return update

        sweep(3, begin, g.it[0])
        for step in range(1, COARSE_SWEEPS):
            def advance(x, step=step):
                mid, rest = residual(3, g.it[(step - 1) % 2], x)
                update = steps[step][0] * g.e[x] + steps[step][1] * rest * g.rq[x]
                g.e[x] = update
                return mid + update

            sweep(3, advance, g.it[step % 2])

        refine(2, 8, planes_of(3, g.it[(COARSE_SWEEPS - 1) % 2]))
        g = levels[2]
        sweep(2, lambda x: planes_of(2, g.it[1])(x) + g.pair[x // 2], g.it[0])
        go_up(2, g.it[0], g.it[1], store(g.f))

        g = levels[1]
        start_x = place["gx"] * own(2)[0]
        refine(1, 6, lambda x: levels[2].f[jnp.clip(start_x + x - 1, 0, 15), pl.ds(16, 16), :])
        rows = pl.ds(PAD - 1, 26)
        for x in range(10):
            g.it[2].vp[x, rows, :] = g.it[1].vp[x, rows, :] + g.pair[(x + 1) // 2, pl.ds(3, 26), :]
        go_up(1, g.it[2], g.it[3], store(g.f))

        g = levels[0]
        refine(0, 8, lambda x: levels[1].f[x])
        sweep(0, lambda x: planes_of(0, g.it[1])(x) + g.pair[x // 2], g.it[2])
        finish(0, g.it[2])
        go_up(0, g.it[2], g.it[3], store(out))

    return kernel


class Plan:
    def __init__(self, shape):
        self.shapes = []
        self.tree = Names()
        self.tree.level = []
        for level in range(LEVELS):
            nx, ny = WINDOW[level] or tuple(n >> level for n in shape)[:2]
            g = Names()

            def planes(n, ny=ny):
                return self.add(pltpu.VMEM((n, ny, LANES), jnp.float32))

            def halo(exchanged, nx=nx, ny=ny):
                h = Names()
                h.vp = self.add(pltpu.VMEM((nx + 2, round_up(ny) + 2 * PAD, LANES), jnp.float32))
                if exchanged:
                    for name, rows in (("zs", ny), ("zr", ny), ("ys", nx), ("yr", nx)):
                        setattr(h, name, self.add(pltpu.VMEM((2, round_up(rows), LANES), jnp.float32)))
                    h.send = self.add(pltpu.SemaphoreType.DMA((6,)))
                    h.recv = self.add(pltpu.SemaphoreType.DMA((6,)))
                return h

            exchanged = WINDOW[level] is None
            g.b = halo(exchanged)
            g.sx = planes(nx + 1)
            for name in ("sym", "syp", "szm", "szp", "q", "rq", "e"):
                setattr(g, name, planes(nx))
            if level > 0:
                g.f = planes(nx)
                g.c = planes(nx)
            if level == 1:
                g.pair = self.add(pltpu.VMEM((nx // 2 + 2, 32, LANES), jnp.float32))
            elif level < LEVELS - 1:
                g.pair = planes(nx // 2)
            g.it = [halo(exchanged) for _ in range(4 if exchanged else 2)]
            self.tree.level.append(g)
        self.tree.gather = [self.gathered(1), self.gathered(2)]

    def gathered(self, arrays):
        h = Names()
        h.block = self.add(pltpu.VMEM((arrays, 16, LANES), jnp.float32))
        h.near = self.add(pltpu.VMEM((4, arrays, 16, LANES), jnp.float32))
        h.column = self.add(pltpu.VMEM((arrays, 48, LANES), jnp.float32))
        h.all = self.add(pltpu.VMEM((3, 4, arrays, 48, LANES), jnp.float32))
        h.near_send = self.add(pltpu.SemaphoreType.DMA((4,)))
        h.near_recv = self.add(pltpu.SemaphoreType.DMA((4,)))
        h.all_send = self.add(pltpu.SemaphoreType.DMA((3, 4)))
        h.all_recv = self.add(pltpu.SemaphoreType.DMA((3, 4)))
        return h

    def add(self, shape):
        self.shapes.append(shape)
        return len(self.shapes) - 1

    def unpack(self, refs):
        def walk(node):
            if isinstance(node, int):
                return refs[node]
            if isinstance(node, list):
                return [walk(item) for item in node]
            result = Names()
            for name, item in vars(node).items():
                setattr(result, name, walk(item))
            return result

        return walk(self.tree)


def solution(mesh):
    sizes = dict(mesh.shape)

    def local(rhs, coef_b, coef_c):
        shape = rhs.shape
        plan = Plan(shape)
        return pl.pallas_call(
            make_kernel(shape, sizes, plan),
            out_shape=jax.ShapeDtypeStruct(shape, jnp.float32),
            in_specs=[pl.BlockSpec(memory_space=pltpu.VMEM)] * 3,
            out_specs=pl.BlockSpec(memory_space=pltpu.VMEM),
            scratch_shapes=plan.shapes,
            compiler_params=pltpu.CompilerParams(
                collective_id=0, has_side_effects=True, vmem_limit_bytes=40 * 2**20),
        )(rhs, coef_b, coef_c)

    return jax.shard_map(
        local,
        mesh=mesh,
        in_specs=(P(*AXES),) * 3,
        out_specs=P(*AXES),
        check_vma=False,
    )
```

```python
import jax
import jax.numpy as jnp
from jax import lax
from jax.experimental import pallas as pl
from jax.experimental.pallas import tpu as pltpu
from jax.sharding import PartitionSpec as P

LEVELS = 4
COARSE_SWEEPS = 6
CENTRE = 1.1
RADIUS = 0.9
LANES = 128
PAD = 8

MESH = pl.DeviceIdType.MESH
AXES = ("gx", "gy", "gz")


def chebyshev(sweeps):
    ratio = RADIUS / CENTRE
    factors = [(0.0, 1.0 / CENTRE)]
    for _ in range(sweeps - 1):
        following = 1.0 / (2.0 * CENTRE / RADIUS - ratio)
        factors.append((following * ratio, 2.0 * following / RADIUS))
        ratio = following
    return factors


def round_up(value):
    return -(-value // 8) * 8


class Names:
    pass


def exact_dot(left, matrix):
    high = left.astype(jnp.bfloat16)
    rest = left - high.astype(jnp.float32)
    middle = rest.astype(jnp.bfloat16)
    low = (rest - middle.astype(jnp.float32)).astype(jnp.bfloat16)
    total = jnp.dot(low, matrix, preferred_element_type=jnp.float32)
    total = total + jnp.dot(middle, matrix, preferred_element_type=jnp.float32)
    return total + jnp.dot(high, matrix, preferred_element_type=jnp.float32)


WINDOW = (None, (16, 40), (16, 48), (8, 24))
FIRST_ROW = (0, 8, 18, 9)
NEAR = (-2, -1, 1, 2)
TOGETHER = 8


def make_kernel(shape, sizes, plan):
    count = {axis: sizes[axis] for axis in AXES}

    def kernel(rhs, coef_b, coef_c, out, *scratch):
        refs = plan.unpack(scratch)
        place = {axis: lax.axis_index(axis) for axis in AXES}

        def beyond(axis, step):
            return lax.rem(place[axis] + count[axis] + step, count[axis])

        after = {axis: beyond(axis, 1) for axis in AXES}
        before = {axis: beyond(axis, -1) for axis in AXES}
        def own(level):
            return tuple(n >> level for n in shape)

        def first_plane(level):
            if level > 1:
                return 0
            return place["gx"] * own(level)[0] - (4 if level == 1 else 0)

        sides = (-1, 0, 1)
        around_all = [(dx, dy, dz) for dx in sides for dy in sides for dz in sides if (dx, dy, dz) != (0, 0, 0)]
        around_xz = [(dx, dz) for dx in range(4) for dz in (-1, 0, 1) if (dx, dz) != (0, 0)]

        barrier = pltpu.get_barrier_semaphore()
        partners = [offset for offset in around_all if sum(map(abs, offset)) == 1]
        for offset in partners:
            pl.semaphore_signal(barrier, inc=1, device_id={a: beyond(a, d) for a, d in zip(AXES, offset)},
                                device_id_type=MESH)
        pl.semaphore_wait(barrier, len(partners))

        lane = lax.broadcasted_iota(jnp.int32, (1, LANES), 1)

        def dims(level):
            return WINDOW[level] or own(level)[:2]

        def clear_rim(level, h):
            nx, ny = dims(level)
            h.vp[0] = jnp.zeros(h.vp.shape[1:], jnp.float32)
            h.vp[nx + 1] = jnp.zeros(h.vp.shape[1:], jnp.float32)
            rim = jnp.zeros((nx, PAD, LANES), jnp.float32)
            h.vp[pl.ds(1, nx), pl.ds(0, PAD), :] = rim
            h.vp[pl.ds(1, nx), pl.ds(PAD + ny, PAD), :] = rim

        for level in range(LEVELS):
            if WINDOW[level]:
                for h in [refs.level[level].b] + refs.level[level].it:
                    clear_rim(level, h)

        def copies(level, h):
            nx, ny = dims(level)
            rows = pl.ds(PAD, round_up(ny))
            vp, zs, zr, ys, yr = h.vp, h.zs, h.zr, h.ys, h.yr
            pairs = (
                (vp.at[nx, rows], vp.at[0, rows], "gx", after),
                (vp.at[1, rows], vp.at[nx + 1, rows], "gx", before),
                (ys.at[0], yr.at[0], "gy", after),
                (ys.at[1], yr.at[1], "gy", before),
                (zs.at[0], zr.at[0], "gz", after),
                (zs.at[1], zr.at[1], "gz", before),
            )
            return [
                pltpu.make_async_remote_copy(
                    src_ref=src, dst_ref=dst, send_sem=h.send.at[i], recv_sem=h.recv.at[i],
                    device_id={axis: where[axis]}, device_id_type=MESH)
                for i, (src, dst, axis, where) in enumerate(pairs)
            ]

        def finish(level, h):
            if WINDOW[level]:
                return
            nx, ny = dims(level)
            for copy in copies(level, h):
                copy.wait()
            for x in range(nx):
                h.vp[x + 1, pl.ds(PAD - 1, 1), :] = h.yr[0, pl.ds(x, 1), :]
                h.vp[x + 1, pl.ds(PAD + ny, 1), :] = h.yr[1, pl.ds(x, 1), :]

        def planes(n, make, put, carry=None):
            step = min(n, TOGETHER)

            def body(i, carry):
                made = [make(i * step + k) for k in range(step)]
                for k in range(step):
                    if carry is None:
                        put(i * step + k, made[k])
                    else:
                        carry = put(i * step + k, made[k], carry)
                return carry

            if carry is not None:
                return lax.fori_loop(0, n // step, body, carry)

            def plain(i, zero):
                body(i, None)
                return zero

            lax.fori_loop(0, n // step, plain, 0)

        def sweep(level, make, h):
            nx, ny = dims(level)
            nz = own(level)[2]
            def keep(x, plane):
                h.vp[x + 1, pl.ds(PAD, ny), :] = plane

            if WINDOW[level]:
                planes(nx, make, keep)
                return
            zero = jnp.zeros((ny, LANES), jnp.float32)

            def pack(x, plane, carry):
                keep(x, plane)
                high, low = carry
                h.ys[0, pl.ds(x, 1), :] = plane[ny - 1:ny]
                h.ys[1, pl.ds(x, 1), :] = plane[0:1]
                here = lane == x
                high = jnp.where(here, pltpu.roll(plane, lax.rem(x + LANES - (nz - 1), LANES), 1), high)
                low = jnp.where(here, pltpu.roll(plane, x, 1), low)
                return high, low

            high, low = planes(nx, make, pack, (zero, zero))
            h.zs[0, pl.ds(0, ny), :] = high
            h.zs[1, pl.ds(0, ny), :] = low
            for copy in copies(level, h):
                copy.start()

        def around(level, h, x):
            nx, ny = dims(level)
            vp = h.vp
            mid = vp[x + 1, pl.ds(PAD, ny), :]
            zm, zp = pltpu.roll(mid, 1, 1), pltpu.roll(mid, LANES - 1, 1)
            if level == 0:
                zlow, zhigh = h.zr[0], h.zr[1]
                zm = jnp.where(lane == 0, pltpu.roll(zlow, lax.rem(LANES - x, LANES), 1), zm)
                zp = jnp.where(lane == LANES - 1, pltpu.roll(zhigh, LANES - 1 - x, 1), zp)
            return (mid, vp[x, pl.ds(PAD, ny), :], vp[x + 2, pl.ds(PAD, ny), :],
                    vp[x + 1, pl.ds(PAD - 1, ny), :], vp[x + 1, pl.ds(PAD + 1, ny), :], zm, zp)

        def residual(level, h, x):
            g = refs.level[level]
            mid, xm, xp, ym, yp, zm, zp = around(level, h, x)
            total = g.sx[x] * xm + g.sx[x + 1] * xp + g.sym[x] * ym + g.syp[x] * yp + g.szm[x] * zm + g.szp[x] * zp
            return mid, source(level, x) - g.q[x] * mid + total

        def source(level, x):
            return rhs[x] if level == 0 else refs.level[level].f[x]

        def reaction(level, x):
            return coef_c[x] if level == 0 else refs.level[level].c[x]

        row_of = lax.broadcasted_iota(jnp.int32, (LANES, LANES), 0)
        col_of = lax.broadcasted_iota(jnp.int32, (LANES, LANES), 1)

        def pairing(level, wide, narrow):
            half = wide // 2
            return (half if level == 0 else half + jnp.where(wide >= 96, 64, 0)) == narrow

        def coarsen(level, count_x, get, put=None):
            pair = refs.level[level].pair
            shrink = jnp.where(pairing(level, row_of, col_of), 0.125, 0.0).astype(jnp.bfloat16)

            def put_pair(x, plane):
                pair[x, pl.ds(0, plane.shape[0]), :] = plane

            planes(count_x // 2, lambda x: get(2 * x) + get(2 * x + 1), put_pair)
            half = (own(1)[1] // 2) if level == 1 else dims(level)[1] // 2
            made = []
            for x in range(count_x // 2):
                even = pair[x, pl.ds(0, half, 2), :]
                odd = pair[x, pl.ds(1, half, 2), :]
                made.append(exact_dot(even + odd, shrink))
            if put is not None:
                for x, plane in enumerate(made):
                    put(x, plane)
            return made

        def refine(level, count_x, get):
            pair = refs.level[level].pair
            grow = jnp.where(pairing(level, col_of, row_of), 1.0, 0.0).astype(jnp.bfloat16)
            for x in range(count_x):
                wide = exact_dot(get(x), grow)
                rows = wide.shape[0]
                pair[x, pl.ds(0, rows, 2), :] = wide
                pair[x, pl.ds(1, rows, 2), :] = wide

        def block_parts(h, which, made):
            rows = own(1)[1]
            outer = jnp.zeros((rows, LANES), jnp.float32)
            for x, plane in enumerate(made):
                if x % 2:
                    h.pairs[which, x // 2] = made[x - 1] + pltpu.roll(plane, 64, 1)
                low = (lane >= 8 * x) & (lane < 8 * x + 8)
                high = (lane >= 64 + 8 * x) & (lane < 72 + 8 * x)
                outer = jnp.where(low, pltpu.roll(plane, 8 * x, 1), outer)
                outer = jnp.where(high, pltpu.roll(plane, 8 * x + 8, 1), outer)
            h.outer[which] = outer

        def part_copies(h, deep):
            every = []
            for i, (dx, dy, dz) in enumerate(around_all):
                rows = {-1: pl.ds(0, 8), 0: pl.ds(0, own(1)[1]), 1: pl.ds(own(1)[1] - 8, 8)}[dy]
                pairs = {-1: pl.ds(0, deep), 0: pl.ds(0, 4), 1: pl.ds(4 - deep, deep)}[dx]
                every_array = slice(None)
                if dz == 0:
                    src = h.pairs.at[every_array, pairs, rows]
                    dst = h.pairs_in.at[1 - dx, 1 - dy, every_array, pairs, rows]
                else:
                    src = h.outer.at[every_array, rows]
                    dst = h.outer_in.at[1 - dx, 1 - dy, (1 - dz) // 2, every_array, rows]
                every.append(pltpu.make_async_remote_copy(
                    src_ref=src, dst_ref=dst, send_sem=h.send.at[i], recv_sem=h.recv.at[i],
                    device_id={a: beyond(a, d) for a, d in zip(AXES, (dx, dy, dz))}, device_id_type=MESH))
            return every

        def parts_start(h, deep):
            for copy in part_copies(h, deep):
                copy.start()

        def parts_end(h, deep):
            for copy in part_copies(h, deep):
                copy.wait()

        def part_plane(h, which, plane):
            x = plane + 4
            dx, x = x // 8 - 1, x % 8
            rows_own = own(1)[1]
            pieces = []
            for dy, rows in ((-1, pl.ds(rows_own - 8, 8)), (0, pl.ds(0, rows_own)), (1, pl.ds(0, 8))):
                if (dx, dy) == (0, 0):
                    piece = h.pairs[which, x // 2, rows, :]
                else:
                    piece = h.pairs_in[1 + dx, 1 + dy, which, x // 2, rows, :]
                left = h.outer_in[1 + dx, 1 + dy, 0, which, rows, :]
                right = h.outer_in[1 + dx, 1 + dy, 1, which, rows, :]
                if x % 2:
                    piece = pltpu.roll(piece, 64, 1)
                piece = jnp.where(lane < 64, piece, 0.0)
                piece = jnp.where((lane >= 64) & (lane < 72), pltpu.roll(right, 64 - 8 * x, 1), piece)
                pieces.append(jnp.where(lane >= 120, pltpu.roll(left, (56 - 8 * x) % LANES, 1), piece))
            return pieces

        def put_pieces(ref, index, first, pieces):
            for piece in pieces:
                ref[index, pl.ds(first, piece.shape[0]), :] = piece
                first += piece.shape[0]

        def store(ref):
            def put(x, plane):
                ref[x] = plane

            return put

        def block_to(h, which):
            def put(x, plane):
                mean = pltpu.roll(jnp.where(lane < 32, plane, 0.0), 32 * x, 1)
                rows = pl.ds(0, 12)
                h.block[which, rows, :] = mean if x == 0 else h.block[which, rows, :] + mean

            return put

        def near_copies(h):
            return [
                pltpu.make_async_remote_copy(
                    src_ref=h.block, dst_ref=h.near.at[3 - i], send_sem=h.near_send.at[i],
                    recv_sem=h.near_recv.at[3 - i], device_id={"gy": beyond("gy", dy)}, device_id_type=MESH)
                for i, dy in enumerate(NEAR)
            ]

        def all_copies(h):
            return [
                pltpu.make_async_remote_copy(
                    src_ref=h.column, dst_ref=h.all.at[1 - dz, place["gx"]], send_sem=h.all_send.at[1 - dz, dx],
                    recv_sem=h.all_recv.at[1 - dz, dx],
                    device_id={"gx": beyond("gx", dx), "gz": beyond("gz", dz)}, device_id_type=MESH)
                for dx, dz in around_xz
            ]

        def gather_near(h):
            for copy in near_copies(h):
                copy.start()

        def gather_all(h, arrays):
            for copy in near_copies(h):
                copy.wait()
            for k in range(arrays):
                h.column[k, pl.ds(0, 6), :] = h.near[0, k, pl.ds(6, 6), :]
                h.column[k, pl.ds(6, 12), :] = h.near[1, k, pl.ds(0, 12), :]
                h.column[k, pl.ds(18, 12), :] = h.block[k, pl.ds(0, 12), :]
                h.column[k, pl.ds(30, 12), :] = h.near[2, k, pl.ds(0, 12), :]
                h.column[k, pl.ds(42, 6), :] = h.near[3, k, pl.ds(0, 6), :]
            for copy in all_copies(h):
                copy.start()
            h.all[1, place["gx"]] = h.column[...]

        def gather_end(h):
            for copy in all_copies(h):
                copy.wait()

        def gathered(h, which, x, dx):
            left, here, right = (h.all[i, x, which] for i in range(3))
            plane = jnp.where(lane < 32, pltpu.roll(here, (LANES - 32 * dx) % LANES, 1), 0.0)
            plane = jnp.where((lane >= 32) & (lane < 64), pltpu.roll(right, (LANES + 32 - 32 * dx) % LANES, 1), plane)
            return jnp.where(lane >= 96, pltpu.roll(left, 96 - 32 * dx, 1), plane)

        def setup(level):
            g = refs.level[level]
            nx, ny = dims(level)
            nz = own(level)[2]
            half = 0.5 * 4.0 ** (LEVELS - 1 - level)
            finish(level, g.b)
            start_x, cells_x = first_plane(level), own(level)[0] * count["gx"]
            cells_y = own(level)[1]
            row = lax.broadcasted_iota(jnp.int32, (ny, 1), 0) + place["gy"] * cells_y - FIRST_ROW[level]
            if level == 0:
                column, used = lane, lane >= 0
            else:
                column = jnp.where(lane < 96, lane, lane - LANES)
                reach = 8 if level == 1 else nz
                used = (column < nz + reach) & (column >= -reach)
            column = column + place["gz"] * nz
            keep_ym = jnp.where(row == 0, 0.0, 1.0)
            keep_yp = jnp.where(row == cells_y * count["gy"] - 1, 0.0, 1.0)
            keep_zm = jnp.where(column == 0, 0.0, 1.0)
            keep_zp = jnp.where(column == nz * count["gz"] - 1, 0.0, 1.0)

            def make(x):
                mid, xm, xp, ym, yp, zm, zp = around(level, g.b, x)
                keep_xm = jnp.where((start_x + x == 0) | (start_x + x == cells_x), 0.0, 1.0)
                keep_xp = jnp.where(start_x + x == cells_x - 1, 0.0, 1.0)
                fxm, fxp = half * (mid + xm * keep_xm), half * (mid + xp * keep_xp)
                fym, fyp = half * (mid + ym * keep_ym), half * (mid + yp * keep_yp)
                fzm, fzp = half * (mid + zm * keep_zm), half * (mid + zp * keep_zp)
                q = reaction(level, x) + (fxm + fxp + fym + fyp + fzm + fzp)
                return (q, jnp.where(used, 1.0 / q, 0.0), fxm * keep_xm,
                        fym * keep_ym, fyp * keep_yp, fzm * keep_zm, fzp * keep_zp)

            def put(x, values):
                for name, value in zip(("q", "rq", "sx", "sym", "syp", "szm", "szp"), values):
                    getattr(g, name)[x] = value

            planes(nx, make, put)
            last = g.b.vp[nx, pl.ds(PAD, ny), :] + g.b.vp[nx + 1, pl.ds(PAD, ny), :]
            g.sx[nx] = half * last * jnp.where(start_x + nx == cells_x, 0.0, 1.0)

        def planes_of(level, h):
            ny = dims(level)[1]
            return lambda x: h.vp[x + 1, pl.ds(PAD, ny), :]

        levels = refs.level
        (_, first), (carry_e, weight_r) = chebyshev(2)
        of_f, of_bc = refs.gather

        def start_down(level):
            g = levels[level]
            sweep(level, lambda x: source(level, x) * g.rq[x] * first, g.it[0])

        def go_down(level):
            g = levels[level]

            def second(x):
                mid, rest = residual(level, g.it[0], x)
                return mid * (1.0 + carry_e) + weight_r * rest * g.rq[x]

            finish(level, g.it[0])
            sweep(level, second, g.it[1])

        def leave(level, put=None):
            g = levels[level]
            finish(level, g.it[1])
            if level == 1:
                rows = slice(FIRST_ROW[1], FIRST_ROW[1] + own(1)[1])
                return coarsen(1, own(1)[0], lambda x: residual(1, g.it[1], x + 4)[1][rows], put)
            return coarsen(level, dims(level)[0], lambda x: residual(level, g.it[1], x)[1], put)

        def go_up(level, begun, ended, put):
            g = levels[level]

            def third(x):
                mid, rest = residual(level, begun, x)
                update = first * rest * g.rq[x]
                g.e[x] = update
                return mid + update

            sweep(level, third, ended)
            finish(level, ended)

            def last(x):
                mid, rest = residual(level, ended, x)
                return mid + carry_e * g.e[x] + weight_r * rest * g.rq[x]

            planes(dims(level)[0], last, put)

        parts_f, parts_bc = refs.parts
        own_planes = own(0)[0]
        sweep(0, lambda x: coef_b[x], levels[0].b)
        made_b = coarsen(0, own_planes, lambda x: coef_b[x])
        block_parts(parts_bc, 0, made_b)
        made_c = coarsen(0, own_planes, lambda x: coef_c[x])
        block_parts(parts_bc, 1, made_c)
        for which, made in enumerate((made_b, made_c)):
            for x, plane in enumerate(made):
                levels[1].e[x, pl.ds(0, own(1)[1]), :] = plane
            coarsen(1, own(1)[0], lambda x: levels[1].e[x, pl.ds(0, own(1)[1]), :], block_to(of_bc, which))

        setup(0)
        start_down(0)
        gather_near(of_bc)
        go_down(0)
        parts_start(parts_bc, 3)
        gather_all(of_bc, 2)

        block_parts(parts_f, 0, leave(0))
        parts_start(parts_f, 2)

        parts_end(parts_bc, 3)
        for w in range(-1, 17):
            put_pieces(levels[1].b.vp, w + 1, PAD, part_plane(parts_bc, 0, w))
            if 0 <= w < 16:
                put_pieces(levels[1].c, w, 0, part_plane(parts_bc, 1, w))
        setup(1)
        gather_end(of_bc)
        for dx in range(4):
            def spread(x, carry, dx=dx):
                levels[2].b.vp[4 * x + dx + 1, pl.ds(PAD, 48), :] = gathered(of_bc, 0, x, dx)
                levels[2].c[4 * x + dx] = gathered(of_bc, 1, x, dx)
                return carry

            lax.fori_loop(0, 4, spread, 0)
        coarsen(2, 16, planes_of(2, levels[2].b), store(levels[3].f))
        sweep(3, lambda x: levels[3].f[x], levels[3].b)
        coarsen(2, 16, lambda x: levels[2].c[x], store(levels[3].c))
        setup(2)
        setup(3)

        parts_end(parts_f, 2)
        for w in range(16):
            put_pieces(levels[1].f, w, 0, part_plane(parts_f, 0, w))
        start_down(1)
        go_down(1)
        leave(1, block_to(of_f, 0))
        gather_near(of_f)
        gather_all(of_f, 1)
        gather_end(of_f)
        for dx in range(4):
            def spread_f(x, carry, dx=dx):
                levels[2].f[4 * x + dx] = gathered(of_f, 0, x, dx)
                return carry

            lax.fori_loop(0, 4, spread_f, 0)

        start_down(2)
        go_down(2)
        leave(2, store(levels[3].f))

        g = levels[3]
        steps = chebyshev(COARSE_SWEEPS)

        def begin(x):
            update = source(3, x) * g.rq[x] * steps[0][1]
            g.e[x] = update
            return update

        sweep(3, begin, g.it[0])
        for step in range(1, COARSE_SWEEPS):
            def advance(x, step=step):
                mid, rest = residual(3, g.it[(step - 1) % 2], x)
                update = steps[step][0] * g.e[x] + steps[step][1] * rest * g.rq[x]
                g.e[x] = update
                return mid + update

            sweep(3, advance, g.it[step % 2])

        refine(2, 8, planes_of(3, g.it[(COARSE_SWEEPS - 1) % 2]))
        g = levels[2]
        sweep(2, lambda x: planes_of(2, g.it[1])(x) + g.pair[x // 2], g.it[0])
        go_up(2, g.it[0], g.it[1], store(g.f))

        g = levels[1]
        start_x = place["gx"] * own(2)[0] - 2
        refine(1, 8, lambda x: levels[2].f[jnp.clip(start_x + x, 0, 15), pl.ds(14, 20), :])
        sweep(1, lambda x: planes_of(1, g.it[1])(x) + g.pair[x // 2], g.it[0])
        go_up(1, g.it[0], g.it[1], store(g.f))

        g = levels[0]
        refine(0, 10, lambda x: levels[1].f[x + 3])
        begun = g.it[2]
        for x in range(18):
            begun.vp[x] = g.it[1].vp[x] + g.pair[(x + 1) // 2, pl.ds(8, 64), :]
        own_rows = own(1)[1]
        edges = [jnp.zeros((own_rows, LANES), jnp.float32)] * 2
        for x in range(8):
            plane = levels[1].f[x + 4, pl.ds(8, own_rows), :]
            for side, column in enumerate((LANES - 1, 64)):
                for target in (2 * x, 2 * x + 1):
                    moved = pltpu.roll(plane, (target - column) % LANES, 1)
                    edges[side] = jnp.where(lane == target, moved, edges[side])
        for side in range(2):
            g.edge[side, pl.ds(0, own_rows, 2), :] = edges[side]
            g.edge[side, pl.ds(1, own_rows, 2), :] = edges[side]
            begun.zr[side] = g.it[1].zr[side] + g.edge[side]
        go_up(0, begun, g.it[3], store(out))

    return kernel


class Plan:
    def __init__(self, shape):
        self.shapes = []
        self.tree = Names()
        self.tree.level = []
        for level in range(LEVELS):
            nx, ny = WINDOW[level] or tuple(n >> level for n in shape)[:2]
            g = Names()

            def planes(n, ny=ny):
                return self.add(pltpu.VMEM((n, ny, LANES), jnp.float32))

            def halo(exchanged, nx=nx, ny=ny):
                h = Names()
                h.vp = self.add(pltpu.VMEM((nx + 2, round_up(ny) + 2 * PAD, LANES), jnp.float32))
                if exchanged:
                    for name, rows in (("zs", ny), ("zr", ny), ("ys", nx), ("yr", nx)):
                        setattr(h, name, self.add(pltpu.VMEM((2, round_up(rows), LANES), jnp.float32)))
                    h.send = self.add(pltpu.SemaphoreType.DMA((6,)))
                    h.recv = self.add(pltpu.SemaphoreType.DMA((6,)))
                return h

            exchanged = WINDOW[level] is None
            g.b = halo(exchanged)
            g.sx = planes(nx + 1)
            for name in ("sym", "syp", "szm", "szp", "q", "rq", "e"):
                setattr(g, name, planes(nx))
            if level > 0:
                g.f = planes(nx)
                g.c = planes(nx)
            if level == 0:
                g.pair = self.add(pltpu.VMEM((10, 80, LANES), jnp.float32))
                g.edge = planes(2)
            elif level < LEVELS - 1:
                g.pair = planes(nx // 2)
            g.it = [halo(exchanged) for _ in range(4 if exchanged else 2)]
            self.tree.level.append(g)
        self.tree.gather = [self.gathered(1), self.gathered(2)]
        self.tree.parts = [self.parted(1, shape[1] // 2), self.parted(2, shape[1] // 2)]

    def parted(self, arrays, rows):
        h = Names()
        h.pairs = self.add(pltpu.VMEM((arrays, 4, rows, LANES), jnp.float32))
        h.outer = self.add(pltpu.VMEM((arrays, rows, LANES), jnp.float32))
        h.pairs_in = self.add(pltpu.VMEM((3, 3, arrays, 4, rows, LANES), jnp.float32))
        h.outer_in = self.add(pltpu.VMEM((3, 3, 2, arrays, rows, LANES), jnp.float32))
        h.send = self.add(pltpu.SemaphoreType.DMA((26,)))
        h.recv = self.add(pltpu.SemaphoreType.DMA((26,)))
        return h

    def gathered(self, arrays):
        h = Names()
        h.block = self.add(pltpu.VMEM((arrays, 16, LANES), jnp.float32))
        h.near = self.add(pltpu.VMEM((4, arrays, 16, LANES), jnp.float32))
        h.column = self.add(pltpu.VMEM((arrays, 48, LANES), jnp.float32))
        h.all = self.add(pltpu.VMEM((3, 4, arrays, 48, LANES), jnp.float32))
        h.near_send = self.add(pltpu.SemaphoreType.DMA((4,)))
        h.near_recv = self.add(pltpu.SemaphoreType.DMA((4,)))
        h.all_send = self.add(pltpu.SemaphoreType.DMA((3, 4)))
        h.all_recv = self.add(pltpu.SemaphoreType.DMA((3, 4)))
        return h

    def add(self, shape):
        self.shapes.append(shape)
        return len(self.shapes) - 1

    def unpack(self, refs):
        def walk(node):
            if isinstance(node, int):
                return refs[node]
            if isinstance(node, list):
                return [walk(item) for item in node]
            result = Names()
            for name, item in vars(node).items():
                setattr(result, name, walk(item))
            return result

        return walk(self.tree)


def solution(mesh):
    sizes = dict(mesh.shape)

    def local(rhs, coef_b, coef_c):
        shape = rhs.shape
        plan = Plan(shape)
        return pl.pallas_call(
            make_kernel(shape, sizes, plan),
            out_shape=jax.ShapeDtypeStruct(shape, jnp.float32),
            in_specs=[pl.BlockSpec(memory_space=pltpu.VMEM)] * 3,
            out_specs=pl.BlockSpec(memory_space=pltpu.VMEM),
            scratch_shapes=plan.shapes,
            compiler_params=pltpu.CompilerParams(
                collective_id=0, has_side_effects=True, vmem_limit_bytes=40 * 2**20),
        )(rhs, coef_b, coef_c)

    return jax.shard_map(
        local,
        mesh=mesh,
        in_specs=(P(*AXES),) * 3,
        out_specs=P(*AXES),
        check_vma=False,
    )
```

```python
import jax
import jax.numpy as jnp
from jax import lax
from jax.experimental import pallas as pl
from jax.experimental.pallas import tpu as pltpu
from jax.sharding import PartitionSpec as P

LEVELS = 4
COARSE_SWEEPS = 6
CENTRE = 1.1
RADIUS = 0.9
LANES = 128
PAD = 8

MESH = pl.DeviceIdType.MESH
AXES = ("gx", "gy", "gz")


def chebyshev(sweeps):
    ratio = RADIUS / CENTRE
    factors = [(0.0, 1.0 / CENTRE)]
    for _ in range(sweeps - 1):
        following = 1.0 / (2.0 * CENTRE / RADIUS - ratio)
        factors.append((following * ratio, 2.0 * following / RADIUS))
        ratio = following
    return factors


def round_up(value):
    return -(-value // 8) * 8


class Names:
    pass


def exact_dot(left, matrix):
    high = left.astype(jnp.bfloat16)
    rest = left - high.astype(jnp.float32)
    middle = rest.astype(jnp.bfloat16)
    low = (rest - middle.astype(jnp.float32)).astype(jnp.bfloat16)
    total = jnp.dot(low, matrix, preferred_element_type=jnp.float32)
    total = total + jnp.dot(middle, matrix, preferred_element_type=jnp.float32)
    return total + jnp.dot(high, matrix, preferred_element_type=jnp.float32)


WINDOW = (None, (16, 40), (16, 48), (8, 24))
FIRST_ROW = (0, 8, 18, 9)
NEAR = (-2, -1, 1, 2)
TOGETHER = 16


def make_kernel(shape, sizes, plan):
    count = {axis: sizes[axis] for axis in AXES}

    def kernel(rhs_in, coef_b_in, coef_c_in, out, *scratch):
        refs = plan.unpack(scratch)
        rhs, coef_c = refs.rhs, refs.coef_c
        inputs = [
            pltpu.make_async_copy(source, target, refs.load.at[i])
            for i, (source, target) in enumerate((
                (coef_b_in, refs.level[0].b.vp.at[pl.ds(1, shape[0]), pl.ds(PAD, shape[1])]),
                (coef_c_in, coef_c), (rhs_in, rhs)))
        ]
        place = {axis: lax.axis_index(axis) for axis in AXES}

        def beyond(axis, step):
            return lax.rem(place[axis] + count[axis] + step, count[axis])

        after = {axis: beyond(axis, 1) for axis in AXES}
        before = {axis: beyond(axis, -1) for axis in AXES}
        def own(level):
            return tuple(n >> level for n in shape)

        def first_plane(level):
            if level > 1:
                return 0
            return place["gx"] * own(level)[0] - (4 if level == 1 else 0)

        sides = (-1, 0, 1)
        around_all = [(dx, dy, dz) for dx in sides for dy in sides for dz in sides if (dx, dy, dz) != (0, 0, 0)]
        around_xz = [(dx, dz) for dx in range(4) for dz in (-1, 0, 1) if (dx, dz) != (0, 0)]

        barrier = pltpu.get_barrier_semaphore()
        partners = [offset for offset in around_all if sum(map(abs, offset)) == 1]
        for offset in partners:
            pl.semaphore_signal(barrier, inc=1, device_id={a: beyond(a, d) for a, d in zip(AXES, offset)},
                                device_id_type=MESH)
        for copy in inputs:
            copy.start()

        lane = lax.broadcasted_iota(jnp.int32, (1, LANES), 1)

        def dims(level):
            return WINDOW[level] or own(level)[:2]

        def clear_rim(level, h):
            nx, ny = dims(level)
            h.vp[0] = jnp.zeros(h.vp.shape[1:], jnp.float32)
            h.vp[nx + 1] = jnp.zeros(h.vp.shape[1:], jnp.float32)
            rim = jnp.zeros((nx, PAD, LANES), jnp.float32)
            h.vp[pl.ds(1, nx), pl.ds(0, PAD), :] = rim
            h.vp[pl.ds(1, nx), pl.ds(PAD + ny, PAD), :] = rim

        for level in range(LEVELS):
            if WINDOW[level]:
                for h in [refs.level[level].b] + refs.level[level].it:
                    clear_rim(level, h)

        def copies(level, h):
            nx, ny = dims(level)
            rows = pl.ds(PAD, round_up(ny))
            vp, zs, zr, ys, yr = h.vp, h.zs, h.zr, h.ys, h.yr
            pairs = (
                (vp.at[nx, rows], vp.at[0, rows], "gx", after),
                (vp.at[1, rows], vp.at[nx + 1, rows], "gx", before),
                (ys.at[0], yr.at[0], "gy", after),
                (ys.at[1], yr.at[1], "gy", before),
                (zs.at[0], zr.at[0], "gz", after),
                (zs.at[1], zr.at[1], "gz", before),
            )
            return [
                pltpu.make_async_remote_copy(
                    src_ref=src, dst_ref=dst, send_sem=h.send.at[i], recv_sem=h.recv.at[i],
                    device_id={axis: where[axis]}, device_id_type=MESH)
                for i, (src, dst, axis, where) in enumerate(pairs)
            ]

        def finish(level, h):
            if WINDOW[level]:
                return
            nx, ny = dims(level)
            for copy in copies(level, h):
                copy.wait()
            for x in range(nx):
                h.vp[x + 1, pl.ds(PAD - 1, 1), :] = h.yr[0, pl.ds(x, 1), :]
                h.vp[x + 1, pl.ds(PAD + ny, 1), :] = h.yr[1, pl.ds(x, 1), :]

        def planes(n, make, put, carry=None):
            step = min(n, TOGETHER)

            def body(i, carry):
                made = [make(i * step + k) for k in range(step)]
                for k in range(step):
                    if carry is None:
                        put(i * step + k, made[k])
                    else:
                        carry = put(i * step + k, made[k], carry)
                return carry

            if carry is not None:
                return lax.fori_loop(0, n // step, body, carry)

            def plain(i, zero):
                body(i, None)
                return zero

            lax.fori_loop(0, n // step, plain, 0)

        def sweep(level, make, h, held=False):
            nx, ny = dims(level)
            nz = own(level)[2]
            def keep(x, plane):
                h.vp[x + 1, pl.ds(PAD, ny), :] = plane

            if WINDOW[level]:
                planes(nx, make, keep)
                return
            zero = jnp.zeros((ny, LANES), jnp.float32)

            def pack(x, plane, carry):
                if not held:
                    keep(x, plane)
                high, low = carry
                h.ys[0, pl.ds(x, 1), :] = plane[ny - 1:ny]
                h.ys[1, pl.ds(x, 1), :] = plane[0:1]
                here = lane == x
                high = jnp.where(here, pltpu.roll(plane, lax.rem(x + LANES - (nz - 1), LANES), 1), high)
                low = jnp.where(here, pltpu.roll(plane, x, 1), low)
                return high, low

            high, low = planes(nx, make, pack, (zero, zero))
            h.zs[0, pl.ds(0, ny), :] = high
            h.zs[1, pl.ds(0, ny), :] = low
            if held:
                pl.semaphore_wait(barrier, len(partners))
            for copy in copies(level, h):
                copy.start()

        def around(level, h, x):
            nx, ny = dims(level)
            vp = h.vp
            mid = vp[x + 1, pl.ds(PAD, ny), :]
            zm, zp = pltpu.roll(mid, 1, 1), pltpu.roll(mid, LANES - 1, 1)
            if level == 0:
                zlow, zhigh = h.zr[0], h.zr[1]
                zm = jnp.where(lane == 0, pltpu.roll(zlow, lax.rem(LANES - x, LANES), 1), zm)
                zp = jnp.where(lane == LANES - 1, pltpu.roll(zhigh, LANES - 1 - x, 1), zp)
            return (mid, vp[x, pl.ds(PAD, ny), :], vp[x + 2, pl.ds(PAD, ny), :],
                    vp[x + 1, pl.ds(PAD - 1, ny), :], vp[x + 1, pl.ds(PAD + 1, ny), :], zm, zp)

        def residual(level, h, x):
            g = refs.level[level]
            mid, xm, xp, ym, yp, zm, zp = around(level, h, x)
            total = g.sx[x] * xm + g.sx[x + 1] * xp + g.sym[x] * ym + g.syp[x] * yp + g.szm[x] * zm + g.szp[x] * zp
            return mid, source(level, x) - g.q[x] * mid + total

        def source(level, x):
            return rhs[x] if level == 0 else refs.level[level].f[x]

        def reaction(level, x):
            return coef_c[x] if level == 0 else refs.level[level].c[x]

        row_of = lax.broadcasted_iota(jnp.int32, (LANES, LANES), 0)
        col_of = lax.broadcasted_iota(jnp.int32, (LANES, LANES), 1)

        def pairing(level, wide, narrow):
            half = wide // 2
            return (half if level == 0 else half + jnp.where(wide >= 96, 64, 0)) == narrow

        def coarsen(level, count_x, get, put=None):
            pair = refs.level[level].pair
            shrink = jnp.where(pairing(level, row_of, col_of), 0.125, 0.0).astype(jnp.bfloat16)

            def put_pair(x, plane):
                pair[x, pl.ds(0, plane.shape[0]), :] = plane

            planes(count_x // 2, lambda x: get(2 * x) + get(2 * x + 1), put_pair)
            half = (own(1)[1] // 2) if level == 1 else dims(level)[1] // 2
            made = []
            for x in range(count_x // 2):
                even = pair[x, pl.ds(0, half, 2), :]
                odd = pair[x, pl.ds(1, half, 2), :]
                made.append(exact_dot(even + odd, shrink))
            if put is not None:
                for x, plane in enumerate(made):
                    put(x, plane)
            return made

        def refine(level, count_x, get):
            pair = refs.level[level].pair
            grow = jnp.where(pairing(level, col_of, row_of), 1.0, 0.0).astype(jnp.bfloat16)
            for x in range(count_x):
                wide = exact_dot(get(x), grow)
                rows = wide.shape[0]
                pair[x, pl.ds(0, rows, 2), :] = wide
                pair[x, pl.ds(1, rows, 2), :] = wide

        def block_parts(h, which, made):
            rows = own(1)[1]
            outer = jnp.zeros((rows, LANES), jnp.float32)
            for x, plane in enumerate(made):
                if x % 2:
                    h.pairs[which, x // 2] = made[x - 1] + pltpu.roll(plane, 64, 1)
                low = (lane >= 8 * x) & (lane < 8 * x + 8)
                high = (lane >= 64 + 8 * x) & (lane < 72 + 8 * x)
                outer = jnp.where(low, pltpu.roll(plane, 8 * x, 1), outer)
                outer = jnp.where(high, pltpu.roll(plane, 8 * x + 8, 1), outer)
            h.outer[which] = outer

        def part_copies(h, deep, steps=(1, 2, 3)):
            every = []
            for i, (dx, dy, dz) in enumerate(around_all):
                if abs(dx) + abs(dy) + abs(dz) not in steps:
                    continue
                rows = {-1: pl.ds(0, 8), 0: pl.ds(0, own(1)[1]), 1: pl.ds(own(1)[1] - 8, 8)}[dy]
                pairs = {-1: pl.ds(0, deep), 0: pl.ds(0, 4), 1: pl.ds(4 - deep, deep)}[dx]
                every_array = slice(None)
                if dz == 0:
                    src = h.pairs.at[every_array, pairs, rows]
                    dst = h.pairs_in.at[1 - dx, 1 - dy, every_array, pairs, rows]
                else:
                    src = h.outer.at[every_array, rows]
                    dst = h.outer_in.at[1 - dx, 1 - dy, (1 - dz) // 2, every_array, rows]
                every.append(pltpu.make_async_remote_copy(
                    src_ref=src, dst_ref=dst, send_sem=h.send.at[i], recv_sem=h.recv.at[i],
                    device_id={a: beyond(a, d) for a, d in zip(AXES, (dx, dy, dz))}, device_id_type=MESH))
            return every

        def parts_start(h, deep, steps=(1, 2, 3)):
            for copy in part_copies(h, deep, steps):
                copy.start()

        def parts_end(h, deep):
            for copy in part_copies(h, deep):
                copy.wait()

        def part_plane(h, which, plane):
            x = plane + 4
            dx, x = x // 8 - 1, x % 8
            rows_own = own(1)[1]
            pieces = []
            for dy, rows in ((-1, pl.ds(rows_own - 8, 8)), (0, pl.ds(0, rows_own)), (1, pl.ds(0, 8))):
                if (dx, dy) == (0, 0):
                    piece = h.pairs[which, x // 2, rows, :]
                else:
                    piece = h.pairs_in[1 + dx, 1 + dy, which, x // 2, rows, :]
                left = h.outer_in[1 + dx, 1 + dy, 0, which, rows, :]
                right = h.outer_in[1 + dx, 1 + dy, 1, which, rows, :]
                if x % 2:
                    piece = pltpu.roll(piece, 64, 1)
                piece = jnp.where(lane < 64, piece, 0.0)
                piece = jnp.where((lane >= 64) & (lane < 72), pltpu.roll(right, 64 - 8 * x, 1), piece)
                pieces.append(jnp.where(lane >= 120, pltpu.roll(left, (56 - 8 * x) % LANES, 1), piece))
            return pieces

        def put_pieces(ref, index, first, pieces):
            for piece in pieces:
                ref[index, pl.ds(first, piece.shape[0]), :] = piece
                first += piece.shape[0]

        def store(ref):
            def put(x, plane):
                ref[x] = plane

            return put

        def block_to(h, which):
            def put(x, plane):
                mean = pltpu.roll(jnp.where(lane < 32, plane, 0.0), 32 * x, 1)
                rows = pl.ds(0, 12)
                h.block[which, rows, :] = mean if x == 0 else h.block[which, rows, :] + mean

            return put

        def near_copies(h):
            return [
                pltpu.make_async_remote_copy(
                    src_ref=h.block, dst_ref=h.near.at[3 - i], send_sem=h.near_send.at[i],
                    recv_sem=h.near_recv.at[3 - i], device_id={"gy": beyond("gy", dy)}, device_id_type=MESH)
                for i, dy in enumerate(NEAR)
            ]

        def all_copies(h):
            return [
                pltpu.make_async_remote_copy(
                    src_ref=h.column, dst_ref=h.all.at[1 - dz, place["gx"]], send_sem=h.all_send.at[1 - dz, dx],
                    recv_sem=h.all_recv.at[1 - dz, dx],
                    device_id={"gx": beyond("gx", dx), "gz": beyond("gz", dz)}, device_id_type=MESH)
                for dx, dz in around_xz
            ]

        def gather_near(h):
            for copy in near_copies(h):
                copy.start()

        def gather_all(h, arrays):
            for copy in near_copies(h):
                copy.wait()
            for k in range(arrays):
                h.column[k, pl.ds(0, 6), :] = h.near[0, k, pl.ds(6, 6), :]
                h.column[k, pl.ds(6, 12), :] = h.near[1, k, pl.ds(0, 12), :]
                h.column[k, pl.ds(18, 12), :] = h.block[k, pl.ds(0, 12), :]
                h.column[k, pl.ds(30, 12), :] = h.near[2, k, pl.ds(0, 12), :]
                h.column[k, pl.ds(42, 6), :] = h.near[3, k, pl.ds(0, 6), :]
            for copy in all_copies(h):
                copy.start()
            h.all[1, place["gx"]] = h.column[...]

        def gather_end(h):
            for copy in all_copies(h):
                copy.wait()

        def gathered(h, which, x, dx):
            left, here, right = (h.all[i, x, which] for i in range(3))
            plane = jnp.where(lane < 32, pltpu.roll(here, (LANES - 32 * dx) % LANES, 1), 0.0)
            plane = jnp.where((lane >= 32) & (lane < 64), pltpu.roll(right, (LANES + 32 - 32 * dx) % LANES, 1), plane)
            return jnp.where(lane >= 96, pltpu.roll(left, 96 - 32 * dx, 1), plane)

        def setup(level):
            g = refs.level[level]
            nx, ny = dims(level)
            nz = own(level)[2]
            half = 0.5 * 4.0 ** (LEVELS - 1 - level)
            finish(level, g.b)
            start_x, cells_x = first_plane(level), own(level)[0] * count["gx"]
            cells_y = own(level)[1]
            row = lax.broadcasted_iota(jnp.int32, (ny, 1), 0) + place["gy"] * cells_y - FIRST_ROW[level]
            if level == 0:
                column, used = lane, lane >= 0
            else:
                column = jnp.where(lane < 96, lane, lane - LANES)
                reach = 8 if level == 1 else nz
                used = (column < nz + reach) & (column >= -reach)
            column = column + place["gz"] * nz
            keep_ym = jnp.where(row == 0, 0.0, 1.0)
            keep_yp = jnp.where(row == cells_y * count["gy"] - 1, 0.0, 1.0)
            keep_zm = jnp.where(column == 0, 0.0, 1.0)
            keep_zp = jnp.where(column == nz * count["gz"] - 1, 0.0, 1.0)

            def make(x):
                mid, xm, xp, ym, yp, zm, zp = around(level, g.b, x)
                keep_xm = jnp.where((start_x + x == 0) | (start_x + x == cells_x), 0.0, 1.0)
                keep_xp = jnp.where(start_x + x == cells_x - 1, 0.0, 1.0)
                fxm, fxp = half * (mid + xm * keep_xm), half * (mid + xp * keep_xp)
                fym, fyp = half * (mid + ym * keep_ym), half * (mid + yp * keep_yp)
                fzm, fzp = half * (mid + zm * keep_zm), half * (mid + zp * keep_zp)
                q = reaction(level, x) + (fxm + fxp + fym + fyp + fzm + fzp)
                return (q, jnp.where(used, 1.0 / q, 0.0), fxm * keep_xm,
                        fym * keep_ym, fyp * keep_yp, fzm * keep_zm, fzp * keep_zp)

            def put(x, values):
                for name, value in zip(("q", "rq", "sx", "sym", "syp", "szm", "szp"), values):
                    getattr(g, name)[x] = value

            planes(nx, make, put)
            last = g.b.vp[nx, pl.ds(PAD, ny), :] + g.b.vp[nx + 1, pl.ds(PAD, ny), :]
            g.sx[nx] = half * last * jnp.where(start_x + nx == cells_x, 0.0, 1.0)

        def planes_of(level, h):
            ny = dims(level)[1]
            return lambda x: h.vp[x + 1, pl.ds(PAD, ny), :]

        levels = refs.level
        (_, first), (carry_e, weight_r) = chebyshev(2)
        of_f, of_bc = refs.gather

        def start_down(level):
            g = levels[level]
            sweep(level, lambda x: source(level, x) * g.rq[x] * first, g.it[0])

        def go_down(level):
            g = levels[level]

            def second(x):
                mid, rest = residual(level, g.it[0], x)
                return mid * (1.0 + carry_e) + weight_r * rest * g.rq[x]

            finish(level, g.it[0])
            sweep(level, second, g.it[1])

        def leave(level, put=None):
            g = levels[level]
            finish(level, g.it[1])
            if level == 1:
                rows = slice(FIRST_ROW[1], FIRST_ROW[1] + own(1)[1])
                return coarsen(1, own(1)[0], lambda x: residual(1, g.it[1], x + 4)[1][rows], put)
            return coarsen(level, dims(level)[0], lambda x: residual(level, g.it[1], x)[1], put)

        def go_up(level, begun, ended, put):
            g = levels[level]

            def third(x):
                mid, rest = residual(level, begun, x)
                update = first * rest * g.rq[x]
                g.e[x] = update
                return mid + update

            sweep(level, third, ended)
            finish(level, ended)

            def last(x):
                mid, rest = residual(level, ended, x)
                return mid + carry_e * g.e[x] + weight_r * rest * g.rq[x]

            planes(dims(level)[0], last, put)

        parts_f, parts_bc = refs.parts
        own_planes = own(0)[0]
        inputs[0].wait()
        fine_b = planes_of(0, levels[0].b)
        sweep(0, fine_b, levels[0].b, held=True)
        made_b = coarsen(0, own_planes, fine_b)
        inputs[1].wait()
        block_parts(parts_bc, 0, made_b)
        made_c = coarsen(0, own_planes, lambda x: coef_c[x])
        block_parts(parts_bc, 1, made_c)
        parts_start(parts_bc, 3, (1,))
        for which, made in enumerate((made_b, made_c)):
            for x, plane in enumerate(made):
                levels[1].e[x, pl.ds(0, own(1)[1]), :] = plane
            coarsen(1, own(1)[0], lambda x: levels[1].e[x, pl.ds(0, own(1)[1]), :], block_to(of_bc, which))

        setup(0)
        inputs[2].wait()
        start_down(0)
        gather_near(of_bc)
        parts_start(parts_bc, 3, (2,))
        go_down(0)
        parts_start(parts_bc, 3, (3,))
        gather_all(of_bc, 2)

        block_parts(parts_f, 0, leave(0))
        parts_start(parts_f, 2)

        parts_end(parts_bc, 3)
        for w in range(-1, 17):
            put_pieces(levels[1].b.vp, w + 1, PAD, part_plane(parts_bc, 0, w))
            if 0 <= w < 16:
                put_pieces(levels[1].c, w, 0, part_plane(parts_bc, 1, w))
        setup(1)
        gather_end(of_bc)
        for dx in range(4):
            def spread(x, carry, dx=dx):
                levels[2].b.vp[4 * x + dx + 1, pl.ds(PAD, 48), :] = gathered(of_bc, 0, x, dx)
                levels[2].c[4 * x + dx] = gathered(of_bc, 1, x, dx)
                return carry

            lax.fori_loop(0, 4, spread, 0)
        coarsen(2, 16, planes_of(2, levels[2].b), store(levels[3].f))
        sweep(3, lambda x: levels[3].f[x], levels[3].b)
        coarsen(2, 16, lambda x: levels[2].c[x], store(levels[3].c))
        setup(2)
        setup(3)

        parts_end(parts_f, 2)
        for w in range(16):
            put_pieces(levels[1].f, w, 0, part_plane(parts_f, 0, w))
        start_down(1)
        go_down(1)
        leave(1, block_to(of_f, 0))
        gather_near(of_f)
        gather_all(of_f, 1)
        gather_end(of_f)
        for dx in range(4):
            def spread_f(x, carry, dx=dx):
                levels[2].f[4 * x + dx] = gathered(of_f, 0, x, dx)
                return carry

            lax.fori_loop(0, 4, spread_f, 0)

        start_down(2)
        go_down(2)
        leave(2, store(levels[3].f))

        g = levels[3]
        steps = chebyshev(COARSE_SWEEPS)

        def begin(x):
            update = source(3, x) * g.rq[x] * steps[0][1]
            g.e[x] = update
            return update

        sweep(3, begin, g.it[0])
        for step in range(1, COARSE_SWEEPS):
            def advance(x, step=step):
                mid, rest = residual(3, g.it[(step - 1) % 2], x)
                update = steps[step][0] * g.e[x] + steps[step][1] * rest * g.rq[x]
                g.e[x] = update
                return mid + update

            sweep(3, advance, g.it[step % 2])

        refine(2, 8, planes_of(3, g.it[(COARSE_SWEEPS - 1) % 2]))
        g = levels[2]
        sweep(2, lambda x: planes_of(2, g.it[1])(x) + g.pair[x // 2], g.it[0])
        go_up(2, g.it[0], g.it[1], store(g.f))

        g = levels[1]
        start_x = place["gx"] * own(2)[0] - 2
        refine(1, 8, lambda x: levels[2].f[jnp.clip(start_x + x, 0, 15), pl.ds(14, 20), :])
        sweep(1, lambda x: planes_of(1, g.it[1])(x) + g.pair[x // 2], g.it[0])
        go_up(1, g.it[0], g.it[1], store(g.f))

        g = levels[0]
        refine(0, 10, lambda x: levels[1].f[x + 3])
        begun = g.it[2]
        for x in range(18):
            begun.vp[x] = g.it[1].vp[x] + g.pair[(x + 1) // 2, pl.ds(8, 64), :]
        own_rows = own(1)[1]
        edges = [jnp.zeros((own_rows, LANES), jnp.float32)] * 2
        for x in range(8):
            plane = levels[1].f[x + 4, pl.ds(8, own_rows), :]
            for side, column in enumerate((LANES - 1, 64)):
                for target in (2 * x, 2 * x + 1):
                    moved = pltpu.roll(plane, (target - column) % LANES, 1)
                    edges[side] = jnp.where(lane == target, moved, edges[side])
        for side in range(2):
            g.edge[side, pl.ds(0, own_rows, 2), :] = edges[side]
            g.edge[side, pl.ds(1, own_rows, 2), :] = edges[side]
            begun.zr[side] = g.it[1].zr[side] + g.edge[side]
        go_up(0, begun, g.it[3], store(out))

    return kernel


class Plan:
    def __init__(self, shape):
        self.shapes = []
        self.tree = Names()
        self.tree.level = []
        for level in range(LEVELS):
            nx, ny = WINDOW[level] or tuple(n >> level for n in shape)[:2]
            g = Names()

            def planes(n, ny=ny):
                return self.add(pltpu.VMEM((n, ny, LANES), jnp.float32))

            def halo(exchanged, nx=nx, ny=ny):
                h = Names()
                h.vp = self.add(pltpu.VMEM((nx + 2, round_up(ny) + 2 * PAD, LANES), jnp.float32))
                if exchanged:
                    for name, rows in (("zs", ny), ("zr", ny), ("ys", nx), ("yr", nx)):
                        setattr(h, name, self.add(pltpu.VMEM((2, round_up(rows), LANES), jnp.float32)))
                    h.send = self.add(pltpu.SemaphoreType.DMA((6,)))
                    h.recv = self.add(pltpu.SemaphoreType.DMA((6,)))
                return h

            exchanged = WINDOW[level] is None
            g.b = halo(exchanged)
            g.sx = planes(nx + 1)
            for name in ("sym", "syp", "szm", "szp", "q", "rq", "e"):
                setattr(g, name, planes(nx))
            if level > 0:
                g.f = planes(nx)
                g.c = planes(nx)
            if level == 0:
                g.pair = self.add(pltpu.VMEM((10, 80, LANES), jnp.float32))
                g.edge = planes(2)
            elif level < LEVELS - 1:
                g.pair = planes(nx // 2)
            g.it = [halo(exchanged) for _ in range(4 if exchanged else 2)]
            self.tree.level.append(g)
        self.tree.rhs = self.add(pltpu.VMEM(shape, jnp.float32))
        self.tree.coef_c = self.add(pltpu.VMEM(shape, jnp.float32))
        self.tree.load = self.add(pltpu.SemaphoreType.DMA((3,)))
        self.tree.gather = [self.gathered(1), self.gathered(2)]
        self.tree.parts = [self.parted(1, shape[1] // 2), self.parted(2, shape[1] // 2)]

    def parted(self, arrays, rows):
        h = Names()
        h.pairs = self.add(pltpu.VMEM((arrays, 4, rows, LANES), jnp.float32))
        h.outer = self.add(pltpu.VMEM((arrays, rows, LANES), jnp.float32))
        h.pairs_in = self.add(pltpu.VMEM((3, 3, arrays, 4, rows, LANES), jnp.float32))
        h.outer_in = self.add(pltpu.VMEM((3, 3, 2, arrays, rows, LANES), jnp.float32))
        h.send = self.add(pltpu.SemaphoreType.DMA((26,)))
        h.recv = self.add(pltpu.SemaphoreType.DMA((26,)))
        return h

    def gathered(self, arrays):
        h = Names()
        h.block = self.add(pltpu.VMEM((arrays, 16, LANES), jnp.float32))
        h.near = self.add(pltpu.VMEM((4, arrays, 16, LANES), jnp.float32))
        h.column = self.add(pltpu.VMEM((arrays, 48, LANES), jnp.float32))
        h.all = self.add(pltpu.VMEM((3, 4, arrays, 48, LANES), jnp.float32))
        h.near_send = self.add(pltpu.SemaphoreType.DMA((4,)))
        h.near_recv = self.add(pltpu.SemaphoreType.DMA((4,)))
        h.all_send = self.add(pltpu.SemaphoreType.DMA((3, 4)))
        h.all_recv = self.add(pltpu.SemaphoreType.DMA((3, 4)))
        return h

    def add(self, shape):
        self.shapes.append(shape)
        return len(self.shapes) - 1

    def unpack(self, refs):
        def walk(node):
            if isinstance(node, int):
                return refs[node]
            if isinstance(node, list):
                return [walk(item) for item in node]
            result = Names()
            for name, item in vars(node).items():
                setattr(result, name, walk(item))
            return result

        return walk(self.tree)


def solution(mesh):
    sizes = dict(mesh.shape)

    def local(rhs, coef_b, coef_c):
        shape = rhs.shape
        plan = Plan(shape)
        return pl.pallas_call(
            make_kernel(shape, sizes, plan),
            out_shape=jax.ShapeDtypeStruct(shape, jnp.float32),
            in_specs=[pl.BlockSpec(memory_space=pl.ANY)] * 3,
            out_specs=pl.BlockSpec(memory_space=pltpu.VMEM),
            scratch_shapes=plan.shapes,
            compiler_params=pltpu.CompilerParams(
                collective_id=0, has_side_effects=True, vmem_limit_bytes=56 * 2**20),
        )(rhs, coef_b, coef_c)

    return jax.shard_map(
        local,
        mesh=mesh,
        in_specs=(P(*AXES),) * 3,
        out_specs=P(*AXES),
        check_vma=False,
    )
```

```python
import jax
import jax.numpy as jnp
from jax import lax
from jax.experimental import pallas as pl
from jax.experimental.pallas import tpu as pltpu
from jax.sharding import PartitionSpec as P

LEVELS = 4
COARSE_SWEEPS = 6
CENTRE = 1.1
RADIUS = 0.9
LANES = 128
PAD = 8

MESH = pl.DeviceIdType.MESH
AXES = ("gx", "gy", "gz")


def chebyshev(sweeps):
    ratio = RADIUS / CENTRE
    factors = [(0.0, 1.0 / CENTRE)]
    for _ in range(sweeps - 1):
        following = 1.0 / (2.0 * CENTRE / RADIUS - ratio)
        factors.append((following * ratio, 2.0 * following / RADIUS))
        ratio = following
    return factors


def round_up(value):
    return -(-value // 8) * 8


class Names:
    pass


def exact_dot(lefts, matrix):
    left = jnp.concatenate(lefts, axis=0)
    high = left.astype(jnp.bfloat16)
    rest = left - high.astype(jnp.float32)
    middle = rest.astype(jnp.bfloat16)
    low = (rest - middle.astype(jnp.float32)).astype(jnp.bfloat16)
    product = jnp.dot(jnp.concatenate([low, middle, high], axis=0), matrix, preferred_element_type=jnp.float32)
    total, rows = left.shape[0], lefts[0].shape[0]
    product = (product[:total] + product[total:2 * total]) + product[2 * total:]
    return [product[rows * k:rows * k + rows] for k in range(len(lefts))]


WINDOW = (None, (16, 40), (16, 48), (8, 24))
FIRST_ROW = (0, 8, 18, 9)
NEAR = (-2, -1, 1, 2)
TOGETHER = 16


def make_kernel(shape, sizes, plan):
    count = {axis: sizes[axis] for axis in AXES}

    def kernel(rhs_in, coef_b_in, coef_c_in, out, *scratch):
        refs = plan.unpack(scratch)
        rhs, coef_c = refs.rhs, refs.coef_c
        inputs = [
            pltpu.make_async_copy(source, target, refs.load.at[i])
            for i, (source, target) in enumerate((
                (coef_b_in, refs.level[0].b.vp.at[pl.ds(1, shape[0]), pl.ds(PAD, shape[1])]),
                (coef_c_in, coef_c), (rhs_in, rhs)))
        ]
        place = {axis: lax.axis_index(axis) for axis in AXES}

        def beyond(axis, step):
            return lax.rem(place[axis] + count[axis] + step, count[axis])

        after = {axis: beyond(axis, 1) for axis in AXES}
        before = {axis: beyond(axis, -1) for axis in AXES}
        def own(level):
            return tuple(n >> level for n in shape)

        def first_plane(level):
            if level > 1:
                return 0
            return place["gx"] * own(level)[0] - (4 if level == 1 else 0)

        sides = (-1, 0, 1)
        around_all = [(dx, dy, dz) for dx in sides for dy in sides for dz in sides if (dx, dy, dz) != (0, 0, 0)]
        around_xz = [(dx, dz) for dx in range(4) for dz in (-1, 0, 1) if (dx, dz) != (0, 0)]

        barrier = pltpu.get_barrier_semaphore()
        partners = [offset for offset in around_all if sum(map(abs, offset)) == 1]
        for offset in partners:
            pl.semaphore_signal(barrier, inc=1, device_id={a: beyond(a, d) for a, d in zip(AXES, offset)},
                                device_id_type=MESH)
        for copy in inputs:
            copy.start()

        lane = lax.broadcasted_iota(jnp.int32, (1, LANES), 1)

        def dims(level):
            return WINDOW[level] or own(level)[:2]

        def clear_rim(level, h):
            nx, ny = dims(level)
            h.vp[0] = jnp.zeros(h.vp.shape[1:], jnp.float32)
            h.vp[nx + 1] = jnp.zeros(h.vp.shape[1:], jnp.float32)
            rim = jnp.zeros((nx, PAD, LANES), jnp.float32)
            h.vp[pl.ds(1, nx), pl.ds(0, PAD), :] = rim
            h.vp[pl.ds(1, nx), pl.ds(PAD + ny, PAD), :] = rim

        for level in range(LEVELS):
            if WINDOW[level]:
                for h in [refs.level[level].b] + refs.level[level].it:
                    clear_rim(level, h)

        def copies(level, h):
            nx, ny = dims(level)
            rows = pl.ds(PAD, round_up(ny))
            vp, zs, zin, ys, yr = h.vp, h.zs, h.zin, h.ys, h.yr
            pairs = (
                (vp.at[nx, rows], vp.at[0, rows], "gx", after),
                (vp.at[1, rows], vp.at[nx + 1, rows], "gx", before),
                (ys.at[0], yr.at[0], "gy", after),
                (ys.at[1], yr.at[1], "gy", before),
                (zs.at[0], zin.at[0], "gz", after),
                (zs.at[1], zin.at[1], "gz", before),
            )
            return [
                pltpu.make_async_remote_copy(
                    src_ref=src, dst_ref=dst, send_sem=h.send.at[i], recv_sem=h.recv.at[i],
                    device_id={axis: where[axis]}, device_id_type=MESH)
                for i, (src, dst, axis, where) in enumerate(pairs)
            ]

        def finish(level, h):
            if WINDOW[level]:
                return
            nx, ny = dims(level)
            for copy in copies(level, h):
                copy.wait()
            for side in range(2):
                packed = h.zin[side]
                for tile in range(ny // 8):
                    h.zr[side, pl.ds(8 * tile, 8), :] = pltpu.roll(packed, (LANES - nx * tile) % LANES, 1)
            for x in range(nx):
                h.vp[x + 1, pl.ds(PAD - 1, 1), :] = h.yr[0, pl.ds(x, 1), :]
                h.vp[x + 1, pl.ds(PAD + ny, 1), :] = h.yr[1, pl.ds(x, 1), :]

        def planes(n, make, put, carry=None):
            step = min(n, TOGETHER)

            def body(i, carry):
                made = [make(i * step + k) for k in range(step)]
                for k in range(step):
                    if carry is None:
                        put(i * step + k, made[k])
                    else:
                        carry = put(i * step + k, made[k], carry)
                return carry

            if carry is not None:
                return lax.fori_loop(0, n // step, body, carry)

            def plain(i, zero):
                body(i, None)
                return zero

            lax.fori_loop(0, n // step, plain, 0)

        def sweep(level, make, h, held=False):
            nx, ny = dims(level)
            nz = own(level)[2]
            def keep(x, plane):
                h.vp[x + 1, pl.ds(PAD, ny), :] = plane

            if WINDOW[level]:
                planes(nx, make, keep)
                return
            zero = jnp.zeros((ny, LANES), jnp.float32)

            def pack(x, plane, carry):
                if not held:
                    keep(x, plane)
                high, low = carry
                h.ys[0, pl.ds(x, 1), :] = plane[ny - 1:ny]
                h.ys[1, pl.ds(x, 1), :] = plane[0:1]
                here = lane == x
                high = jnp.where(here, pltpu.roll(plane, lax.rem(x + LANES - (nz - 1), LANES), 1), high)
                low = jnp.where(here, pltpu.roll(plane, x, 1), low)
                return high, low

            high, low = planes(nx, make, pack, (zero, zero))
            for side, columns in enumerate((high, low)):
                packed = columns[0:8]
                for tile in range(1, ny // 8):
                    moved = pltpu.roll(columns[8 * tile:8 * tile + 8], nx * tile, 1)
                    packed = jnp.where((lane >= nx * tile) & (lane < nx * tile + nx), moved, packed)
                h.zs[side] = packed
            if held:
                pl.semaphore_wait(barrier, len(partners))
            for copy in copies(level, h):
                copy.start()

        def around(level, h, x):
            nx, ny = dims(level)
            vp = h.vp
            mid = vp[x + 1, pl.ds(PAD, ny), :]
            zm, zp = pltpu.roll(mid, 1, 1), pltpu.roll(mid, LANES - 1, 1)
            if level == 0:
                zlow, zhigh = h.zr[0], h.zr[1]
                zm = jnp.where(lane == 0, pltpu.roll(zlow, lax.rem(LANES - x, LANES), 1), zm)
                zp = jnp.where(lane == LANES - 1, pltpu.roll(zhigh, LANES - 1 - x, 1), zp)
            return (mid, vp[x, pl.ds(PAD, ny), :], vp[x + 2, pl.ds(PAD, ny), :],
                    vp[x + 1, pl.ds(PAD - 1, ny), :], vp[x + 1, pl.ds(PAD + 1, ny), :], zm, zp)

        def residual(level, h, x):
            g = refs.level[level]
            mid, xm, xp, ym, yp, zm, zp = around(level, h, x)
            total = g.sx[x] * xm + g.sx[x + 1] * xp + g.sym[x] * ym + g.syp[x] * yp + g.szm[x] * zm + g.szp[x] * zp
            return mid, source(level, x) - g.q[x] * mid + total

        def source(level, x):
            return rhs[x] if level == 0 else refs.level[level].f[x]

        def reaction(level, x):
            return coef_c[x] if level == 0 else refs.level[level].c[x]

        row_of = lax.broadcasted_iota(jnp.int32, (LANES, LANES), 0)
        col_of = lax.broadcasted_iota(jnp.int32, (LANES, LANES), 1)

        def pairing(level, wide, narrow):
            half = wide // 2
            return (half if level == 0 else half + jnp.where(wide >= 96, 64, 0)) == narrow

        def coarsen(level, count_x, get, put=None):
            pair = refs.level[level].pair
            shrink = jnp.where(pairing(level, row_of, col_of), 0.125, 0.0).astype(jnp.bfloat16)

            def put_pair(x, plane):
                pair[x, pl.ds(0, plane.shape[0]), :] = plane

            planes(count_x // 2, lambda x: get(2 * x) + get(2 * x + 1), put_pair)
            half = 16 if level == 1 else dims(level)[1] // 2
            made = exact_dot([pair[x, pl.ds(0, half, 2), :] + pair[x, pl.ds(1, half, 2), :]
                              for x in range(count_x // 2)], shrink)
            if put is not None:
                for x, plane in enumerate(made):
                    put(x, plane)
            return made

        def refine(level, count_x, get):
            pair = refs.level[level].pair
            grow = jnp.where(pairing(level, col_of, row_of), 1.0, 0.0).astype(jnp.bfloat16)
            rows = min(get(0).shape[0], pair.shape[1] // 2)
            for x, wide in enumerate(exact_dot([get(x) for x in range(count_x)], grow)):
                pair[x, pl.ds(0, rows, 2), :] = wide[:rows]
                pair[x, pl.ds(1, rows, 2), :] = wide[:rows]

        def block_parts(h, which, made):
            rows = own(1)[1]
            outer = jnp.zeros((rows, LANES), jnp.float32)
            for x, plane in enumerate(made):
                if x % 2:
                    h.pairs[which, x // 2] = made[x - 1] + pltpu.roll(plane, 64, 1)
                low = (lane >= 8 * x) & (lane < 8 * x + 8)
                high = (lane >= 64 + 8 * x) & (lane < 72 + 8 * x)
                outer = jnp.where(low, pltpu.roll(plane, 8 * x, 1), outer)
                outer = jnp.where(high, pltpu.roll(plane, 8 * x + 8, 1), outer)
            h.outer[which] = outer

        def part_copies(h, deep, steps=(1, 2, 3)):
            every = []
            for i, (dx, dy, dz) in enumerate(around_all):
                if abs(dx) + abs(dy) + abs(dz) not in steps:
                    continue
                rows = {-1: pl.ds(0, 8), 0: pl.ds(0, own(1)[1]), 1: pl.ds(own(1)[1] - 8, 8)}[dy]
                pairs = {-1: pl.ds(0, deep), 0: pl.ds(0, 4), 1: pl.ds(4 - deep, deep)}[dx]
                every_array = slice(None)
                if dz == 0:
                    src = h.pairs.at[every_array, pairs, rows]
                    dst = h.pairs_in.at[1 - dx, 1 - dy, every_array, pairs, rows]
                else:
                    src = h.outer.at[every_array, rows]
                    dst = h.outer_in.at[1 - dx, 1 - dy, (1 - dz) // 2, every_array, rows]
                every.append(pltpu.make_async_remote_copy(
                    src_ref=src, dst_ref=dst, send_sem=h.send.at[i], recv_sem=h.recv.at[i],
                    device_id={a: beyond(a, d) for a, d in zip(AXES, (dx, dy, dz))}, device_id_type=MESH))
            return every

        def parts_start(h, deep, steps=(1, 2, 3)):
            for copy in part_copies(h, deep, steps):
                copy.start()

        def parts_end(h, deep):
            for copy in part_copies(h, deep):
                copy.wait()

        def part_plane(h, which, plane):
            x = plane + 4
            dx, x = x // 8 - 1, x % 8
            rows_own = own(1)[1]
            pieces = []
            for dy, rows in ((-1, pl.ds(rows_own - 8, 8)), (0, pl.ds(0, rows_own)), (1, pl.ds(0, 8))):
                if (dx, dy) == (0, 0):
                    piece = h.pairs[which, x // 2, rows, :]
                else:
                    piece = h.pairs_in[1 + dx, 1 + dy, which, x // 2, rows, :]
                left = h.outer_in[1 + dx, 1 + dy, 0, which, rows, :]
                right = h.outer_in[1 + dx, 1 + dy, 1, which, rows, :]
                if x % 2:
                    piece = pltpu.roll(piece, 64, 1)
                piece = jnp.where(lane < 64, piece, 0.0)
                piece = jnp.where((lane >= 64) & (lane < 72), pltpu.roll(right, 64 - 8 * x, 1), piece)
                pieces.append(jnp.where(lane >= 120, pltpu.roll(left, (56 - 8 * x) % LANES, 1), piece))
            return pieces

        def put_pieces(ref, index, first, pieces):
            for piece in pieces:
                ref[index, pl.ds(first, piece.shape[0]), :] = piece
                first += piece.shape[0]

        def store(ref):
            def put(x, plane):
                ref[x] = plane

            return put

        def block_to(h, which):
            def put(x, plane):
                mean = pltpu.roll(jnp.where(lane < 32, plane[:12], 0.0), 32 * x, 1)
                rows = pl.ds(0, 12)
                h.block[which, rows, :] = mean if x == 0 else h.block[which, rows, :] + mean

            return put

        def near_copies(h):
            return [
                pltpu.make_async_remote_copy(
                    src_ref=h.block, dst_ref=h.near.at[3 - i], send_sem=h.near_send.at[i],
                    recv_sem=h.near_recv.at[3 - i], device_id={"gy": beyond("gy", dy)}, device_id_type=MESH)
                for i, dy in enumerate(NEAR)
            ]

        def all_copies(h):
            return [
                pltpu.make_async_remote_copy(
                    src_ref=h.column, dst_ref=h.all.at[1 - dz, place["gx"]], send_sem=h.all_send.at[1 - dz, dx],
                    recv_sem=h.all_recv.at[1 - dz, dx],
                    device_id={"gx": beyond("gx", dx), "gz": beyond("gz", dz)}, device_id_type=MESH)
                for dx, dz in around_xz
            ]

        def gather_near(h):
            for copy in near_copies(h):
                copy.start()

        def gather_all(h, arrays):
            for copy in near_copies(h):
                copy.wait()
            for k in range(arrays):
                h.column[k, pl.ds(0, 6), :] = h.near[0, k, pl.ds(6, 6), :]
                h.column[k, pl.ds(6, 12), :] = h.near[1, k, pl.ds(0, 12), :]
                h.column[k, pl.ds(18, 12), :] = h.block[k, pl.ds(0, 12), :]
                h.column[k, pl.ds(30, 12), :] = h.near[2, k, pl.ds(0, 12), :]
                h.column[k, pl.ds(42, 6), :] = h.near[3, k, pl.ds(0, 6), :]
            for copy in all_copies(h):
                copy.start()
            h.all[1, place["gx"]] = h.column[...]

        def gather_end(h):
            for copy in all_copies(h):
                copy.wait()

        def gathered(h, which, x, dx):
            left, here, right = (h.all[i, x, which] for i in range(3))
            plane = jnp.where(lane < 32, pltpu.roll(here, (LANES - 32 * dx) % LANES, 1), 0.0)
            plane = jnp.where((lane >= 32) & (lane < 64), pltpu.roll(right, (LANES + 32 - 32 * dx) % LANES, 1), plane)
            return jnp.where(lane >= 96, pltpu.roll(left, 96 - 32 * dx, 1), plane)

        def setup(level):
            g = refs.level[level]
            nx, ny = dims(level)
            nz = own(level)[2]
            half = 0.5 * 4.0 ** (LEVELS - 1 - level)
            finish(level, g.b)
            start_x, cells_x = first_plane(level), own(level)[0] * count["gx"]
            cells_y = own(level)[1]
            row = lax.broadcasted_iota(jnp.int32, (ny, 1), 0) + place["gy"] * cells_y - FIRST_ROW[level]
            if level == 0:
                column, used = lane, lane >= 0
            else:
                column = jnp.where(lane < 96, lane, lane - LANES)
                reach = 8 if level == 1 else nz
                used = (column < nz + reach) & (column >= -reach)
            column = column + place["gz"] * nz
            keep_ym = jnp.where(row == 0, 0.0, 1.0)
            keep_yp = jnp.where(row == cells_y * count["gy"] - 1, 0.0, 1.0)
            keep_zm = jnp.where(column == 0, 0.0, 1.0)
            keep_zp = jnp.where(column == nz * count["gz"] - 1, 0.0, 1.0)

            def make(x):
                mid, xm, xp, ym, yp, zm, zp = around(level, g.b, x)
                keep_xm = jnp.where((start_x + x == 0) | (start_x + x == cells_x), 0.0, 1.0)
                keep_xp = jnp.where(start_x + x == cells_x - 1, 0.0, 1.0)
                fxm, fxp = half * (mid + xm * keep_xm), half * (mid + xp * keep_xp)
                fym, fyp = half * (mid + ym * keep_ym), half * (mid + yp * keep_yp)
                fzm, fzp = half * (mid + zm * keep_zm), half * (mid + zp * keep_zp)
                q = reaction(level, x) + (fxm + fxp + fym + fyp + fzm + fzp)
                return (q, jnp.where(used, 1.0 / q, 0.0), fxm * keep_xm,
                        fym * keep_ym, fyp * keep_yp, fzm * keep_zm, fzp * keep_zp)

            def put(x, values):
                for name, value in zip(("q", "rq", "sx", "sym", "syp", "szm", "szp"), values):
                    getattr(g, name)[x] = value

            planes(nx, make, put)
            last = g.b.vp[nx, pl.ds(PAD, ny), :] + g.b.vp[nx + 1, pl.ds(PAD, ny), :]
            g.sx[nx] = half * last * jnp.where(start_x + nx == cells_x, 0.0, 1.0)

        def planes_of(level, h):
            ny = dims(level)[1]
            return lambda x: h.vp[x + 1, pl.ds(PAD, ny), :]

        levels = refs.level
        (_, first), (carry_e, weight_r) = chebyshev(2)
        of_f, of_bc = refs.gather

        def start_down(level):
            g = levels[level]
            sweep(level, lambda x: source(level, x) * g.rq[x] * first, g.it[0])

        def go_down(level):
            g = levels[level]

            def second(x):
                mid, rest = residual(level, g.it[0], x)
                return mid * (1.0 + carry_e) + weight_r * rest * g.rq[x]

            finish(level, g.it[0])
            sweep(level, second, g.it[1])

        def leave(level, put=None):
            g = levels[level]
            finish(level, g.it[1])
            if level == 1:
                rows = slice(FIRST_ROW[1], FIRST_ROW[1] + own(1)[1])
                return coarsen(1, own(1)[0], lambda x: residual(1, g.it[1], x + 4)[1][rows], put)
            return coarsen(level, dims(level)[0], lambda x: residual(level, g.it[1], x)[1], put)

        def go_up(level, begun, ended, put):
            g = levels[level]

            def third(x):
                mid, rest = residual(level, begun, x)
                update = first * rest * g.rq[x]
                g.e[x] = update
                return mid + update

            sweep(level, third, ended)
            finish(level, ended)

            def last(x):
                mid, rest = residual(level, ended, x)
                return mid + carry_e * g.e[x] + weight_r * rest * g.rq[x]

            planes(dims(level)[0], last, put)

        parts_f, parts_bc = refs.parts
        own_planes = own(0)[0]
        inputs[0].wait()
        fine_b = planes_of(0, levels[0].b)
        sweep(0, fine_b, levels[0].b, held=True)
        made_b = coarsen(0, own_planes, fine_b)
        inputs[1].wait()
        block_parts(parts_bc, 0, made_b)
        made_c = coarsen(0, own_planes, lambda x: coef_c[x])
        block_parts(parts_bc, 1, made_c)
        parts_start(parts_bc, 3, (1,))
        for which, made in enumerate((made_b, made_c)):
            for x, plane in enumerate(made):
                levels[1].e[x, pl.ds(0, own(1)[1]), :] = plane
            coarsen(1, own(1)[0], lambda x: levels[1].e[x, pl.ds(0, own(1)[1]), :], block_to(of_bc, which))

        setup(0)
        inputs[2].wait()
        start_down(0)
        gather_near(of_bc)
        parts_start(parts_bc, 3, (2,))
        go_down(0)
        parts_start(parts_bc, 3, (3,))

        block_parts(parts_f, 0, leave(0))
        parts_start(parts_f, 2)
        gather_all(of_bc, 2)

        parts_end(parts_bc, 3)
        for w in range(-1, 17):
            put_pieces(levels[1].b.vp, w + 1, PAD, part_plane(parts_bc, 0, w))
            if 0 <= w < 16:
                put_pieces(levels[1].c, w, 0, part_plane(parts_bc, 1, w))
        setup(1)
        parts_end(parts_f, 2)
        for w in range(16):
            put_pieces(levels[1].f, w, 0, part_plane(parts_f, 0, w))
        start_down(1)
        go_down(1)
        leave(1, block_to(of_f, 0))
        gather_near(of_f)
        gather_all(of_f, 1)
        gather_end(of_bc)
        for dx in range(4):
            def spread(x, carry, dx=dx):
                levels[2].b.vp[4 * x + dx + 1, pl.ds(PAD, 48), :] = gathered(of_bc, 0, x, dx)
                levels[2].c[4 * x + dx] = gathered(of_bc, 1, x, dx)
                return carry

            lax.fori_loop(0, 4, spread, 0)
        coarsen(2, 16, planes_of(2, levels[2].b), store(levels[3].f))
        sweep(3, lambda x: levels[3].f[x], levels[3].b)
        coarsen(2, 16, lambda x: levels[2].c[x], store(levels[3].c))
        setup(2)
        setup(3)
        gather_end(of_f)
        for dx in range(4):
            def spread_f(x, carry, dx=dx):
                levels[2].f[4 * x + dx] = gathered(of_f, 0, x, dx)
                return carry

            lax.fori_loop(0, 4, spread_f, 0)

        start_down(2)
        go_down(2)
        leave(2, store(levels[3].f))

        g = levels[3]
        steps = chebyshev(COARSE_SWEEPS)

        def begin(x):
            update = source(3, x) * g.rq[x] * steps[0][1]
            g.e[x] = update
            return update

        sweep(3, begin, g.it[0])
        for step in range(1, COARSE_SWEEPS):
            def advance(x, step=step):
                mid, rest = residual(3, g.it[(step - 1) % 2], x)
                update = steps[step][0] * g.e[x] + steps[step][1] * rest * g.rq[x]
                g.e[x] = update
                return mid + update

            sweep(3, advance, g.it[step % 2])

        refine(2, 8, planes_of(3, g.it[(COARSE_SWEEPS - 1) % 2]))
        g = levels[2]
        sweep(2, lambda x: planes_of(2, g.it[1])(x) + g.pair[x // 2], g.it[0])
        go_up(2, g.it[0], g.it[1], store(g.f))

        g = levels[1]
        start_x = place["gx"] * own(2)[0] - 2
        refine(1, 8, lambda x: levels[2].f[jnp.clip(start_x + x, 0, 15), pl.ds(14, 24), :])
        sweep(1, lambda x: planes_of(1, g.it[1])(x) + g.pair[x // 2], g.it[0])
        go_up(1, g.it[0], g.it[1], store(g.f))

        g = levels[0]
        refine(0, 10, lambda x: levels[1].f[x + 3])
        begun = g.it[2]
        for x in range(18):
            begun.vp[x] = g.it[1].vp[x] + g.pair[(x + 1) // 2, pl.ds(8, 64), :]
        own_rows = own(1)[1]
        edges = [jnp.zeros((own_rows, LANES), jnp.float32)] * 2
        for x in range(8):
            plane = levels[1].f[x + 4, pl.ds(8, own_rows), :]
            for side, column in enumerate((LANES - 1, 64)):
                for target in (2 * x, 2 * x + 1):
                    moved = pltpu.roll(plane, (target - column) % LANES, 1)
                    edges[side] = jnp.where(lane == target, moved, edges[side])
        for side in range(2):
            g.edge[side, pl.ds(0, own_rows, 2), :] = edges[side]
            g.edge[side, pl.ds(1, own_rows, 2), :] = edges[side]
            begun.zr[side] = g.it[1].zr[side] + g.edge[side]
        go_up(0, begun, g.it[3], store(out))

    return kernel


class Plan:
    def __init__(self, shape):
        self.shapes = []
        self.tree = Names()
        self.tree.level = []
        for level in range(LEVELS):
            nx, ny = WINDOW[level] or tuple(n >> level for n in shape)[:2]
            g = Names()

            def planes(n, ny=ny):
                return self.add(pltpu.VMEM((n, ny, LANES), jnp.float32))

            def halo(exchanged, nx=nx, ny=ny):
                h = Names()
                h.vp = self.add(pltpu.VMEM((nx + 2, round_up(ny) + 2 * PAD, LANES), jnp.float32))
                if exchanged:
                    for name, rows in (("zs", 8), ("zin", 8), ("zr", ny), ("ys", nx), ("yr", nx)):
                        setattr(h, name, self.add(pltpu.VMEM((2, round_up(rows), LANES), jnp.float32)))
                    h.send = self.add(pltpu.SemaphoreType.DMA((6,)))
                    h.recv = self.add(pltpu.SemaphoreType.DMA((6,)))
                return h

            exchanged = WINDOW[level] is None
            g.b = halo(exchanged)
            g.sx = planes(nx + 1)
            for name in ("sym", "syp", "szm", "szp", "q", "rq", "e"):
                setattr(g, name, planes(nx))
            if level > 0:
                g.f = planes(nx)
                g.c = planes(nx)
            if level == 0:
                g.pair = self.add(pltpu.VMEM((10, 80, LANES), jnp.float32))
                g.edge = planes(2)
            elif level < LEVELS - 1:
                g.pair = planes(nx // 2)
            g.it = [halo(exchanged) for _ in range(4 if exchanged else 2)]
            self.tree.level.append(g)
        self.tree.rhs = self.add(pltpu.VMEM(shape, jnp.float32))
        self.tree.coef_c = self.add(pltpu.VMEM(shape, jnp.float32))
        self.tree.load = self.add(pltpu.SemaphoreType.DMA((3,)))
        self.tree.gather = [self.gathered(1), self.gathered(2)]
        self.tree.parts = [self.parted(1, shape[1] // 2), self.parted(2, shape[1] // 2)]

    def parted(self, arrays, rows):
        h = Names()
        h.pairs = self.add(pltpu.VMEM((arrays, 4, rows, LANES), jnp.float32))
        h.outer = self.add(pltpu.VMEM((arrays, rows, LANES), jnp.float32))
        h.pairs_in = self.add(pltpu.VMEM((3, 3, arrays, 4, rows, LANES), jnp.float32))
        h.outer_in = self.add(pltpu.VMEM((3, 3, 2, arrays, rows, LANES), jnp.float32))
        h.send = self.add(pltpu.SemaphoreType.DMA((26,)))
        h.recv = self.add(pltpu.SemaphoreType.DMA((26,)))
        return h

    def gathered(self, arrays):
        h = Names()
        h.block = self.add(pltpu.VMEM((arrays, 16, LANES), jnp.float32))
        h.near = self.add(pltpu.VMEM((4, arrays, 16, LANES), jnp.float32))
        h.column = self.add(pltpu.VMEM((arrays, 48, LANES), jnp.float32))
        h.all = self.add(pltpu.VMEM((3, 4, arrays, 48, LANES), jnp.float32))
        h.near_send = self.add(pltpu.SemaphoreType.DMA((4,)))
        h.near_recv = self.add(pltpu.SemaphoreType.DMA((4,)))
        h.all_send = self.add(pltpu.SemaphoreType.DMA((3, 4)))
        h.all_recv = self.add(pltpu.SemaphoreType.DMA((3, 4)))
        return h

    def add(self, shape):
        self.shapes.append(shape)
        return len(self.shapes) - 1

    def unpack(self, refs):
        def walk(node):
            if isinstance(node, int):
                return refs[node]
            if isinstance(node, list):
                return [walk(item) for item in node]
            result = Names()
            for name, item in vars(node).items():
                setattr(result, name, walk(item))
            return result

        return walk(self.tree)


def solution(mesh):
    sizes = dict(mesh.shape)

    def local(rhs, coef_b, coef_c):
        shape = rhs.shape
        plan = Plan(shape)
        return pl.pallas_call(
            make_kernel(shape, sizes, plan),
            out_shape=jax.ShapeDtypeStruct(shape, jnp.float32),
            in_specs=[pl.BlockSpec(memory_space=pl.ANY)] * 3,
            out_specs=pl.BlockSpec(memory_space=pltpu.VMEM),
            scratch_shapes=plan.shapes,
            compiler_params=pltpu.CompilerParams(
                collective_id=0, has_side_effects=True, vmem_limit_bytes=56 * 2**20),
        )(rhs, coef_b, coef_c)

    return jax.shard_map(
        local,
        mesh=mesh,
        in_specs=(P(*AXES),) * 3,
        out_specs=P(*AXES),
        check_vma=False,
    )
```

```python
import jax
import jax.numpy as jnp
from jax import lax
from jax.experimental import pallas as pl
from jax.experimental.pallas import tpu as pltpu
from jax.sharding import PartitionSpec as P

LEVELS = 4
COARSE_SWEEPS = 6
CENTRE = 1.1
RADIUS = 0.9
LANES = 128
PAD = 8

MESH = pl.DeviceIdType.MESH
AXES = ("gx", "gy", "gz")


def chebyshev(sweeps):
    ratio = RADIUS / CENTRE
    factors = [(0.0, 1.0 / CENTRE)]
    for _ in range(sweeps - 1):
        following = 1.0 / (2.0 * CENTRE / RADIUS - ratio)
        factors.append((following * ratio, 2.0 * following / RADIUS))
        ratio = following
    return factors


def round_up(value):
    return -(-value // 8) * 8


class Names:
    pass


def exact_dot(lefts, matrix):
    left = jnp.concatenate(lefts, axis=0)
    high = left.astype(jnp.bfloat16)
    rest = left - high.astype(jnp.float32)
    middle = rest.astype(jnp.bfloat16)
    low = (rest - middle.astype(jnp.float32)).astype(jnp.bfloat16)
    product = jnp.dot(jnp.concatenate([low, middle, high], axis=0), matrix, preferred_element_type=jnp.float32)
    total, rows = left.shape[0], lefts[0].shape[0]
    product = (product[:total] + product[total:2 * total]) + product[2 * total:]
    return [product[rows * k:rows * k + rows] for k in range(len(lefts))]


WINDOW = (None, (16, 40), (16, 48), (8, 24))
FIRST_ROW = (0, 8, 18, 9)
NEAR = (-2, -1, 1, 2)
TOGETHER = 16


def make_kernel(shape, sizes, plan):
    count = {axis: sizes[axis] for axis in AXES}

    def kernel(rhs_in, coef_b_in, coef_c_in, out, *scratch):
        refs = plan.unpack(scratch)
        rhs, coef_c = refs.rhs, refs.coef_c
        inputs = [
            pltpu.make_async_copy(source, target, refs.load.at[i])
            for i, (source, target) in enumerate((
                (coef_b_in, refs.level[0].b.vp.at[pl.ds(1, shape[0]), pl.ds(PAD, shape[1])]),
                (coef_c_in, coef_c), (rhs_in, rhs)))
        ]
        place = {axis: lax.axis_index(axis) for axis in AXES}

        def beyond(axis, step):
            return lax.rem(place[axis] + count[axis] + step, count[axis])

        after = {axis: beyond(axis, 1) for axis in AXES}
        before = {axis: beyond(axis, -1) for axis in AXES}
        def own(level):
            return tuple(n >> level for n in shape)

        def first_plane(level):
            if level > 1:
                return 0
            return place["gx"] * own(level)[0] - (4 if level == 1 else 0)

        sides = (-1, 0, 1)
        around_all = [(dx, dy, dz) for dx in sides for dy in sides for dz in sides if (dx, dy, dz) != (0, 0, 0)]
        around_xz = [(dx, dz) for dx in range(4) for dz in (-1, 0, 1) if (dx, dz) != (0, 0)]

        barrier = pltpu.get_barrier_semaphore()
        partners = [offset for offset in around_all if sum(map(abs, offset)) == 1]
        for offset in partners:
            pl.semaphore_signal(barrier, inc=1, device_id={a: beyond(a, d) for a, d in zip(AXES, offset)},
                                device_id_type=MESH)
        for copy in inputs:
            copy.start()

        lane = lax.broadcasted_iota(jnp.int32, (1, LANES), 1)

        def dims(level):
            return WINDOW[level] or own(level)[:2]

        def clear_rim(level, h):
            nx, ny = dims(level)
            h.vp[0] = jnp.zeros(h.vp.shape[1:], jnp.float32)
            h.vp[nx + 1] = jnp.zeros(h.vp.shape[1:], jnp.float32)
            rim = jnp.zeros((nx, PAD, LANES), jnp.float32)
            h.vp[pl.ds(1, nx), pl.ds(0, PAD), :] = rim
            h.vp[pl.ds(1, nx), pl.ds(PAD + ny, PAD), :] = rim

        for level in range(LEVELS):
            if WINDOW[level]:
                for h in [refs.level[level].b] + refs.level[level].it:
                    clear_rim(level, h)

        def copies(level, h):
            nx, ny = dims(level)
            rows = pl.ds(PAD, round_up(ny))
            vp, zs, zin, ys, yr = h.vp, h.zs, h.zin, h.ys, h.yr
            pairs = (
                (vp.at[nx, rows], vp.at[0, rows], "gx", after),
                (vp.at[1, rows], vp.at[nx + 1, rows], "gx", before),
                (ys.at[0], yr.at[0], "gy", after),
                (ys.at[1], yr.at[1], "gy", before),
                (zs.at[0], zin.at[0], "gz", after),
                (zs.at[1], zin.at[1], "gz", before),
            )
            return [
                pltpu.make_async_remote_copy(
                    src_ref=src, dst_ref=dst, send_sem=h.send.at[i], recv_sem=h.recv.at[i],
                    device_id={axis: where[axis]}, device_id_type=MESH)
                for i, (src, dst, axis, where) in enumerate(pairs)
            ]

        def finish(level, h):
            if WINDOW[level]:
                return
            nx, ny = dims(level)
            for copy in copies(level, h):
                copy.wait()
            for side in range(2):
                packed = h.zin[side]
                for tile in range(ny // 8):
                    h.zr[side, pl.ds(8 * tile, 8), :] = pltpu.roll(packed, (LANES - nx * tile) % LANES, 1)
            for x in range(nx):
                h.vp[x + 1, pl.ds(PAD - 1, 1), :] = h.yr[0, pl.ds(x, 1), :]
                h.vp[x + 1, pl.ds(PAD + ny, 1), :] = h.yr[1, pl.ds(x, 1), :]

        def planes(n, make, put, carry=None):
            step = min(n, TOGETHER)

            def body(i, carry):
                made = [make(i * step + k) for k in range(step)]
                for k in range(step):
                    if carry is None:
                        put(i * step + k, made[k])
                    else:
                        carry = put(i * step + k, made[k], carry)
                return carry

            if carry is not None:
                return lax.fori_loop(0, n // step, body, carry)

            def plain(i, zero):
                body(i, None)
                return zero

            lax.fori_loop(0, n // step, plain, 0)

        def sweep(level, make, h, held=False):
            nx, ny = dims(level)
            nz = own(level)[2]
            def keep(x, plane):
                h.vp[x + 1, pl.ds(PAD, ny), :] = plane

            if WINDOW[level]:
                planes(nx, make, keep)
                return
            zero = jnp.zeros((ny, LANES), jnp.float32)

            def pack(x, plane, carry):
                if not held:
                    keep(x, plane)
                high, low = carry
                h.ys[0, pl.ds(x, 1), :] = plane[ny - 1:ny]
                h.ys[1, pl.ds(x, 1), :] = plane[0:1]
                here = lane == x
                high = jnp.where(here, pltpu.roll(plane, lax.rem(x + LANES - (nz - 1), LANES), 1), high)
                low = jnp.where(here, pltpu.roll(plane, x, 1), low)
                return high, low

            high, low = planes(nx, make, pack, (zero, zero))
            for side, columns in enumerate((high, low)):
                packed = columns[0:8]
                for tile in range(1, ny // 8):
                    moved = pltpu.roll(columns[8 * tile:8 * tile + 8], nx * tile, 1)
                    packed = jnp.where((lane >= nx * tile) & (lane < nx * tile + nx), moved, packed)
                h.zs[side] = packed
            if held:
                pl.semaphore_wait(barrier, len(partners))
            for copy in copies(level, h):
                copy.start()

        def around(level, h, x):
            nx, ny = dims(level)
            vp = h.vp
            mid = vp[x + 1, pl.ds(PAD, ny), :]
            zm, zp = pltpu.roll(mid, 1, 1), pltpu.roll(mid, LANES - 1, 1)
            if level == 0:
                zlow, zhigh = h.zr[0], h.zr[1]
                zm = jnp.where(lane == 0, pltpu.roll(zlow, lax.rem(LANES - x, LANES), 1), zm)
                zp = jnp.where(lane == LANES - 1, pltpu.roll(zhigh, LANES - 1 - x, 1), zp)
            return (mid, vp[x, pl.ds(PAD, ny), :], vp[x + 2, pl.ds(PAD, ny), :],
                    vp[x + 1, pl.ds(PAD - 1, ny), :], vp[x + 1, pl.ds(PAD + 1, ny), :], zm, zp)

        def residual(level, h, x):
            g = refs.level[level]
            mid, xm, xp, ym, yp, zm, zp = around(level, h, x)
            total = g.sx[x] * xm + g.sx[x + 1] * xp + g.sym[x] * ym + g.syp[x] * yp + g.szm[x] * zm + g.szp[x] * zp
            return mid, source(level, x) - g.q[x] * mid + total

        def source(level, x):
            return rhs[x] if level == 0 else refs.level[level].f[x]

        def reaction(level, x):
            return coef_c[x] if level == 0 else refs.level[level].c[x]

        row_of = lax.broadcasted_iota(jnp.int32, (LANES, LANES), 0)
        col_of = lax.broadcasted_iota(jnp.int32, (LANES, LANES), 1)

        def pairing(level, wide, narrow):
            half = wide // 2
            return (half if level == 0 else half + jnp.where(wide >= 96, 64, 0)) == narrow

        def coarsen(level, count_x, get, put=None):
            pair = refs.level[level].pair
            shrink = jnp.where(pairing(level, row_of, col_of), 0.125, 0.0).astype(jnp.bfloat16)

            def put_pair(x, plane):
                pair[x, pl.ds(0, plane.shape[0]), :] = plane

            planes(count_x // 2, lambda x: get(2 * x) + get(2 * x + 1), put_pair)
            half = 16 if level == 1 else dims(level)[1] // 2
            made = exact_dot([pair[x, pl.ds(0, half, 2), :] + pair[x, pl.ds(1, half, 2), :]
                              for x in range(count_x // 2)], shrink)
            if put is not None:
                for x, plane in enumerate(made):
                    put(x, plane)
            return made

        def refine(level, count_x, get):
            pair = refs.level[level].pair
            grow = jnp.where(pairing(level, col_of, row_of), 1.0, 0.0).astype(jnp.bfloat16)
            rows = min(get(0).shape[0], pair.shape[1] // 2)
            for x, wide in enumerate(exact_dot([get(x) for x in range(count_x)], grow)):
                pair[x, pl.ds(0, rows, 2), :] = wide[:rows]
                pair[x, pl.ds(1, rows, 2), :] = wide[:rows]

        def block_parts(h, which, made):
            rows = own(1)[1]
            outer = jnp.zeros((rows, LANES), jnp.float32)
            for x, plane in enumerate(made):
                if x % 2:
                    h.pairs[which, x // 2] = made[x - 1] + pltpu.roll(plane, 64, 1)
                low = (lane >= 8 * x) & (lane < 8 * x + 8)
                high = (lane >= 64 + 8 * x) & (lane < 72 + 8 * x)
                outer = jnp.where(low, pltpu.roll(plane, 8 * x, 1), outer)
                outer = jnp.where(high, pltpu.roll(plane, 8 * x + 8, 1), outer)
            h.outer[which] = outer

        def part_copies(h, deep, steps=(1, 2, 3)):
            every = []
            for i, (dx, dy, dz) in enumerate(around_all):
                if abs(dx) + abs(dy) + abs(dz) not in steps:
                    continue
                rows = {-1: pl.ds(0, 8), 0: pl.ds(0, own(1)[1]), 1: pl.ds(own(1)[1] - 8, 8)}[dy]
                pairs = {-1: pl.ds(0, deep), 0: pl.ds(0, 4), 1: pl.ds(4 - deep, deep)}[dx]
                every_array = slice(None)
                if dz == 0:
                    src = h.pairs.at[every_array, pairs, rows]
                    dst = h.pairs_in.at[1 - dx, 1 - dy, every_array, pairs, rows]
                else:
                    src = h.outer.at[every_array, rows]
                    dst = h.outer_in.at[1 - dx, 1 - dy, (1 - dz) // 2, every_array, rows]
                every.append(pltpu.make_async_remote_copy(
                    src_ref=src, dst_ref=dst, send_sem=h.send.at[i], recv_sem=h.recv.at[i],
                    device_id={a: beyond(a, d) for a, d in zip(AXES, (dx, dy, dz))}, device_id_type=MESH))
            return every

        def parts_start(h, deep, steps=(1, 2, 3)):
            for copy in part_copies(h, deep, steps):
                copy.start()

        def parts_end(h, deep):
            for copy in part_copies(h, deep):
                copy.wait()

        def part_plane(h, which, plane):
            x = plane + 4
            dx, x = x // 8 - 1, x % 8
            rows_own = own(1)[1]
            pieces = []
            for dy, rows in ((-1, pl.ds(rows_own - 8, 8)), (0, pl.ds(0, rows_own)), (1, pl.ds(0, 8))):
                if (dx, dy) == (0, 0):
                    piece = h.pairs[which, x // 2, rows, :]
                else:
                    piece = h.pairs_in[1 + dx, 1 + dy, which, x // 2, rows, :]
                left = h.outer_in[1 + dx, 1 + dy, 0, which, rows, :]
                right = h.outer_in[1 + dx, 1 + dy, 1, which, rows, :]
                if x % 2:
                    piece = pltpu.roll(piece, 64, 1)
                piece = jnp.where(lane < 64, piece, 0.0)
                piece = jnp.where((lane >= 64) & (lane < 72), pltpu.roll(right, 64 - 8 * x, 1), piece)
                pieces.append(jnp.where(lane >= 120, pltpu.roll(left, (56 - 8 * x) % LANES, 1), piece))
            return pieces

        def put_pieces(ref, index, first, pieces):
            for piece in pieces:
                ref[index, pl.ds(first, piece.shape[0]), :] = piece
                first += piece.shape[0]

        def store(ref):
            def put(x, plane):
                ref[x] = plane

            return put

        levels = refs.level
        of_f, of_bc = refs.gather

        def block_to(h, which):
            def put(x, plane):
                mean = pltpu.roll(jnp.where(lane < 32, plane[:12], 0.0), 32 * x, 1)
                rows = pl.ds(0, 12)
                h.block[which, rows, :] = mean if x == 0 else h.block[which, rows, :] + mean

            return put

        def near_copies(h):
            return [
                pltpu.make_async_remote_copy(
                    src_ref=h.block, dst_ref=h.near.at[3 - i], send_sem=h.near_send.at[i],
                    recv_sem=h.near_recv.at[3 - i], device_id={"gy": beyond("gy", dy)}, device_id_type=MESH)
                for i, dy in enumerate(NEAR)
            ]

        def all_copies(h):
            every = []
            for dx, dz in around_xz:
                src, dst = h.column, h.all.at[1 - dz, place["gx"]]
                if dz and h is of_f:
                    src, dst = h.halves.at[(1 + dz) // 2], h.side.at[(1 - dz) // 2, place["gx"]]
                every.append(pltpu.make_async_remote_copy(
                    src_ref=src, dst_ref=dst, send_sem=h.all_send.at[1 - dz, dx], recv_sem=h.all_recv.at[1 - dz, dx],
                    device_id={"gx": beyond("gx", dx), "gz": beyond("gz", dz)}, device_id_type=MESH))
            return every

        def gather_near(h):
            for copy in near_copies(h):
                copy.start()

        def gather_all(h, arrays):
            for copy in near_copies(h):
                copy.wait()
            for k in range(arrays):
                h.column[k, pl.ds(0, 6), :] = h.near[0, k, pl.ds(6, 6), :]
                h.column[k, pl.ds(6, 12), :] = h.near[1, k, pl.ds(0, 12), :]
                h.column[k, pl.ds(18, 12), :] = h.block[k, pl.ds(0, 12), :]
                h.column[k, pl.ds(30, 12), :] = h.near[2, k, pl.ds(0, 12), :]
                h.column[k, pl.ds(42, 6), :] = h.near[3, k, pl.ds(0, 6), :]
            if h is of_f:
                lower = lax.rem(lane, 32) < 16
                top, bottom = h.column[0, pl.ds(0, 24), :], h.column[0, pl.ds(24, 24), :]
                h.halves[0] = jnp.where(lower, top, pltpu.roll(bottom, 16, 1))
                h.halves[1] = jnp.where(lower, pltpu.roll(bottom, LANES - 16, 1), top)
            for copy in all_copies(h):
                copy.start()
            h.all[1, place["gx"]] = h.column[...]

        def gather_end(h):
            for copy in all_copies(h):
                copy.wait()

        def gathered(h, which, x, dx):
            if h is of_f:
                here = h.all[1, x, which]
                left, right = h.side[0, x], h.side[1, x]
                plane = jnp.where(lane < 32, pltpu.roll(here, (LANES - 32 * dx) % LANES, 1), 0.0)
                parts = []
                for k, part in enumerate((plane[:24], plane[24:])):
                    moved = pltpu.roll(right, (LANES + 32 - 16 * k - 32 * dx) % LANES, 1)
                    part = jnp.where((lane >= 32) & (lane < 48), moved, part)
                    moved = pltpu.roll(left, (LANES + 96 + 16 * k - 32 * dx) % LANES, 1)
                    parts.append(jnp.where(lane >= 112, moved, part))
                return jnp.concatenate(parts, axis=0)
            left, here, right = (h.all[i, x, which] for i in range(3))
            plane = jnp.where(lane < 32, pltpu.roll(here, (LANES - 32 * dx) % LANES, 1), 0.0)
            plane = jnp.where((lane >= 32) & (lane < 64), pltpu.roll(right, (LANES + 32 - 32 * dx) % LANES, 1), plane)
            return jnp.where(lane >= 96, pltpu.roll(left, 96 - 32 * dx, 1), plane)

        def setup(level):
            g = refs.level[level]
            nx, ny = dims(level)
            nz = own(level)[2]
            half = 0.5 * 4.0 ** (LEVELS - 1 - level)
            finish(level, g.b)
            start_x, cells_x = first_plane(level), own(level)[0] * count["gx"]
            cells_y = own(level)[1]
            row = lax.broadcasted_iota(jnp.int32, (ny, 1), 0) + place["gy"] * cells_y - FIRST_ROW[level]
            if level == 0:
                column, used = lane, lane >= 0
            else:
                column = jnp.where(lane < 96, lane, lane - LANES)
                reach = 8 if level == 1 else nz
                used = (column < nz + reach) & (column >= -reach)
            column = column + place["gz"] * nz
            keep_ym = jnp.where(row == 0, 0.0, 1.0)
            keep_yp = jnp.where(row == cells_y * count["gy"] - 1, 0.0, 1.0)
            keep_zm = jnp.where(column == 0, 0.0, 1.0)
            keep_zp = jnp.where(column == nz * count["gz"] - 1, 0.0, 1.0)

            def make(x):
                mid, xm, xp, ym, yp, zm, zp = around(level, g.b, x)
                keep_xm = jnp.where((start_x + x == 0) | (start_x + x == cells_x), 0.0, 1.0)
                keep_xp = jnp.where(start_x + x == cells_x - 1, 0.0, 1.0)
                fxm, fxp = half * (mid + xm * keep_xm), half * (mid + xp * keep_xp)
                fym, fyp = half * (mid + ym * keep_ym), half * (mid + yp * keep_yp)
                fzm, fzp = half * (mid + zm * keep_zm), half * (mid + zp * keep_zp)
                q = reaction(level, x) + (fxm + fxp + fym + fyp + fzm + fzp)
                return (q, jnp.where(used, 1.0 / q, 0.0), fxm * keep_xm,
                        fym * keep_ym, fyp * keep_yp, fzm * keep_zm, fzp * keep_zp)

            def put(x, values):
                for name, value in zip(("q", "rq", "sx", "sym", "syp", "szm", "szp"), values):
                    getattr(g, name)[x] = value

            planes(nx, make, put)
            last = g.b.vp[nx, pl.ds(PAD, ny), :] + g.b.vp[nx + 1, pl.ds(PAD, ny), :]
            g.sx[nx] = half * last * jnp.where(start_x + nx == cells_x, 0.0, 1.0)

        def planes_of(level, h):
            ny = dims(level)[1]
            return lambda x: h.vp[x + 1, pl.ds(PAD, ny), :]

        (_, first), (carry_e, weight_r) = chebyshev(2)

        def start_down(level):
            g = levels[level]
            sweep(level, lambda x: source(level, x) * g.rq[x] * first, g.it[0])

        def go_down(level):
            g = levels[level]

            def second(x):
                mid, rest = residual(level, g.it[0], x)
                return mid * (1.0 + carry_e) + weight_r * rest * g.rq[x]

            finish(level, g.it[0])
            sweep(level, second, g.it[1])

        def leave(level, put=None):
            g = levels[level]
            finish(level, g.it[1])
            if level == 1:
                rows = slice(FIRST_ROW[1], FIRST_ROW[1] + own(1)[1])
                return coarsen(1, own(1)[0], lambda x: residual(1, g.it[1], x + 4)[1][rows], put)
            return coarsen(level, dims(level)[0], lambda x: residual(level, g.it[1], x)[1], put)

        def go_up(level, begun, ended, put):
            g = levels[level]

            def third(x):
                mid, rest = residual(level, begun, x)
                update = first * rest * g.rq[x]
                g.e[x] = update
                return mid + update

            sweep(level, third, ended)
            finish(level, ended)

            def last(x):
                mid, rest = residual(level, ended, x)
                return mid + carry_e * g.e[x] + weight_r * rest * g.rq[x]

            planes(dims(level)[0], last, put)

        parts_f, parts_bc = refs.parts
        own_planes = own(0)[0]
        inputs[0].wait()
        fine_b = planes_of(0, levels[0].b)
        sweep(0, fine_b, levels[0].b, held=True)
        made_b = coarsen(0, own_planes, fine_b)
        inputs[1].wait()
        block_parts(parts_bc, 0, made_b)
        made_c = coarsen(0, own_planes, lambda x: coef_c[x])
        block_parts(parts_bc, 1, made_c)
        parts_start(parts_bc, 3, (1,))
        for which, made in enumerate((made_b, made_c)):
            for x, plane in enumerate(made):
                levels[1].e[x, pl.ds(0, own(1)[1]), :] = plane
            coarsen(1, own(1)[0], lambda x: levels[1].e[x, pl.ds(0, own(1)[1]), :], block_to(of_bc, which))

        setup(0)
        inputs[2].wait()
        start_down(0)
        gather_near(of_bc)
        parts_start(parts_bc, 3, (2,))
        go_down(0)
        parts_start(parts_bc, 3, (3,))

        block_parts(parts_f, 0, leave(0))
        parts_start(parts_f, 2)
        gather_all(of_bc, 2)

        parts_end(parts_bc, 3)
        for w in range(-1, 17):
            put_pieces(levels[1].b.vp, w + 1, PAD, part_plane(parts_bc, 0, w))
            if 0 <= w < 16:
                put_pieces(levels[1].c, w, 0, part_plane(parts_bc, 1, w))
        setup(1)
        parts_end(parts_f, 2)
        for w in range(16):
            put_pieces(levels[1].f, w, 0, part_plane(parts_f, 0, w))
        start_down(1)
        go_down(1)
        leave(1, block_to(of_f, 0))
        gather_near(of_f)
        gather_all(of_f, 1)
        gather_end(of_bc)
        for dx in range(4):
            for x in range(4):
                levels[2].b.vp[4 * x + dx + 1, pl.ds(PAD, 48), :] = gathered(of_bc, 0, x, dx)
                levels[2].c[4 * x + dx] = gathered(of_bc, 1, x, dx)
        coarsen(2, 16, planes_of(2, levels[2].b), store(levels[3].f))
        sweep(3, lambda x: levels[3].f[x], levels[3].b)
        coarsen(2, 16, lambda x: levels[2].c[x], store(levels[3].c))
        setup(2)
        setup(3)
        gather_end(of_f)
        for dx in range(4):
            for x in range(4):
                levels[2].f[4 * x + dx] = gathered(of_f, 0, x, dx)

        start_down(2)
        go_down(2)
        leave(2, store(levels[3].f))

        g = levels[3]
        steps = chebyshev(COARSE_SWEEPS)

        def begin(x):
            update = source(3, x) * g.rq[x] * steps[0][1]
            g.e[x] = update
            return update

        sweep(3, begin, g.it[0])
        for step in range(1, COARSE_SWEEPS):
            def advance(x, step=step):
                mid, rest = residual(3, g.it[(step - 1) % 2], x)
                update = steps[step][0] * g.e[x] + steps[step][1] * rest * g.rq[x]
                g.e[x] = update
                return mid + update

            sweep(3, advance, g.it[step % 2])

        refine(2, 8, planes_of(3, g.it[(COARSE_SWEEPS - 1) % 2]))
        g = levels[2]
        sweep(2, lambda x: planes_of(2, g.it[1])(x) + g.pair[x // 2], g.it[0])
        go_up(2, g.it[0], g.it[1], store(g.f))

        g = levels[1]
        start_x = place["gx"] * own(2)[0] - 2
        refine(1, 8, lambda x: levels[2].f[jnp.clip(start_x + x, 0, 15), pl.ds(14, 24), :])
        sweep(1, lambda x: planes_of(1, g.it[1])(x) + g.pair[x // 2], g.it[0])
        go_up(1, g.it[0], g.it[1], store(g.f))

        g = levels[0]
        refine(0, 10, lambda x: levels[1].f[x + 3])
        begun = g.it[2]
        for x in range(18):
            begun.vp[x] = g.it[1].vp[x] + g.pair[(x + 1) // 2, pl.ds(8, 64), :]
        own_rows = own(1)[1]
        edges = [jnp.zeros((own_rows, LANES), jnp.float32)] * 2
        for x in range(8):
            plane = levels[1].f[x + 4, pl.ds(8, own_rows), :]
            for side, column in enumerate((LANES - 1, 64)):
                for target in (2 * x, 2 * x + 1):
                    moved = pltpu.roll(plane, (target - column) % LANES, 1)
                    edges[side] = jnp.where(lane == target, moved, edges[side])
        for side in range(2):
            g.edge[side, pl.ds(0, own_rows, 2), :] = edges[side]
            g.edge[side, pl.ds(1, own_rows, 2), :] = edges[side]
            begun.zr[side] = g.it[1].zr[side] + g.edge[side]
        go_up(0, begun, g.it[3], store(out))

    return kernel


class Plan:
    def __init__(self, shape):
        self.shapes = []
        self.tree = Names()
        self.tree.level = []
        for level in range(LEVELS):
            nx, ny = WINDOW[level] or tuple(n >> level for n in shape)[:2]
            g = Names()

            def planes(n, ny=ny):
                return self.add(pltpu.VMEM((n, ny, LANES), jnp.float32))

            def halo(exchanged, nx=nx, ny=ny):
                h = Names()
                h.vp = self.add(pltpu.VMEM((nx + 2, round_up(ny) + 2 * PAD, LANES), jnp.float32))
                if exchanged:
                    for name, rows in (("zs", 8), ("zin", 8), ("zr", ny), ("ys", nx), ("yr", nx)):
                        setattr(h, name, self.add(pltpu.VMEM((2, round_up(rows), LANES), jnp.float32)))
                    h.send = self.add(pltpu.SemaphoreType.DMA((6,)))
                    h.recv = self.add(pltpu.SemaphoreType.DMA((6,)))
                return h

            exchanged = WINDOW[level] is None
            g.b = halo(exchanged)
            g.sx = planes(nx + 1)
            for name in ("sym", "syp", "szm", "szp", "q", "rq", "e"):
                setattr(g, name, planes(nx))
            if level > 0:
                g.f = planes(nx)
                g.c = planes(nx)
            if level == 0:
                g.pair = self.add(pltpu.VMEM((10, 80, LANES), jnp.float32))
                g.edge = planes(2)
            elif level < LEVELS - 1:
                g.pair = planes(nx // 2)
            g.it = [halo(exchanged) for _ in range(4 if exchanged else 2)]
            self.tree.level.append(g)
        self.tree.rhs = self.add(pltpu.VMEM(shape, jnp.float32))
        self.tree.coef_c = self.add(pltpu.VMEM(shape, jnp.float32))
        self.tree.load = self.add(pltpu.SemaphoreType.DMA((3,)))
        self.tree.gather = [self.gathered(1), self.gathered(2)]
        self.tree.parts = [self.parted(1, shape[1] // 2), self.parted(2, shape[1] // 2)]

    def parted(self, arrays, rows):
        h = Names()
        h.pairs = self.add(pltpu.VMEM((arrays, 4, rows, LANES), jnp.float32))
        h.outer = self.add(pltpu.VMEM((arrays, rows, LANES), jnp.float32))
        h.pairs_in = self.add(pltpu.VMEM((3, 3, arrays, 4, rows, LANES), jnp.float32))
        h.outer_in = self.add(pltpu.VMEM((3, 3, 2, arrays, rows, LANES), jnp.float32))
        h.send = self.add(pltpu.SemaphoreType.DMA((26,)))
        h.recv = self.add(pltpu.SemaphoreType.DMA((26,)))
        return h

    def gathered(self, arrays):
        h = Names()
        h.block = self.add(pltpu.VMEM((arrays, 16, LANES), jnp.float32))
        h.near = self.add(pltpu.VMEM((4, arrays, 16, LANES), jnp.float32))
        h.column = self.add(pltpu.VMEM((arrays, 48, LANES), jnp.float32))
        h.all = self.add(pltpu.VMEM((3, 4, arrays, 48, LANES), jnp.float32))
        if arrays == 1:
            h.halves = self.add(pltpu.VMEM((2, 24, LANES), jnp.float32))
            h.side = self.add(pltpu.VMEM((2, 4, 24, LANES), jnp.float32))
        h.near_send = self.add(pltpu.SemaphoreType.DMA((4,)))
        h.near_recv = self.add(pltpu.SemaphoreType.DMA((4,)))
        h.all_send = self.add(pltpu.SemaphoreType.DMA((3, 4)))
        h.all_recv = self.add(pltpu.SemaphoreType.DMA((3, 4)))
        return h

    def add(self, shape):
        self.shapes.append(shape)
        return len(self.shapes) - 1

    def unpack(self, refs):
        def walk(node):
            if isinstance(node, int):
                return refs[node]
            if isinstance(node, list):
                return [walk(item) for item in node]
            result = Names()
            for name, item in vars(node).items():
                setattr(result, name, walk(item))
            return result

        return walk(self.tree)


def solution(mesh):
    sizes = dict(mesh.shape)

    def local(rhs, coef_b, coef_c):
        shape = rhs.shape
        plan = Plan(shape)
        return pl.pallas_call(
            make_kernel(shape, sizes, plan),
            out_shape=jax.ShapeDtypeStruct(shape, jnp.float32),
            in_specs=[pl.BlockSpec(memory_space=pl.ANY)] * 3,
            out_specs=pl.BlockSpec(memory_space=pltpu.VMEM),
            scratch_shapes=plan.shapes,
            compiler_params=pltpu.CompilerParams(
                collective_id=0, has_side_effects=True, vmem_limit_bytes=56 * 2**20),
        )(rhs, coef_b, coef_c)

    return jax.shard_map(
        local,
        mesh=mesh,
        in_specs=(P(*AXES),) * 3,
        out_specs=P(*AXES),
        check_vma=False,
    )
```

```python
import jax
import jax.numpy as jnp
from jax import lax
from jax.experimental import pallas as pl
from jax.experimental.pallas import tpu as pltpu
from jax.sharding import PartitionSpec as P

LEVELS = 4
COARSE_SWEEPS = 6
CENTRE = 1.1
RADIUS = 0.9
LANES = 128
PAD = 8

MESH = pl.DeviceIdType.MESH
AXES = ("gx", "gy", "gz")


def chebyshev(sweeps):
    ratio = RADIUS / CENTRE
    factors = [(0.0, 1.0 / CENTRE)]
    for _ in range(sweeps - 1):
        following = 1.0 / (2.0 * CENTRE / RADIUS - ratio)
        factors.append((following * ratio, 2.0 * following / RADIUS))
        ratio = following
    return factors


def round_up(value):
    return -(-value // 8) * 8


class Names:
    pass


def exact_dot(lefts, matrix):
    left = jnp.concatenate(lefts, axis=0)
    high = left.astype(jnp.bfloat16)
    rest = left - high.astype(jnp.float32)
    middle = rest.astype(jnp.bfloat16)
    low = (rest - middle.astype(jnp.float32)).astype(jnp.bfloat16)
    product = jnp.dot(jnp.concatenate([low, middle, high], axis=0), matrix, preferred_element_type=jnp.float32)
    total, rows = left.shape[0], lefts[0].shape[0]
    product = (product[:total] + product[total:2 * total]) + product[2 * total:]
    return [product[rows * k:rows * k + rows] for k in range(len(lefts))]


WINDOW = (None, (16, 40), (16, 48), (8, 24))
FIRST_ROW = (0, 8, 18, 9)
NEAR = (-2, -1, 1, 2)
TOGETHER = 16


def make_kernel(shape, sizes, plan):
    count = {axis: sizes[axis] for axis in AXES}

    def kernel(rhs_in, coef_b_in, coef_c_in, out, *scratch):
        refs = plan.unpack(scratch)
        rhs, coef_c = refs.rhs, refs.coef_c
        inputs = [
            pltpu.make_async_copy(source, target, refs.load.at[i])
            for i, (source, target) in enumerate((
                (coef_b_in, refs.level[0].b.vp.at[pl.ds(1, shape[0]), pl.ds(PAD, shape[1])]),
                (coef_c_in, coef_c), (rhs_in, rhs)))
        ]
        place = {axis: lax.axis_index(axis) for axis in AXES}

        def beyond(axis, step):
            return lax.rem(place[axis] + count[axis] + step, count[axis])

        after = {axis: beyond(axis, 1) for axis in AXES}
        before = {axis: beyond(axis, -1) for axis in AXES}
        def own(level):
            return tuple(n >> level for n in shape)

        def first_plane(level):
            if level > 1:
                return 0
            return place["gx"] * own(level)[0] - (4 if level == 1 else 0)

        sides = (-1, 0, 1)
        around_all = [(dx, dy, dz) for dx in sides for dy in sides for dz in sides if (dx, dy, dz) != (0, 0, 0)]
        around_xz = [(dx, dz) for dx in range(4) for dz in (-1, 0, 1) if (dx, dz) != (0, 0)]

        barrier = pltpu.get_barrier_semaphore()
        partners = [offset for offset in around_all if sum(map(abs, offset)) == 1]
        for offset in partners:
            pl.semaphore_signal(barrier, inc=1, device_id={a: beyond(a, d) for a, d in zip(AXES, offset)},
                                device_id_type=MESH)
        for copy in inputs:
            copy.start()

        lane = lax.broadcasted_iota(jnp.int32, (1, LANES), 1)

        def dims(level):
            return WINDOW[level] or own(level)[:2]

        def clear_rim(level, h):
            nx, ny = dims(level)
            h.vp[0] = jnp.zeros(h.vp.shape[1:], jnp.float32)
            h.vp[nx + 1] = jnp.zeros(h.vp.shape[1:], jnp.float32)
            rim = jnp.zeros((nx, PAD, LANES), jnp.float32)
            h.vp[pl.ds(1, nx), pl.ds(0, PAD), :] = rim
            h.vp[pl.ds(1, nx), pl.ds(PAD + ny, PAD), :] = rim

        for level in range(LEVELS):
            if WINDOW[level]:
                for h in [refs.level[level].b] + refs.level[level].it:
                    clear_rim(level, h)

        def copies(level, h):
            nx, ny = dims(level)
            rows = pl.ds(PAD, round_up(ny))
            vp, zs, zin, ys, yr = h.vp, h.zs, h.zin, h.ys, h.yr
            pairs = (
                (vp.at[nx, rows], vp.at[0, rows], "gx", after),
                (vp.at[1, rows], vp.at[nx + 1, rows], "gx", before),
                (ys.at[0], yr.at[0], "gy", after),
                (ys.at[1], yr.at[1], "gy", before),
                (zs.at[0], zin.at[0], "gz", after),
                (zs.at[1], zin.at[1], "gz", before),
            )
            return [
                pltpu.make_async_remote_copy(
                    src_ref=src, dst_ref=dst, send_sem=h.send.at[i], recv_sem=h.recv.at[i],
                    device_id={axis: where[axis]}, device_id_type=MESH)
                for i, (src, dst, axis, where) in enumerate(pairs)
            ]

        def finish(level, h):
            if WINDOW[level]:
                return
            nx, ny = dims(level)
            for copy in copies(level, h):
                copy.wait()
            for side in range(2):
                packed = h.zin[side]
                for tile in range(ny // 8):
                    h.zr[side, pl.ds(8 * tile, 8), :] = pltpu.roll(packed, (LANES - nx * tile) % LANES, 1)
            for x in range(nx):
                h.vp[x + 1, pl.ds(PAD - 1, 1), :] = h.yr[0, pl.ds(x, 1), :]
                h.vp[x + 1, pl.ds(PAD + ny, 1), :] = h.yr[1, pl.ds(x, 1), :]

        def planes(n, make, put, carry=None):
            step = min(n, TOGETHER)

            def body(i, carry):
                made = [make(i * step + k) for k in range(step)]
                for k in range(step):
                    if carry is None:
                        put(i * step + k, made[k])
                    else:
                        carry = put(i * step + k, made[k], carry)
                return carry

            if carry is not None:
                return lax.fori_loop(0, n // step, body, carry)

            def plain(i, zero):
                body(i, None)
                return zero

            lax.fori_loop(0, n // step, plain, 0)

        def sweep(level, make, h, held=False):
            nx, ny = dims(level)
            nz = own(level)[2]
            def keep(x, plane):
                h.vp[x + 1, pl.ds(PAD, ny), :] = plane

            if WINDOW[level]:
                planes(nx, make, keep)
                return
            zero = jnp.zeros((ny, LANES), jnp.float32)

            def pack(x, plane, carry):
                if not held:
                    keep(x, plane)
                high, low = carry
                h.ys[0, pl.ds(x, 1), :] = plane[ny - 1:ny]
                h.ys[1, pl.ds(x, 1), :] = plane[0:1]
                here = lane == x
                high = jnp.where(here, pltpu.roll(plane, lax.rem(x + LANES - (nz - 1), LANES), 1), high)
                low = jnp.where(here, pltpu.roll(plane, x, 1), low)
                return high, low

            high, low = planes(nx, make, pack, (zero, zero))
            for side, columns in enumerate((high, low)):
                packed = columns[0:8]
                for tile in range(1, ny // 8):
                    moved = pltpu.roll(columns[8 * tile:8 * tile + 8], nx * tile, 1)
                    packed = jnp.where((lane >= nx * tile) & (lane < nx * tile + nx), moved, packed)
                h.zs[side] = packed
            if held:
                pl.semaphore_wait(barrier, len(partners))
            for copy in copies(level, h):
                copy.start()

        def around(level, h, x):
            nx, ny = dims(level)
            vp = h.vp
            mid = vp[x + 1, pl.ds(PAD, ny), :]
            zm, zp = pltpu.roll(mid, 1, 1), pltpu.roll(mid, LANES - 1, 1)
            if level == 0:
                zlow, zhigh = h.zr[0], h.zr[1]
                zm = jnp.where(lane == 0, pltpu.roll(zlow, lax.rem(LANES - x, LANES), 1), zm)
                zp = jnp.where(lane == LANES - 1, pltpu.roll(zhigh, LANES - 1 - x, 1), zp)
            return (mid, vp[x, pl.ds(PAD, ny), :], vp[x + 2, pl.ds(PAD, ny), :],
                    vp[x + 1, pl.ds(PAD - 1, ny), :], vp[x + 1, pl.ds(PAD + 1, ny), :], zm, zp)

        def residual(level, h, x):
            g = refs.level[level]
            mid, xm, xp, ym, yp, zm, zp = around(level, h, x)
            total = g.sx[x] * xm + g.sx[x + 1] * xp + g.sym[x] * ym + g.syp[x] * yp + g.szm[x] * zm + g.szp[x] * zp
            return mid, source(level, x) - g.q[x] * mid + total

        def source(level, x):
            return rhs[x] if level == 0 else refs.level[level].f[x]

        def reaction(level, x):
            return coef_c[x] if level == 0 else refs.level[level].c[x]

        row_of = lax.broadcasted_iota(jnp.int32, (LANES, LANES), 0)
        col_of = lax.broadcasted_iota(jnp.int32, (LANES, LANES), 1)

        def pairing(level, wide, narrow):
            half = wide // 2
            return (half if level == 0 else half + jnp.where(wide >= 96, 64, 0)) == narrow

        def coarsen(level, count_x, get, put=None):
            pair = refs.level[level].pair
            shrink = jnp.where(pairing(level, row_of, col_of), 0.125, 0.0).astype(jnp.bfloat16)

            def put_pair(x, plane):
                pair[x, pl.ds(0, plane.shape[0]), :] = plane

            planes(count_x // 2, lambda x: get(2 * x) + get(2 * x + 1), put_pair)
            half = 16 if level == 1 else dims(level)[1] // 2
            made = exact_dot([pair[x, pl.ds(0, half, 2), :] + pair[x, pl.ds(1, half, 2), :]
                              for x in range(count_x // 2)], shrink)
            if put is not None:
                for x, plane in enumerate(made):
                    put(x, plane)
            return made

        def refine(level, count_x, get):
            pair = refs.level[level].pair
            grow = jnp.where(pairing(level, col_of, row_of), 1.0, 0.0).astype(jnp.bfloat16)
            rows = min(get(0).shape[0], pair.shape[1] // 2)
            for x, wide in enumerate(exact_dot([get(x) for x in range(count_x)], grow)):
                pair[x, pl.ds(0, rows, 2), :] = wide[:rows]
                pair[x, pl.ds(1, rows, 2), :] = wide[:rows]

        def block_parts(h, which, made):
            rows = own(1)[1]
            outer = jnp.zeros((rows, LANES), jnp.float32)
            for x, plane in enumerate(made):
                if x % 2:
                    h.pairs[which, x // 2] = made[x - 1] + pltpu.roll(plane, 64, 1)
                low = (lane >= 8 * x) & (lane < 8 * x + 8)
                high = (lane >= 64 + 8 * x) & (lane < 72 + 8 * x)
                outer = jnp.where(low, pltpu.roll(plane, 8 * x, 1), outer)
                outer = jnp.where(high, pltpu.roll(plane, 8 * x + 8, 1), outer)
            h.outer[which] = outer

        def part_copies(h, deep, steps=(1, 2, 3)):
            every = []
            for i, (dx, dy, dz) in enumerate(around_all):
                if abs(dx) + abs(dy) + abs(dz) not in steps:
                    continue
                rows = {-1: pl.ds(0, 8), 0: pl.ds(0, own(1)[1]), 1: pl.ds(own(1)[1] - 8, 8)}[dy]
                pairs = {-1: pl.ds(0, deep), 0: pl.ds(0, 4), 1: pl.ds(4 - deep, deep)}[dx]
                every_array = slice(None)
                if dz == 0:
                    src = h.pairs.at[every_array, pairs, rows]
                    dst = h.pairs_in.at[1 - dx, 1 - dy, every_array, pairs, rows]
                else:
                    src = h.outer.at[every_array, rows]
                    dst = h.outer_in.at[1 - dx, 1 - dy, (1 - dz) // 2, every_array, rows]
                every.append(pltpu.make_async_remote_copy(
                    src_ref=src, dst_ref=dst, send_sem=h.send.at[i], recv_sem=h.recv.at[i],
                    device_id={a: beyond(a, d) for a, d in zip(AXES, (dx, dy, dz))}, device_id_type=MESH))
            return every

        def parts_start(h, deep, steps=(1, 2, 3)):
            for copy in part_copies(h, deep, steps):
                copy.start()

        def parts_end(h, deep):
            for copy in part_copies(h, deep):
                copy.wait()

        def part_plane(h, which, plane):
            x = plane + 4
            dx, x = x // 8 - 1, x % 8
            rows_own = own(1)[1]
            pieces = []
            for dy, rows in ((-1, pl.ds(rows_own - 8, 8)), (0, pl.ds(0, rows_own)), (1, pl.ds(0, 8))):
                if (dx, dy) == (0, 0):
                    piece = h.pairs[which, x // 2, rows, :]
                else:
                    piece = h.pairs_in[1 + dx, 1 + dy, which, x // 2, rows, :]
                left = h.outer_in[1 + dx, 1 + dy, 0, which, rows, :]
                right = h.outer_in[1 + dx, 1 + dy, 1, which, rows, :]
                if x % 2:
                    piece = pltpu.roll(piece, 64, 1)
                piece = jnp.where(lane < 64, piece, 0.0)
                piece = jnp.where((lane >= 64) & (lane < 72), pltpu.roll(right, 64 - 8 * x, 1), piece)
                pieces.append(jnp.where(lane >= 120, pltpu.roll(left, (56 - 8 * x) % LANES, 1), piece))
            return pieces

        def put_pieces(ref, index, first, pieces):
            for piece in pieces:
                ref[index, pl.ds(first, piece.shape[0]), :] = piece
                first += piece.shape[0]

        def store(ref):
            def put(x, plane):
                ref[x] = plane

            return put

        levels = refs.level
        of_f, of_bc = refs.gather

        def block_to(h, which):
            def put(x, plane):
                mean = pltpu.roll(jnp.where(lane < 32, plane[:12], 0.0), 32 * x, 1)
                rows = pl.ds(0, 12)
                h.block[which, rows, :] = mean if x == 0 else h.block[which, rows, :] + mean

            return put

        def near_copies(h):
            return [
                pltpu.make_async_remote_copy(
                    src_ref=h.block, dst_ref=h.near.at[3 - i], send_sem=h.near_send.at[i],
                    recv_sem=h.near_recv.at[3 - i], device_id={"gy": beyond("gy", dy)}, device_id_type=MESH)
                for i, dy in enumerate(NEAR)
            ]

        def all_copies(h):
            every = []
            for dx, dz in around_xz:
                src, dst = h.column, h.all.at[1 - dz, place["gx"]]
                if dz and h is of_f:
                    src, dst = h.halves.at[(1 + dz) // 2], h.side.at[(1 - dz) // 2, place["gx"]]
                every.append(pltpu.make_async_remote_copy(
                    src_ref=src, dst_ref=dst, send_sem=h.all_send.at[1 - dz, dx], recv_sem=h.all_recv.at[1 - dz, dx],
                    device_id={"gx": beyond("gx", dx), "gz": beyond("gz", dz)}, device_id_type=MESH))
            return every

        def gather_near(h):
            for copy in near_copies(h):
                copy.start()

        def gather_all(h, arrays):
            for copy in near_copies(h):
                copy.wait()
            for k in range(arrays):
                h.column[k, pl.ds(0, 6), :] = h.near[0, k, pl.ds(6, 6), :]
                h.column[k, pl.ds(6, 12), :] = h.near[1, k, pl.ds(0, 12), :]
                h.column[k, pl.ds(18, 12), :] = h.block[k, pl.ds(0, 12), :]
                h.column[k, pl.ds(30, 12), :] = h.near[2, k, pl.ds(0, 12), :]
                h.column[k, pl.ds(42, 6), :] = h.near[3, k, pl.ds(0, 6), :]
            if h is of_f:
                lower = lax.rem(lane, 32) < 16
                top, bottom = h.column[0, pl.ds(0, 24), :], h.column[0, pl.ds(24, 24), :]
                h.halves[0] = jnp.where(lower, top, pltpu.roll(bottom, 16, 1))
                h.halves[1] = jnp.where(lower, pltpu.roll(bottom, LANES - 16, 1), top)
            for copy in all_copies(h):
                copy.start()
            h.all[1, place["gx"]] = h.column[...]

        def gather_end(h):
            for copy in all_copies(h):
                copy.wait()

        def gathered(h, which, x, dx):
            if h is of_f:
                here = h.all[1, x, which]
                left, right = h.side[0, x], h.side[1, x]
                plane = jnp.where(lane < 32, pltpu.roll(here, (LANES - 32 * dx) % LANES, 1), 0.0)
                parts = []
                for k, part in enumerate((plane[:24], plane[24:])):
                    moved = pltpu.roll(right, (LANES + 32 - 16 * k - 32 * dx) % LANES, 1)
                    part = jnp.where((lane >= 32) & (lane < 48), moved, part)
                    moved = pltpu.roll(left, (LANES + 96 + 16 * k - 32 * dx) % LANES, 1)
                    parts.append(jnp.where(lane >= 112, moved, part))
                return jnp.concatenate(parts, axis=0)
            left, here, right = (h.all[i, x, which] for i in range(3))
            plane = jnp.where(lane < 32, pltpu.roll(here, (LANES - 32 * dx) % LANES, 1), 0.0)
            plane = jnp.where((lane >= 32) & (lane < 64), pltpu.roll(right, (LANES + 32 - 32 * dx) % LANES, 1), plane)
            return jnp.where(lane >= 96, pltpu.roll(left, 96 - 32 * dx, 1), plane)

        def setup(level):
            g = refs.level[level]
            nx, ny = dims(level)
            nz = own(level)[2]
            half = 0.5 * 4.0 ** (LEVELS - 1 - level)
            finish(level, g.b)
            start_x, cells_x = first_plane(level), own(level)[0] * count["gx"]
            cells_y = own(level)[1]
            row = lax.broadcasted_iota(jnp.int32, (ny, 1), 0) + place["gy"] * cells_y - FIRST_ROW[level]
            if level == 0:
                column, used = lane, lane >= 0
            else:
                column = jnp.where(lane < 96, lane, lane - LANES)
                reach = 8 if level == 1 else nz
                used = (column < nz + reach) & (column >= -reach)
            column = column + place["gz"] * nz
            keep_ym = jnp.where(row == 0, 0.0, 1.0)
            keep_yp = jnp.where(row == cells_y * count["gy"] - 1, 0.0, 1.0)
            keep_zm = jnp.where(column == 0, 0.0, 1.0)
            keep_zp = jnp.where(column == nz * count["gz"] - 1, 0.0, 1.0)

            def make(x):
                mid, xm, xp, ym, yp, zm, zp = around(level, g.b, x)
                keep_xm = jnp.where((start_x + x == 0) | (start_x + x == cells_x), 0.0, 1.0)
                keep_xp = jnp.where(start_x + x == cells_x - 1, 0.0, 1.0)
                fxm, fxp = half * (mid + xm * keep_xm), half * (mid + xp * keep_xp)
                fym, fyp = half * (mid + ym * keep_ym), half * (mid + yp * keep_yp)
                fzm, fzp = half * (mid + zm * keep_zm), half * (mid + zp * keep_zp)
                q = reaction(level, x) + (fxm + fxp + fym + fyp + fzm + fzp)
                return (q, jnp.where(used, 1.0 / q, 0.0), fxm * keep_xm,
                        fym * keep_ym, fyp * keep_yp, fzm * keep_zm, fzp * keep_zp)

            def put(x, values):
                for name, value in zip(("q", "rq", "sx", "sym", "syp", "szm", "szp"), values):
                    getattr(g, name)[x] = value

            planes(nx, make, put)
            last = g.b.vp[nx, pl.ds(PAD, ny), :] + g.b.vp[nx + 1, pl.ds(PAD, ny), :]
            g.sx[nx] = half * last * jnp.where(start_x + nx == cells_x, 0.0, 1.0)

        def planes_of(level, h):
            ny = dims(level)[1]
            return lambda x: h.vp[x + 1, pl.ds(PAD, ny), :]

        (_, first), (carry_e, weight_r) = chebyshev(2)

        def start_down(level):
            g = levels[level]
            sweep(level, lambda x: source(level, x) * g.rq[x] * first, g.it[0])

        def go_down(level):
            g = levels[level]

            def second(x):
                mid, rest = residual(level, g.it[0], x)
                return mid * (1.0 + carry_e) + weight_r * rest * g.rq[x]

            finish(level, g.it[0])
            sweep(level, second, g.it[1])

        def leave(level, put=None):
            g = levels[level]
            finish(level, g.it[1])
            if level == 1:
                rows = slice(FIRST_ROW[1], FIRST_ROW[1] + own(1)[1])
                return coarsen(1, own(1)[0], lambda x: residual(1, g.it[1], x + 4)[1][rows], put)
            return coarsen(level, dims(level)[0], lambda x: residual(level, g.it[1], x)[1], put)

        def go_up(level, begun, ended, put):
            g = levels[level]

            def third(x):
                mid, rest = residual(level, begun, x)
                update = first * rest * g.rq[x]
                g.e[x] = update
                return mid + update

            sweep(level, third, ended)
            finish(level, ended)

            def last(x):
                mid, rest = residual(level, ended, x)
                return mid + carry_e * g.e[x] + weight_r * rest * g.rq[x]

            planes(dims(level)[0], last, put)

        parts_f, parts_bc = refs.parts
        own_planes = own(0)[0]
        inputs[0].wait()
        fine_b = planes_of(0, levels[0].b)
        sweep(0, fine_b, levels[0].b, held=True)
        made_b = coarsen(0, own_planes, fine_b)
        inputs[1].wait()
        block_parts(parts_bc, 0, made_b)
        made_c = coarsen(0, own_planes, lambda x: coef_c[x])
        block_parts(parts_bc, 1, made_c)
        parts_start(parts_bc, 3, (1,))
        for which, made in enumerate((made_b, made_c)):
            for x, plane in enumerate(made):
                levels[1].e[x, pl.ds(0, own(1)[1]), :] = plane
            coarsen(1, own(1)[0], lambda x: levels[1].e[x, pl.ds(0, own(1)[1]), :], block_to(of_bc, which))

        setup(0)
        inputs[2].wait()
        start_down(0)
        gather_near(of_bc)
        parts_start(parts_bc, 3, (2,))
        go_down(0)
        parts_start(parts_bc, 3, (3,))

        block_parts(parts_f, 0, leave(0))
        parts_start(parts_f, 2)
        gather_all(of_bc, 2)

        parts_end(parts_bc, 3)
        for w in range(-1, 17):
            put_pieces(levels[1].b.vp, w + 1, PAD, part_plane(parts_bc, 0, w))
            if 0 <= w < 16:
                put_pieces(levels[1].c, w, 0, part_plane(parts_bc, 1, w))
        setup(1)
        parts_end(parts_f, 2)
        for w in range(16):
            put_pieces(levels[1].f, w, 0, part_plane(parts_f, 0, w))
        start_down(1)
        go_down(1)
        leave(1, block_to(of_f, 0))
        gather_near(of_f)
        gather_all(of_f, 1)
        gather_end(of_bc)
        for dx in range(4):
            for x in range(4):
                levels[2].b.vp[4 * x + dx + 1, pl.ds(PAD, 48), :] = gathered(of_bc, 0, x, dx)
                levels[2].c[4 * x + dx] = gathered(of_bc, 1, x, dx)
        coarsen(2, 16, planes_of(2, levels[2].b), store(levels[3].f))
        sweep(3, lambda x: levels[3].f[x], levels[3].b)
        coarsen(2, 16, lambda x: levels[2].c[x], store(levels[3].c))
        setup(2)
        setup(3)
        gather_end(of_f)
        for dx in range(4):
            for x in range(4):
                levels[2].f[4 * x + dx] = gathered(of_f, 0, x, dx)

        start_down(2)
        go_down(2)
        leave(2, store(levels[3].f))

        g = levels[3]
        steps = chebyshev(COARSE_SWEEPS)

        def begin(x):
            update = source(3, x) * g.rq[x] * steps[0][1]
            g.e[x] = update
            return update

        sweep(3, begin, g.it[0])
        for step in range(1, COARSE_SWEEPS):
            def advance(x, step=step):
                mid, rest = residual(3, g.it[(step - 1) % 2], x)
                update = steps[step][0] * g.e[x] + steps[step][1] * rest * g.rq[x]
                g.e[x] = update
                return mid + update

            sweep(3, advance, g.it[step % 2])

        refine(2, 8, planes_of(3, g.it[(COARSE_SWEEPS - 1) % 2]))
        g = levels[2]
        sweep(2, lambda x: planes_of(2, g.it[1])(x) + g.pair[x // 2], g.it[0])
        go_up(2, g.it[0], g.it[1], store(g.f))

        g = levels[1]
        start_x = place["gx"] * own(2)[0] - 2
        refine(1, 8, lambda x: levels[2].f[jnp.clip(start_x + x, 0, 15), pl.ds(14, 24), :])
        sweep(1, lambda x: planes_of(1, g.it[1])(x) + g.pair[x // 2], g.it[0])
        go_up(1, g.it[0], g.it[1], store(g.f))

        g = levels[0]
        refine(0, 10, lambda x: levels[1].f[x + 3])
        begun = g.it[2]
        for x in range(18):
            begun.vp[x] = g.it[1].vp[x] + g.pair[(x + 1) // 2, pl.ds(8, 64), :]
        own_rows = own(1)[1]
        edges = [jnp.zeros((own_rows, LANES), jnp.float32)] * 2
        for x in range(8):
            plane = levels[1].f[x + 4, pl.ds(8, own_rows), :]
            for side, column in enumerate((LANES - 1, 64)):
                for target in (2 * x, 2 * x + 1):
                    moved = pltpu.roll(plane, (target - column) % LANES, 1)
                    edges[side] = jnp.where(lane == target, moved, edges[side])
        for side in range(2):
            g.edge[side, pl.ds(0, own_rows, 2), :] = edges[side]
            g.edge[side, pl.ds(1, own_rows, 2), :] = edges[side]
            begun.zr[side] = g.it[1].zr[side] + g.edge[side]
        go_up(0, begun, g.it[3], store(out))

    return kernel


class Plan:
    def __init__(self, shape):
        self.shapes = []
        self.tree = Names()
        self.tree.level = []
        for level in range(LEVELS):
            nx, ny = WINDOW[level] or tuple(n >> level for n in shape)[:2]
            g = Names()

            def planes(n, ny=ny):
                return self.add(pltpu.VMEM((n, ny, LANES), jnp.float32))

            def halo(exchanged, nx=nx, ny=ny):
                h = Names()
                h.vp = self.add(pltpu.VMEM((nx + 2, round_up(ny) + 2 * PAD, LANES), jnp.float32))
                if exchanged:
                    for name, rows in (("zs", 8), ("zin", 8), ("zr", ny), ("ys", nx), ("yr", nx)):
                        setattr(h, name, self.add(pltpu.VMEM((2, round_up(rows), LANES), jnp.float32)))
                    h.send = self.add(pltpu.SemaphoreType.DMA((6,)))
                    h.recv = self.add(pltpu.SemaphoreType.DMA((6,)))
                return h

            exchanged = WINDOW[level] is None
            g.b = halo(exchanged)
            g.sx = planes(nx + 1)
            for name in ("sym", "syp", "szm", "szp", "q", "rq", "e"):
                setattr(g, name, planes(nx))
            if level > 0:
                g.f = planes(nx)
                g.c = planes(nx)
            if level == 0:
                g.pair = self.add(pltpu.VMEM((10, 80, LANES), jnp.float32))
                g.edge = planes(2)
            elif level < LEVELS - 1:
                g.pair = planes(nx // 2)
            g.it = [halo(exchanged) for _ in range(4 if exchanged else 2)]
            self.tree.level.append(g)
        self.tree.rhs = self.add(pltpu.VMEM(shape, jnp.float32))
        self.tree.coef_c = self.add(pltpu.VMEM(shape, jnp.float32))
        self.tree.load = self.add(pltpu.SemaphoreType.DMA((3,)))
        self.tree.gather = [self.gathered(1), self.gathered(2)]
        self.tree.parts = [self.parted(1, shape[1] // 2), self.parted(2, shape[1] // 2)]

    def parted(self, arrays, rows):
        h = Names()
        h.pairs = self.add(pltpu.VMEM((arrays, 4, rows, LANES), jnp.float32))
        h.outer = self.add(pltpu.VMEM((arrays, rows, LANES), jnp.float32))
        h.pairs_in = self.add(pltpu.VMEM((3, 3, arrays, 4, rows, LANES), jnp.float32))
        h.outer_in = self.add(pltpu.VMEM((3, 3, 2, arrays, rows, LANES), jnp.float32))
        h.send = self.add(pltpu.SemaphoreType.DMA((26,)))
        h.recv = self.add(pltpu.SemaphoreType.DMA((26,)))
        return h

    def gathered(self, arrays):
        h = Names()
        h.block = self.add(pltpu.VMEM((arrays, 16, LANES), jnp.float32))
        h.near = self.add(pltpu.VMEM((4, arrays, 16, LANES), jnp.float32))
        h.column = self.add(pltpu.VMEM((arrays, 48, LANES), jnp.float32))
        h.all = self.add(pltpu.VMEM((3, 4, arrays, 48, LANES), jnp.float32))
        if arrays == 1:
            h.halves = self.add(pltpu.VMEM((2, 24, LANES), jnp.float32))
            h.side = self.add(pltpu.VMEM((2, 4, 24, LANES), jnp.float32))
        h.near_send = self.add(pltpu.SemaphoreType.DMA((4,)))
        h.near_recv = self.add(pltpu.SemaphoreType.DMA((4,)))
        h.all_send = self.add(pltpu.SemaphoreType.DMA((3, 4)))
        h.all_recv = self.add(pltpu.SemaphoreType.DMA((3, 4)))
        return h

    def add(self, shape):
        self.shapes.append(shape)
        return len(self.shapes) - 1

    def unpack(self, refs):
        def walk(node):
            if isinstance(node, int):
                return refs[node]
            if isinstance(node, list):
                return [walk(item) for item in node]
            result = Names()
            for name, item in vars(node).items():
                setattr(result, name, walk(item))
            return result

        return walk(self.tree)


def solution(mesh):
    sizes = dict(mesh.shape)

    def local(rhs, coef_b, coef_c):
        shape = rhs.shape
        plan = Plan(shape)
        return pl.pallas_call(
            make_kernel(shape, sizes, plan),
            out_shape=jax.ShapeDtypeStruct(shape, jnp.float32),
            in_specs=[pl.BlockSpec(memory_space=pl.ANY)] * 3,
            out_specs=pl.BlockSpec(memory_space=pltpu.VMEM),
            scratch_shapes=plan.shapes,
            compiler_params=pltpu.CompilerParams(
                collective_id=0, has_side_effects=True, vmem_limit_bytes=40 * 2**20),
        )(rhs, coef_b, coef_c)

    return jax.shard_map(
        local,
        mesh=mesh,
        in_specs=(P(*AXES),) * 3,
        out_specs=P(*AXES),
        check_vma=False,
    )
```

```python
import jax
import jax.numpy as jnp
from jax import lax
from jax.experimental import pallas as pl
from jax.experimental.pallas import tpu as pltpu
from jax.sharding import PartitionSpec as P

LEVELS = 4
COARSE_SWEEPS = 6
CENTRE = 1.1
RADIUS = 0.9
LANES = 128
PAD = 8

MESH = pl.DeviceIdType.MESH
AXES = ("gx", "gy", "gz")


def chebyshev(sweeps):
    ratio = RADIUS / CENTRE
    factors = [(0.0, 1.0 / CENTRE)]
    for _ in range(sweeps - 1):
        following = 1.0 / (2.0 * CENTRE / RADIUS - ratio)
        factors.append((following * ratio, 2.0 * following / RADIUS))
        ratio = following
    return factors


def round_up(value):
    return -(-value // 8) * 8


class Names:
    pass


def exact_dot(lefts, matrix):
    left = jnp.concatenate(lefts, axis=0)
    high = left.astype(jnp.bfloat16)
    rest = left - high.astype(jnp.float32)
    middle = rest.astype(jnp.bfloat16)
    low = (rest - middle.astype(jnp.float32)).astype(jnp.bfloat16)
    product = jnp.dot(jnp.concatenate([low, middle, high], axis=0), matrix, preferred_element_type=jnp.float32)
    total, rows = left.shape[0], lefts[0].shape[0]
    product = (product[:total] + product[total:2 * total]) + product[2 * total:]
    return [product[rows * k:rows * k + rows] for k in range(len(lefts))]


WINDOW = (None, (16, 40), (16, 48), (8, 24))
FIRST_ROW = (0, 8, 18, 9)
NEAR = (-2, -1, 1, 2)
TOGETHER = 16


def make_kernel(shape, sizes, plan):
    count = {axis: sizes[axis] for axis in AXES}

    def kernel(rhs_in, coef_b_in, coef_c_in, out, *scratch):
        refs = plan.unpack(scratch)
        rhs, coef_c = refs.rhs, refs.coef_c
        inputs = [
            pltpu.make_async_copy(source, target, refs.load.at[i])
            for i, (source, target) in enumerate((
                (coef_b_in, refs.level[0].b.vp.at[pl.ds(1, shape[0]), pl.ds(PAD, shape[1])]),
                (coef_c_in, coef_c), (rhs_in, rhs)))
        ]
        place = {axis: lax.axis_index(axis) for axis in AXES}

        def beyond(axis, step):
            return lax.rem(place[axis] + count[axis] + step, count[axis])

        after = {axis: beyond(axis, 1) for axis in AXES}
        before = {axis: beyond(axis, -1) for axis in AXES}
        def own(level):
            return tuple(n >> level for n in shape)

        def first_plane(level):
            if level > 1:
                return 0
            return place["gx"] * own(level)[0] - (4 if level == 1 else 0)

        sides = (-1, 0, 1)
        around_all = [(dx, dy, dz) for dx in sides for dy in sides for dz in sides if (dx, dy, dz) != (0, 0, 0)]
        around_xz = [(dx, dz) for dx in range(4) for dz in (-1, 0, 1) if (dx, dz) != (0, 0)]

        barrier = pltpu.get_barrier_semaphore()
        partners = [offset for offset in around_all if sum(map(abs, offset)) == 1]
        for offset in partners:
            pl.semaphore_signal(barrier, inc=1, device_id={a: beyond(a, d) for a, d in zip(AXES, offset)},
                                device_id_type=MESH)
        for copy in inputs:
            copy.start()

        lane = lax.broadcasted_iota(jnp.int32, (1, LANES), 1)

        def dims(level):
            return WINDOW[level] or own(level)[:2]

        def clear_rim(level, h):
            nx, ny = dims(level)
            h.vp[0] = jnp.zeros(h.vp.shape[1:], jnp.float32)
            h.vp[nx + 1] = jnp.zeros(h.vp.shape[1:], jnp.float32)
            rim = jnp.zeros((nx, PAD, LANES), jnp.float32)
            h.vp[pl.ds(1, nx), pl.ds(0, PAD), :] = rim
            h.vp[pl.ds(1, nx), pl.ds(PAD + ny, PAD), :] = rim

        for level in range(LEVELS):
            if WINDOW[level]:
                for h in [refs.level[level].b] + refs.level[level].it:
                    clear_rim(level, h)

        def copies(level, h):
            nx, ny = dims(level)
            rows = pl.ds(PAD, round_up(ny))
            vp, zs, zin, ys, yr = h.vp, h.zs, h.zin, h.ys, h.yr
            pairs = (
                (vp.at[nx, rows], vp.at[0, rows], "gx", after),
                (vp.at[1, rows], vp.at[nx + 1, rows], "gx", before),
                (ys.at[0], yr.at[0], "gy", after),
                (ys.at[1], yr.at[1], "gy", before),
                (zs.at[0], zin.at[0], "gz", after),
                (zs.at[1], zin.at[1], "gz", before),
            )
            return [
                pltpu.make_async_remote_copy(
                    src_ref=src, dst_ref=dst, send_sem=h.send.at[i], recv_sem=h.recv.at[i],
                    device_id={axis: where[axis]}, device_id_type=MESH)
                for i, (src, dst, axis, where) in enumerate(pairs)
            ]

        def finish(level, h):
            if WINDOW[level]:
                return
            nx, ny = dims(level)
            for copy in copies(level, h):
                copy.wait()
            for side in range(2):
                packed = h.zin[side]
                for tile in range(ny // 8):
                    h.zr[side, pl.ds(8 * tile, 8), :] = pltpu.roll(packed, (LANES - nx * tile) % LANES, 1)
            for x in range(nx):
                h.vp[x + 1, pl.ds(PAD - 1, 1), :] = h.yr[0, pl.ds(x, 1), :]
                h.vp[x + 1, pl.ds(PAD + ny, 1), :] = h.yr[1, pl.ds(x, 1), :]

        def planes(n, make, put, carry=None):
            step = min(n, TOGETHER)

            def body(i, carry):
                made = [make(i * step + k) for k in range(step)]
                for k in range(step):
                    if carry is None:
                        put(i * step + k, made[k])
                    else:
                        carry = put(i * step + k, made[k], carry)
                return carry

            if carry is not None:
                return lax.fori_loop(0, n // step, body, carry)

            def plain(i, zero):
                body(i, None)
                return zero

            lax.fori_loop(0, n // step, plain, 0)

        def sweep(level, make, h, held=False):
            nx, ny = dims(level)
            nz = own(level)[2]
            def keep(x, plane):
                h.vp[x + 1, pl.ds(PAD, ny), :] = plane

            if WINDOW[level]:
                planes(nx, make, keep)
                return
            zero = jnp.zeros((ny, LANES), jnp.float32)

            def pack(x, plane, carry):
                if not held:
                    keep(x, plane)
                high, low = carry
                h.ys[0, pl.ds(x, 1), :] = plane[ny - 1:ny]
                h.ys[1, pl.ds(x, 1), :] = plane[0:1]
                here = lane == x
                high = jnp.where(here, pltpu.roll(plane, lax.rem(x + LANES - (nz - 1), LANES), 1), high)
                low = jnp.where(here, pltpu.roll(plane, x, 1), low)
                return high, low

            high, low = planes(nx, make, pack, (zero, zero))
            for side, columns in enumerate((high, low)):
                packed = columns[0:8]
                for tile in range(1, ny // 8):
                    moved = pltpu.roll(columns[8 * tile:8 * tile + 8], nx * tile, 1)
                    packed = jnp.where((lane >= nx * tile) & (lane < nx * tile + nx), moved, packed)
                h.zs[side] = packed
            if held:
                pl.semaphore_wait(barrier, len(partners))
            for copy in copies(level, h):
                copy.start()

        def around(level, h, x):
            nx, ny = dims(level)
            vp = h.vp
            mid = vp[x + 1, pl.ds(PAD, ny), :]
            zm, zp = pltpu.roll(mid, 1, 1), pltpu.roll(mid, LANES - 1, 1)
            if level == 0:
                zlow, zhigh = h.zr[0], h.zr[1]
                zm = jnp.where(lane == 0, pltpu.roll(zlow, lax.rem(LANES - x, LANES), 1), zm)
                zp = jnp.where(lane == LANES - 1, pltpu.roll(zhigh, LANES - 1 - x, 1), zp)
            return (mid, vp[x, pl.ds(PAD, ny), :], vp[x + 2, pl.ds(PAD, ny), :],
                    vp[x + 1, pl.ds(PAD - 1, ny), :], vp[x + 1, pl.ds(PAD + 1, ny), :], zm, zp)

        def residual(level, h, x):
            g = refs.level[level]
            mid, xm, xp, ym, yp, zm, zp = around(level, h, x)
            total = g.sx[x] * xm + g.sx[x + 1] * xp + g.sym[x] * ym + g.syp[x] * yp + g.szm[x] * zm + g.szp[x] * zp
            return mid, source(level, x) - g.q[x] * mid + total

        def source(level, x):
            return rhs[x] if level == 0 else refs.level[level].f[x]

        def reaction(level, x):
            return coef_c[x] if level == 0 else refs.level[level].c[x]

        row_of = lax.broadcasted_iota(jnp.int32, (LANES, LANES), 0)
        col_of = lax.broadcasted_iota(jnp.int32, (LANES, LANES), 1)

        def pairing(level, wide, narrow):
            half = wide // 2
            return (half if level == 0 else half + jnp.where(wide >= 96, 64, 0)) == narrow

        def coarsen(level, count_x, get, put=None):
            pair = refs.level[level].pair
            shrink = jnp.where(pairing(level, row_of, col_of), 0.125, 0.0).astype(jnp.bfloat16)

            def put_pair(x, plane):
                pair[x, pl.ds(0, plane.shape[0]), :] = plane

            planes(count_x // 2, lambda x: get(2 * x) + get(2 * x + 1), put_pair)
            half = 16 if level == 1 else dims(level)[1] // 2
            made = exact_dot([pair[x, pl.ds(0, half, 2), :] + pair[x, pl.ds(1, half, 2), :]
                              for x in range(count_x // 2)], shrink)
            if put is not None:
                for x, plane in enumerate(made):
                    put(x, plane)
            return made

        def refine(level, count_x, get):
            pair = refs.level[level].pair
            grow = jnp.where(pairing(level, col_of, row_of), 1.0, 0.0).astype(jnp.bfloat16)
            rows = min(get(0).shape[0], pair.shape[1] // 2)
            for x, wide in enumerate(exact_dot([get(x) for x in range(count_x)], grow)):
                pair[x, pl.ds(0, rows, 2), :] = wide[:rows]
                pair[x, pl.ds(1, rows, 2), :] = wide[:rows]

        def block_parts(h, which, made):
            rows = own(1)[1]
            outer = jnp.zeros((rows, LANES), jnp.float32)
            for x, plane in enumerate(made):
                if x % 2:
                    h.pairs[which, x // 2] = made[x - 1] + pltpu.roll(plane, 64, 1)
                low = (lane >= 8 * x) & (lane < 8 * x + 8)
                high = (lane >= 64 + 8 * x) & (lane < 72 + 8 * x)
                outer = jnp.where(low, pltpu.roll(plane, 8 * x, 1), outer)
                outer = jnp.where(high, pltpu.roll(plane, 8 * x + 8, 1), outer)
            h.outer[which] = outer

        def part_copies(h, deep, steps=(1, 2, 3)):
            every = []
            for i, (dx, dy, dz) in enumerate(around_all):
                if abs(dx) + abs(dy) + abs(dz) not in steps:
                    continue
                rows = {-1: pl.ds(0, 8), 0: pl.ds(0, own(1)[1]), 1: pl.ds(own(1)[1] - 8, 8)}[dy]
                pairs = {-1: pl.ds(0, deep), 0: pl.ds(0, 4), 1: pl.ds(4 - deep, deep)}[dx]
                every_array = slice(None)
                if dz == 0:
                    src = h.pairs.at[every_array, pairs, rows]
                    dst = h.pairs_in.at[1 - dx, 1 - dy, every_array, pairs, rows]
                else:
                    src = h.outer.at[every_array, rows]
                    dst = h.outer_in.at[1 - dx, 1 - dy, (1 - dz) // 2, every_array, rows]
                every.append(pltpu.make_async_remote_copy(
                    src_ref=src, dst_ref=dst, send_sem=h.send.at[i], recv_sem=h.recv.at[i],
                    device_id={a: beyond(a, d) for a, d in zip(AXES, (dx, dy, dz))}, device_id_type=MESH))
            return every

        def parts_start(h, deep, steps=(1, 2, 3)):
            for copy in part_copies(h, deep, steps):
                copy.start()

        def parts_end(h, deep):
            for copy in part_copies(h, deep):
                copy.wait()

        def part_plane(h, which, plane):
            x = plane + 4
            dx, x = x // 8 - 1, x % 8
            rows_own = own(1)[1]
            pieces = []
            for dy, rows in ((-1, pl.ds(rows_own - 8, 8)), (0, pl.ds(0, rows_own)), (1, pl.ds(0, 8))):
                if (dx, dy) == (0, 0):
                    piece = h.pairs[which, x // 2, rows, :]
                else:
                    piece = h.pairs_in[1 + dx, 1 + dy, which, x // 2, rows, :]
                left = h.outer_in[1 + dx, 1 + dy, 0, which, rows, :]
                right = h.outer_in[1 + dx, 1 + dy, 1, which, rows, :]
                if x % 2:
                    piece = pltpu.roll(piece, 64, 1)
                piece = jnp.where(lane < 64, piece, 0.0)
                piece = jnp.where((lane >= 64) & (lane < 72), pltpu.roll(right, 64 - 8 * x, 1), piece)
                pieces.append(jnp.where(lane >= 120, pltpu.roll(left, (56 - 8 * x) % LANES, 1), piece))
            return pieces

        def put_pieces(ref, index, first, pieces):
            for piece in pieces:
                ref[index, pl.ds(first, piece.shape[0]), :] = piece
                first += piece.shape[0]

        def store(ref):
            def put(x, plane):
                ref[x] = plane

            return put

        levels = refs.level
        of_f, of_bc = refs.gather

        def block_to(h, which):
            def put(x, plane):
                mean = pltpu.roll(jnp.where(lane < 32, plane[:12], 0.0), 32 * x, 1)
                rows = pl.ds(0, 12)
                h.block[which, rows, :] = mean if x == 0 else h.block[which, rows, :] + mean

            return put

        def near_copies(h):
            return [
                pltpu.make_async_remote_copy(
                    src_ref=h.block, dst_ref=h.near.at[3 - i], send_sem=h.near_send.at[i],
                    recv_sem=h.near_recv.at[3 - i], device_id={"gy": beyond("gy", dy)}, device_id_type=MESH)
                for i, dy in enumerate(NEAR)
            ]

        def all_copies(h):
            every = []
            for dx, dz in around_xz:
                src, dst = h.column, h.all.at[1 - dz, place["gx"]]
                if dz and h is of_f:
                    src, dst = h.halves.at[(1 + dz) // 2], h.side.at[(1 - dz) // 2, place["gx"]]
                every.append(pltpu.make_async_remote_copy(
                    src_ref=src, dst_ref=dst, send_sem=h.all_send.at[1 - dz, dx], recv_sem=h.all_recv.at[1 - dz, dx],
                    device_id={"gx": beyond("gx", dx), "gz": beyond("gz", dz)}, device_id_type=MESH))
            return every

        def gather_near(h):
            for copy in near_copies(h):
                copy.start()

        def gather_all(h, arrays):
            for copy in near_copies(h):
                copy.wait()
            for k in range(arrays):
                h.column[k, pl.ds(0, 6), :] = h.near[0, k, pl.ds(6, 6), :]
                h.column[k, pl.ds(6, 12), :] = h.near[1, k, pl.ds(0, 12), :]
                h.column[k, pl.ds(18, 12), :] = h.block[k, pl.ds(0, 12), :]
                h.column[k, pl.ds(30, 12), :] = h.near[2, k, pl.ds(0, 12), :]
                h.column[k, pl.ds(42, 6), :] = h.near[3, k, pl.ds(0, 6), :]
            if h is of_f:
                lower = lax.rem(lane, 32) < 16
                top, bottom = h.column[0, pl.ds(0, 24), :], h.column[0, pl.ds(24, 24), :]
                h.halves[0] = jnp.where(lower, top, pltpu.roll(bottom, 16, 1))
                h.halves[1] = jnp.where(lower, pltpu.roll(bottom, LANES - 16, 1), top)
            for copy in all_copies(h):
                copy.start()
            h.all[1, place["gx"]] = h.column[...]

        def gather_end(h):
            for copy in all_copies(h):
                copy.wait()

        def gathered(h, which, x, dx):
            if h is of_f:
                here = h.all[1, x, which]
                left, right = h.side[0, x], h.side[1, x]
                plane = jnp.where(lane < 32, pltpu.roll(here, (LANES - 32 * dx) % LANES, 1), 0.0)
                parts = []
                for k, part in enumerate((plane[:24], plane[24:])):
                    moved = pltpu.roll(right, (LANES + 32 - 16 * k - 32 * dx) % LANES, 1)
                    part = jnp.where((lane >= 32) & (lane < 48), moved, part)
                    moved = pltpu.roll(left, (LANES + 96 + 16 * k - 32 * dx) % LANES, 1)
                    parts.append(jnp.where(lane >= 112, moved, part))
                return jnp.concatenate(parts, axis=0)
            left, here, right = (h.all[i, x, which] for i in range(3))
            plane = jnp.where(lane < 32, pltpu.roll(here, (LANES - 32 * dx) % LANES, 1), 0.0)
            plane = jnp.where((lane >= 32) & (lane < 64), pltpu.roll(right, (LANES + 32 - 32 * dx) % LANES, 1), plane)
            return jnp.where(lane >= 96, pltpu.roll(left, 96 - 32 * dx, 1), plane)

        def setup(level):
            g = refs.level[level]
            nx, ny = dims(level)
            nz = own(level)[2]
            half = 0.5 * 4.0 ** (LEVELS - 1 - level)
            finish(level, g.b)
            start_x, cells_x = first_plane(level), own(level)[0] * count["gx"]
            cells_y = own(level)[1]
            row = lax.broadcasted_iota(jnp.int32, (ny, 1), 0) + place["gy"] * cells_y - FIRST_ROW[level]
            if level == 0:
                column, used = lane, lane >= 0
            else:
                column = jnp.where(lane < 96, lane, lane - LANES)
                reach = 8 if level == 1 else nz
                used = (column < nz + reach) & (column >= -reach)
            column = column + place["gz"] * nz
            keep_ym = jnp.where(row == 0, 0.0, 1.0)
            keep_yp = jnp.where(row == cells_y * count["gy"] - 1, 0.0, 1.0)
            keep_zm = jnp.where(column == 0, 0.0, 1.0)
            keep_zp = jnp.where(column == nz * count["gz"] - 1, 0.0, 1.0)

            def make(x):
                mid, xm, xp, ym, yp, zm, zp = around(level, g.b, x)
                keep_xm = jnp.where((start_x + x == 0) | (start_x + x == cells_x), 0.0, 1.0)
                keep_xp = jnp.where(start_x + x == cells_x - 1, 0.0, 1.0)
                fxm, fxp = half * (mid + xm * keep_xm), half * (mid + xp * keep_xp)
                fym, fyp = half * (mid + ym * keep_ym), half * (mid + yp * keep_yp)
                fzm, fzp = half * (mid + zm * keep_zm), half * (mid + zp * keep_zp)
                q = reaction(level, x) + (fxm + fxp + fym + fyp + fzm + fzp)
                return (q, jnp.where(used, 1.0 / q, 0.0), fxm * keep_xm,
                        fym * keep_ym, fyp * keep_yp, fzm * keep_zm, fzp * keep_zp)

            def put(x, values):
                for name, value in zip(("q", "rq", "sx", "sym", "syp", "szm", "szp"), values):
                    getattr(g, name)[x] = value

            planes(nx, make, put)
            last = g.b.vp[nx, pl.ds(PAD, ny), :] + g.b.vp[nx + 1, pl.ds(PAD, ny), :]
            g.sx[nx] = half * last * jnp.where(start_x + nx == cells_x, 0.0, 1.0)

        def planes_of(level, h):
            ny = dims(level)[1]
            return lambda x: h.vp[x + 1, pl.ds(PAD, ny), :]

        (_, first), (carry_e, weight_r) = chebyshev(2)

        def start_down(level):
            g = levels[level]
            sweep(level, lambda x: source(level, x) * g.rq[x] * first, g.it[0])

        def go_down(level):
            g = levels[level]

            def second(x):
                mid, rest = residual(level, g.it[0], x)
                return mid * (1.0 + carry_e) + weight_r * rest * g.rq[x]

            finish(level, g.it[0])
            sweep(level, second, g.it[1])

        def leave(level, put=None):
            g = levels[level]
            finish(level, g.it[1])
            if level == 1:
                rows = slice(FIRST_ROW[1], FIRST_ROW[1] + own(1)[1])
                return coarsen(1, own(1)[0], lambda x: residual(1, g.it[1], x + 4)[1][rows], put)
            return coarsen(level, dims(level)[0], lambda x: residual(level, g.it[1], x)[1], put)

        def go_up(level, begun, ended, put):
            g = levels[level]

            def third(x):
                mid, rest = residual(level, begun, x)
                update = first * rest * g.rq[x]
                g.e[x] = update
                return mid + update

            sweep(level, third, ended)
            finish(level, ended)

            def last(x):
                mid, rest = residual(level, ended, x)
                return mid + carry_e * g.e[x] + weight_r * rest * g.rq[x]

            planes(dims(level)[0], last, put)

        parts_f, parts_bc = refs.parts
        own_planes = own(0)[0]
        inputs[0].wait()
        fine_b = planes_of(0, levels[0].b)
        sweep(0, fine_b, levels[0].b, held=True)
        made_b = coarsen(0, own_planes, fine_b)
        inputs[1].wait()
        block_parts(parts_bc, 0, made_b)
        made_c = coarsen(0, own_planes, lambda x: coef_c[x])
        block_parts(parts_bc, 1, made_c)
        parts_start(parts_bc, 3, (1,))
        for which, made in enumerate((made_b, made_c)):
            for x, plane in enumerate(made):
                levels[1].e[x, pl.ds(0, own(1)[1]), :] = plane
            coarsen(1, own(1)[0], lambda x: levels[1].e[x, pl.ds(0, own(1)[1]), :], block_to(of_bc, which))

        setup(0)
        inputs[2].wait()
        start_down(0)
        gather_near(of_bc)
        parts_start(parts_bc, 3, (2,))
        go_down(0)
        parts_start(parts_bc, 3, (3,))

        block_parts(parts_f, 0, leave(0))
        parts_start(parts_f, 2)

        parts_end(parts_bc, 3)
        for w in range(-1, 17):
            put_pieces(levels[1].b.vp, w + 1, PAD, part_plane(parts_bc, 0, w))
            if 0 <= w < 16:
                put_pieces(levels[1].c, w, 0, part_plane(parts_bc, 1, w))
        setup(1)
        gather_all(of_bc, 2)
        parts_end(parts_f, 2)
        for w in range(16):
            put_pieces(levels[1].f, w, 0, part_plane(parts_f, 0, w))
        start_down(1)
        go_down(1)
        leave(1, block_to(of_f, 0))
        gather_near(of_f)
        gather_all(of_f, 1)
        gather_end(of_bc)
        for dx in range(4):
            for x in range(4):
                levels[2].b.vp[4 * x + dx + 1, pl.ds(PAD, 48), :] = gathered(of_bc, 0, x, dx)
                levels[2].c[4 * x + dx] = gathered(of_bc, 1, x, dx)
        coarsen(2, 16, planes_of(2, levels[2].b), store(levels[3].f))
        sweep(3, lambda x: levels[3].f[x], levels[3].b)
        coarsen(2, 16, lambda x: levels[2].c[x], store(levels[3].c))
        setup(2)
        setup(3)
        gather_end(of_f)
        for dx in range(4):
            for x in range(4):
                levels[2].f[4 * x + dx] = gathered(of_f, 0, x, dx)

        start_down(2)
        go_down(2)
        leave(2, store(levels[3].f))

        g = levels[3]
        steps = chebyshev(COARSE_SWEEPS)

        def begin(x):
            update = source(3, x) * g.rq[x] * steps[0][1]
            g.e[x] = update
            return update

        sweep(3, begin, g.it[0])
        for step in range(1, COARSE_SWEEPS):
            def advance(x, step=step):
                mid, rest = residual(3, g.it[(step - 1) % 2], x)
                update = steps[step][0] * g.e[x] + steps[step][1] * rest * g.rq[x]
                g.e[x] = update
                return mid + update

            sweep(3, advance, g.it[step % 2])

        refine(2, 8, planes_of(3, g.it[(COARSE_SWEEPS - 1) % 2]))
        g = levels[2]
        sweep(2, lambda x: planes_of(2, g.it[1])(x) + g.pair[x // 2], g.it[0])
        go_up(2, g.it[0], g.it[1], store(g.f))

        g = levels[1]
        start_x = place["gx"] * own(2)[0] - 2
        refine(1, 8, lambda x: levels[2].f[jnp.clip(start_x + x, 0, 15), pl.ds(14, 24), :])
        sweep(1, lambda x: planes_of(1, g.it[1])(x) + g.pair[x // 2], g.it[0])
        go_up(1, g.it[0], g.it[1], store(g.f))

        g = levels[0]
        refine(0, 10, lambda x: levels[1].f[x + 3])
        begun = g.it[2]
        for x in range(18):
            begun.vp[x] = g.it[1].vp[x] + g.pair[(x + 1) // 2, pl.ds(8, 64), :]
        own_rows = own(1)[1]
        edges = [jnp.zeros((own_rows, LANES), jnp.float32)] * 2
        for x in range(8):
            plane = levels[1].f[x + 4, pl.ds(8, own_rows), :]
            for side, column in enumerate((LANES - 1, 64)):
                for target in (2 * x, 2 * x + 1):
                    moved = pltpu.roll(plane, (target - column) % LANES, 1)
                    edges[side] = jnp.where(lane == target, moved, edges[side])
        for side in range(2):
            g.edge[side, pl.ds(0, own_rows, 2), :] = edges[side]
            g.edge[side, pl.ds(1, own_rows, 2), :] = edges[side]
            begun.zr[side] = g.it[1].zr[side] + g.edge[side]
        go_up(0, begun, g.it[3], store(out))

    return kernel


class Plan:
    def __init__(self, shape):
        self.shapes = []
        self.tree = Names()
        self.tree.level = []
        for level in range(LEVELS):
            nx, ny = WINDOW[level] or tuple(n >> level for n in shape)[:2]
            g = Names()

            def planes(n, ny=ny):
                return self.add(pltpu.VMEM((n, ny, LANES), jnp.float32))

            def halo(exchanged, nx=nx, ny=ny):
                h = Names()
                h.vp = self.add(pltpu.VMEM((nx + 2, round_up(ny) + 2 * PAD, LANES), jnp.float32))
                if exchanged:
                    for name, rows in (("zs", 8), ("zin", 8), ("zr", ny), ("ys", nx), ("yr", nx)):
                        setattr(h, name, self.add(pltpu.VMEM((2, round_up(rows), LANES), jnp.float32)))
                    h.send = self.add(pltpu.SemaphoreType.DMA((6,)))
                    h.recv = self.add(pltpu.SemaphoreType.DMA((6,)))
                return h

            exchanged = WINDOW[level] is None
            g.b = halo(exchanged)
            g.sx = planes(nx + 1)
            for name in ("sym", "syp", "szm", "szp", "q", "rq", "e"):
                setattr(g, name, planes(nx))
            if level > 0:
                g.f = planes(nx)
                g.c = planes(nx)
            if level == 0:
                g.pair = self.add(pltpu.VMEM((10, 80, LANES), jnp.float32))
                g.edge = planes(2)
            elif level < LEVELS - 1:
                g.pair = planes(nx // 2)
            g.it = [halo(exchanged) for _ in range(4 if exchanged else 2)]
            self.tree.level.append(g)
        self.tree.rhs = self.add(pltpu.VMEM(shape, jnp.float32))
        self.tree.coef_c = self.add(pltpu.VMEM(shape, jnp.float32))
        self.tree.load = self.add(pltpu.SemaphoreType.DMA((3,)))
        self.tree.gather = [self.gathered(1), self.gathered(2)]
        self.tree.parts = [self.parted(1, shape[1] // 2), self.parted(2, shape[1] // 2)]

    def parted(self, arrays, rows):
        h = Names()
        h.pairs = self.add(pltpu.VMEM((arrays, 4, rows, LANES), jnp.float32))
        h.outer = self.add(pltpu.VMEM((arrays, rows, LANES), jnp.float32))
        h.pairs_in = self.add(pltpu.VMEM((3, 3, arrays, 4, rows, LANES), jnp.float32))
        h.outer_in = self.add(pltpu.VMEM((3, 3, 2, arrays, rows, LANES), jnp.float32))
        h.send = self.add(pltpu.SemaphoreType.DMA((26,)))
        h.recv = self.add(pltpu.SemaphoreType.DMA((26,)))
        return h

    def gathered(self, arrays):
        h = Names()
        h.block = self.add(pltpu.VMEM((arrays, 16, LANES), jnp.float32))
        h.near = self.add(pltpu.VMEM((4, arrays, 16, LANES), jnp.float32))
        h.column = self.add(pltpu.VMEM((arrays, 48, LANES), jnp.float32))
        h.all = self.add(pltpu.VMEM((3, 4, arrays, 48, LANES), jnp.float32))
        if arrays == 1:
            h.halves = self.add(pltpu.VMEM((2, 24, LANES), jnp.float32))
            h.side = self.add(pltpu.VMEM((2, 4, 24, LANES), jnp.float32))
        h.near_send = self.add(pltpu.SemaphoreType.DMA((4,)))
        h.near_recv = self.add(pltpu.SemaphoreType.DMA((4,)))
        h.all_send = self.add(pltpu.SemaphoreType.DMA((3, 4)))
        h.all_recv = self.add(pltpu.SemaphoreType.DMA((3, 4)))
        return h

    def add(self, shape):
        self.shapes.append(shape)
        return len(self.shapes) - 1

    def unpack(self, refs):
        def walk(node):
            if isinstance(node, int):
                return refs[node]
            if isinstance(node, list):
                return [walk(item) for item in node]
            result = Names()
            for name, item in vars(node).items():
                setattr(result, name, walk(item))
            return result

        return walk(self.tree)


def solution(mesh):
    sizes = dict(mesh.shape)

    def local(rhs, coef_b, coef_c):
        shape = rhs.shape
        plan = Plan(shape)
        return pl.pallas_call(
            make_kernel(shape, sizes, plan),
            out_shape=jax.ShapeDtypeStruct(shape, jnp.float32),
            in_specs=[pl.BlockSpec(memory_space=pl.ANY)] * 3,
            out_specs=pl.BlockSpec(memory_space=pltpu.VMEM),
            scratch_shapes=plan.shapes,
            compiler_params=pltpu.CompilerParams(
                collective_id=0, has_side_effects=True, vmem_limit_bytes=56 * 2**20),
        )(rhs, coef_b, coef_c)

    return jax.shard_map(
        local,
        mesh=mesh,
        in_specs=(P(*AXES),) * 3,
        out_specs=P(*AXES),
        check_vma=False,
    )
```
